32 devices in a mesh: dp: 16 (over z, y, core), mp: 2 (over x).
Axes of the slice: x: 2, y: 2, z: 4, core: 2. Of those that a mesh axis runs over, the one named last changes fastest.
Arguments:
- enc_in: bfloat16 [64, 512, 512], P(('dp', 'mp')), may hold values from -6 to 6
- enc_segments: int32 [64, 512], P('dp'), may hold values from 0 to 3, never falling along the last dimension, each value on 1 to 256 neighbouring positions
- enc_pad: int32 [64, 512], P('dp'), may hold values 0 or 1
- enc_buckets: int32 [1023], replicated, may hold values from 0 to 31
- dec_in: bfloat16 [64, 64, 512], P(('dp', 'mp')), may hold values from -6 to 6
- dec_segments: int32 [64, 64], P('dp'), may hold values from 0 to 3, never falling along the last dimension, each value on 1 to 32 neighbouring positions
- dec_buckets: int32 [64], replicated, may hold values from 0 to 31
- enc_cot: bfloat16 [64, 512, 512], P(('dp', 'mp')), may hold values from -6 to 6
- dec_cot: bfloat16 [64, 64, 512], P(('dp', 'mp')), may hold values from -6 to 6
- enc_norm1: float32 [512], replicated, may hold values from 0.1 to 1.9
- enc_query: bfloat16 [512, 512], P(None, 'mp'), may hold values from -0.03125 to 0.03125
- enc_kv: bfloat16 [2, 512, 512], P(None, None, 'mp'), may hold values from -0.25 to 0.25
- enc_out_proj: bfloat16 [512, 512], P('mp'), may hold values from -2 to 2
- enc_bias: bfloat16 [32, 8], P(None, 'mp'), may hold values from -4 to 4
- enc_norm2: float32 [512], replicated, may hold values from 0.1 to 1.9
- enc_ff_in: bfloat16 [512, 2048], P(None, 'mp'), may hold values from -0.25 to 0.25
- enc_ff_out: bfloat16 [2048, 512], P('mp'), may hold values from -0.125 to 0.125
- enc_final: float32 [512], replicated, may hold values from 0.1 to 1.9
- dec_norm1: float32 [512], replicated, may hold values from 0.1 to 1.9
- dec_query: bfloat16 [512, 512], P(None, 'mp'), may hold values from -0.03125 to 0.03125
- dec_kv: bfloat16 [2, 512, 512], P(None, None, 'mp'), may hold values from -0.25 to 0.25
- dec_out_proj: bfloat16 [512, 512], P('mp'), may hold values from -0.75 to 0.75
- dec_bias: bfloat16 [32, 8], P(None, 'mp'), may hold values from -4 to 4
- dec_norm2: float32 [512], replicated, may hold values from 0.1 to 1.9
- cross_query: bfloat16 [512, 512], P(None, 'mp'), may hold values from -0.03125 to 0.03125
- cross_kv: bfloat16 [2, 512, 512], P(None, None, 'mp'), may hold values from -0.25 to 0.25
- cross_out: bfloat16 [512, 512], P('mp'), may hold values from -2 to 2
- dec_norm3: float32 [512], replicated, may hold values from 0.1 to 1.9
- dec_ff_in: bfloat16 [512, 2048], P(None, 'mp'), may hold values from -0.25 to 0.25
- dec_ff_out: bfloat16 [2048, 512], P('mp'), may hold values from -0.125 to 0.125
Outputs:
- enc_out: bfloat16 [64, 512, 512], P(('dp', 'mp'))
- dec_out: bfloat16 [64, 64, 512], P(('dp', 'mp'))
- enc_in_grad: float32 [64, 512, 512], P(('dp', 'mp'))
- dec_in_grad: float32 [64, 64, 512], P(('dp', 'mp'))
- enc_norm1_grad: float32 [512], replicated
- enc_query_grad: float32 [512, 512], P(None, 'mp')
- enc_kv_grad: float32 [2, 512, 512], P(None, None, 'mp')
- enc_out_proj_grad: float32 [512, 512], P('mp')
- enc_bias_grad: float32 [32, 8], P(None, 'mp')
- enc_norm2_grad: float32 [512], replicated
- enc_ff_in_grad: float32 [512, 2048], P(None, 'mp')
- enc_ff_out_grad: float32 [2048, 512], P('mp')
- enc_final_grad: float32 [512], replicated
- dec_norm1_grad: float32 [512], replicated
- dec_query_grad: float32 [512, 512], P(None, 'mp')
- dec_kv_grad: float32 [2, 512, 512], P(None, None, 'mp')
- dec_out_proj_grad: float32 [512, 512], P('mp')
- dec_bias_grad: float32 [32, 8], P(None, 'mp')
- dec_norm2_grad: float32 [512], replicated
- cross_query_grad: float32 [512, 512], P(None, 'mp')
- cross_kv_grad: float32 [2, 512, 512], P(None, None, 'mp')
- cross_out_grad: float32 [512, 512], P('mp')
- dec_norm3_grad: float32 [512], replicated
- dec_ff_in_grad: float32 [512, 2048], P(None, 'mp')
- dec_ff_out_grad: float32 [2048, 512], P('mp')
The draws below stay inside these ranges and needn't reach their ends.
All inputs are finite; a program needn't handle non-finite values. No bound on the sum of `enc_pad` on one device may be relied on, other than what follows from the above.
Results may differ from the reference program's by a relative error of at most 0.03.
Values may be sent and summed in bfloat16 or wider, within the bound.
No kernel may reach another device: no remote copies, remote signals or barrier semaphores. Data moves between devices by JAX's collectives and lax.ppermute only.
A program may use at most 192 MiB of HBM per device.

```python
import math
import jax
import jax.numpy as jnp
import numpy as np
from jax import lax

D = 512
HEADS = 8
HEAD_DIM = 64
FF = 2048
BUCKETS = 32
ENC_LEN = 512
DEC_LEN = 64
SEGMENTS = 4
INNER = 512
ROWS = 64


def with_ends(result, own_key, least, largest):
    extent = result.shape
    index_at = [jax.random.randint(jax.random.fold_in(own_key, axis), (), 0, extent[axis]) for axis in range(len(extent))]
    result = result.at[tuple(index_at)].set(least)
    longest = extent.index(max(extent))
    index_at[longest] = (index_at[longest] + 1) % extent[longest]
    return result.at[tuple(index_at)].set(largest)


def shard_levels(rng, shape, pieces, low, high):
    loudness = 1.0
    for axis_at, shards_of in pieces:
        heights = jax.random.uniform(jax.random.fold_in(jax.random.fold_in(rng, 6), axis_at), (shards_of,), jnp.float32, low / len(pieces), high / len(pieces))
        loudness = loudness * jnp.repeat(jnp.exp(heights), shape[axis_at] // shards_of).reshape((-1,) + (1,) * (len(shape) - 1 - axis_at))
    return loudness


def length_profile(amount, total, most, lean):
    portions = [(1 << 20) // math.isqrt(standing ** lean) + 1 for standing in range(2, amount + 1)]
    surplus, given = total - most - (amount - 1), [1] * (amount - 1)
    while surplus > 0:
        candidates = [i for i in range(amount - 1) if given[i] < most]
        whole, remaining = sum([portions[i] for i in candidates]), surplus
        for i in candidates:
            more = min(most - given[i], max(1, remaining * portions[i] // whole), surplus)
            given[i] = given[i] + more
            surplus = surplus - more
    return np.array([most] + given)


def ragged(stream_key, count, total, bound, lean):
    if count == 2:
        one = jax.random.randint(stream_key, (), max(1, total - bound), min(bound, total - 1) + 1)
        return jnp.stack([one, total - one])
    lengths = jnp.asarray(length_profile(count, total, bound, lean), jnp.int32)
    couples = (count - 1) // 2
    source_of, taker = lengths[1:1 + 2 * couples:2], lengths[2:2 + 2 * couples:2]
    slack = jnp.minimum(source_of - 1, bound - taker)
    shifted = jax.random.randint(jax.random.fold_in(stream_key, 1), (couples,), 0, 1 << 20) % (slack + 1)
    lengths = lengths.at[1:1 + 2 * couples:2].set(source_of - shifted).at[2:2 + 2 * couples:2].set(taker + shifted)
    return lengths[jax.random.permutation(jax.random.fold_in(stream_key, 2), count)]


def noise(stream_key, shape, width, bound, shards=(), held_as=jnp.bfloat16):
    entries = width * jax.random.normal(stream_key, shape, jnp.float32)
    if shards:
        entries = entries * shard_levels(stream_key, shape, shards, -0.22, 0.18)
    return jnp.clip(entries, -bound, bound).astype(held_as)


def setup_inputs(seed: int = 0) -> dict:
    key_of = jax.random.split(jax.random.key(seed), 31)
    enc_in = noise(key_of[0], (ROWS, ENC_LEN, D), 1.0, 6.0, ((0, 32),))
    enc_segments = jax.vmap(lambda own: jnp.searchsorted(jnp.cumsum(ragged(own, SEGMENTS, ENC_LEN, ENC_LEN // 2, 0)), jnp.arange(ENC_LEN), side="right"))(jax.random.split(key_of[1], ROWS)).reshape((ROWS, ENC_LEN)).astype(jnp.int32)
    enc_pad = with_ends((jax.random.randint(key_of[2], (ROWS, ENC_LEN), 0, 8) < 7).astype(jnp.int32), jax.random.fold_in(key_of[2], 1), 0, 1)
    enc_buckets = with_ends(jax.random.randint(key_of[3], (2 * ENC_LEN - 1,), 0, BUCKETS), jax.random.fold_in(key_of[3], 1), 0, BUCKETS - 1).astype(jnp.int32)
    dec_in = noise(key_of[4], (ROWS, DEC_LEN, D), 1.0, 6.0, ((0, 32),))
    dec_segments = jax.vmap(lambda own: jnp.searchsorted(jnp.cumsum(ragged(own, SEGMENTS, DEC_LEN, DEC_LEN // 2, 0)), jnp.arange(DEC_LEN), side="right"))(jax.random.split(key_of[5], ROWS)).reshape((ROWS, DEC_LEN)).astype(jnp.int32)
    dec_buckets = with_ends(jax.random.randint(key_of[6], (DEC_LEN,), 0, BUCKETS), jax.random.fold_in(key_of[6], 1), 0, BUCKETS - 1).astype(jnp.int32)
    enc_cot = noise(key_of[7], (ROWS, ENC_LEN, D), 1.0, 6.0, ((0, 32),))
    dec_cot = noise(key_of[8], (ROWS, DEC_LEN, D), 1.0, 6.0, ((0, 32),))
    enc_norm1 = jnp.clip(1.0 + 0.18 * jax.random.normal(key_of[9], (D,), jnp.float32), 0.1, 1.9)
    enc_query = noise(key_of[10], (D, INNER), (D * HEAD_DIM) ** -0.5, 0.03125, ((1, 2),))
    enc_kv = noise(key_of[11], (2, D, INNER), D ** -0.5, 0.25, ((2, 2),))
    enc_out_proj = noise(key_of[12], (INNER, D), (max(1, 2 * INNER * SEGMENTS // ENC_LEN)) ** -0.5, 2.0, ((0, 2),))
    enc_bias = noise(key_of[13], (BUCKETS, HEADS), 1.0, 4.0, ((1, 2),))
    enc_norm2 = jnp.clip(1.0 + 0.18 * jax.random.normal(key_of[14], (D,), jnp.float32), 0.1, 1.9)
    enc_ff_in = noise(key_of[15], (D, FF), D ** -0.5, 0.25, ((1, 2),))
    enc_ff_out = noise(key_of[16], (FF, D), FF ** -0.5, 0.125, ((0, 2),))
    enc_final = jnp.clip(1.0 + 0.18 * jax.random.normal(key_of[17], (D,), jnp.float32), 0.1, 1.9)
    dec_norm1 = jnp.clip(1.0 + 0.18 * jax.random.normal(key_of[18], (D,), jnp.float32), 0.1, 1.9)
    dec_query = noise(key_of[19], (D, INNER), (D * HEAD_DIM) ** -0.5, 0.03125, ((1, 2),))
    dec_kv = noise(key_of[20], (2, D, INNER), D ** -0.5, 0.25, ((2, 2),))
    dec_out_proj = noise(key_of[21], (INNER, D), (max(1, 2 * INNER * SEGMENTS // DEC_LEN)) ** -0.5, 0.75, ((0, 2),))
    dec_bias = noise(key_of[22], (BUCKETS, HEADS), 1.0, 4.0, ((1, 2),))
    dec_norm2 = jnp.clip(1.0 + 0.18 * jax.random.normal(key_of[23], (D,), jnp.float32), 0.1, 1.9)
    cross_query = noise(key_of[24], (D, INNER), (D * HEAD_DIM) ** -0.5, 0.03125, ((1, 2),))
    cross_kv = noise(key_of[25], (2, D, INNER), D ** -0.5, 0.25, ((2, 2),))
    cross_out = noise(key_of[26], (INNER, D), (max(1, 2 * INNER * SEGMENTS // ENC_LEN)) ** -0.5, 2.0, ((0, 2),))
    dec_norm3 = jnp.clip(1.0 + 0.18 * jax.random.normal(key_of[27], (D,), jnp.float32), 0.1, 1.9)
    dec_ff_in = noise(key_of[28], (D, FF), D ** -0.5, 0.25, ((1, 2),))
    dec_ff_out = noise(key_of[29], (FF, D), FF ** -0.5, 0.125, ((0, 2),))
    return {"enc_in": enc_in, "enc_segments": enc_segments, "enc_pad": enc_pad, "enc_buckets": enc_buckets, "dec_in": dec_in, "dec_segments": dec_segments, "dec_buckets": dec_buckets, "enc_cot": enc_cot, "dec_cot": dec_cot, "enc_norm1": enc_norm1, "enc_query": enc_query, "enc_kv": enc_kv, "enc_out_proj": enc_out_proj, "enc_bias": enc_bias, "enc_norm2": enc_norm2, "enc_ff_in": enc_ff_in, "enc_ff_out": enc_ff_out, "enc_final": enc_final, "dec_norm1": dec_norm1, "dec_query": dec_query, "dec_kv": dec_kv, "dec_out_proj": dec_out_proj, "dec_bias": dec_bias, "dec_norm2": dec_norm2, "cross_query": cross_query, "cross_kv": cross_kv, "cross_out": cross_out, "dec_norm3": dec_norm3, "dec_ff_in": dec_ff_in, "dec_ff_out": dec_ff_out}


@jax.custom_vjp
def low(v):
    return lax.optimization_barrier(v.astype(jnp.bfloat16)).astype(jnp.float32)

@jax.custom_vjp
def low_back(v):
    return v

def low_keep(v):
    return (low(v), None)

def low_pass(kept, grad):
    return (grad,)

def back_keep(v):
    return (v, None)

def back_low(kept, grad):
    return (low(grad),)
low.defvjp(low_keep, low_pass)
low_back.defvjp(back_keep, back_low)
masked_value = -1e+30
norm_eps = 1e-06
highest = lax.Precision.HIGHEST

def rounded_both(values):
    return low(low_back(values))

def rms_scale(values, gain_vec):
    mean_square = lax.optimization_barrier(jnp.mean(values * values, axis=-1, keepdims=True))
    return values * lax.rsqrt(mean_square + norm_eps) * gain_vec

def split_heads(values):
    return values.reshape(values.shape[:-1] + (HEADS, HEAD_DIM))

def attend(queries, key_rows, value_rows, pos_bias, allowed):
    scores = low_back(jnp.einsum('qhd,khd->hqk', queries, key_rows, precision=highest))
    scores = jnp.where(allowed[None], scores + pos_bias, masked_value)
    attn_probs = low(jax.nn.softmax(scores, axis=-1))
    return rounded_both(jnp.einsum('hqk,khd->qhd', attn_probs, value_rows, precision=highest))

def visible_keys(segment_ids, padding):
    first_column = jnp.ones(segment_ids.shape[:-1] + (1,), jnp.bool_)
    starts = jnp.concatenate([first_column, segment_ids[..., 1:] != segment_ids[..., :-1]], axis=-1)
    return (padding == 1) | starts

def layer_forward(enc_x, dec_x, params, enc_seg, pad_rows, dec_seg, enc_buckets, dec_buckets):
    enc_norm1, enc_query, enc_kv, enc_out_proj, enc_bias, enc_norm2, enc_ff_in, enc_ff_out, enc_final, dec_norm1, dec_query, dec_kv, dec_out_proj, dec_bias, dec_norm2, cross_query, cross_kv, cross_out, dec_norm3, dec_ff_in, dec_ff_out = params
    group_rows = enc_x.shape[0]
    positions = jnp.arange(ENC_LEN, dtype=jnp.int32)
    offsets = positions[None, :] - positions[:, None] + ENC_LEN - 1
    enc_pos = jnp.transpose(enc_bias[enc_buckets[offsets]], (2, 0, 1))
    dec_places = jnp.arange(DEC_LEN, dtype=jnp.int32)
    distance = jnp.clip(dec_places[:, None] - dec_places[None, :], 0, DEC_LEN - 1)
    dec_pos = jnp.transpose(dec_bias[dec_buckets[distance]], (2, 0, 1))
    causal = dec_places[None, :] <= dec_places[:, None]
    visible = visible_keys(enc_seg, pad_rows)
    normed = low(rms_scale(enc_x, enc_norm1))
    queries = split_heads(rounded_both(jnp.einsum('gld,de->gle', normed, enc_query, precision=highest)))
    kv_rows = split_heads(rounded_both(jnp.einsum('gld,cde->cgle', normed, enc_kv, precision=highest)))

    def enc_row(packed):
        row_query, row_keys, row_values, row_segments, row_visible = packed
        allowed = (row_segments[:, None] == row_segments[None, :]) & row_visible[None, :]
        return attend(row_query, row_keys, row_values, enc_pos, allowed)
    enc_mixed = lax.map(jax.checkpoint(enc_row), (queries, kv_rows[0], kv_rows[1], enc_seg, visible))
    enc_mixed = enc_mixed.reshape(group_rows, ENC_LEN, INNER)
    enc_x1 = enc_x + low_back(jnp.einsum('gle,ed->gld', enc_mixed, enc_out_proj, precision=highest))
    normed_ff = low(rms_scale(enc_x1, enc_norm2))
    hidden = low(jax.nn.gelu(low_back(jnp.einsum('gld,df->glf', normed_ff, enc_ff_in, precision=highest))))
    enc_y = enc_x1 + low_back(jnp.einsum('glf,fd->gld', hidden, enc_ff_out, precision=highest))
    memory = low(rms_scale(enc_y, enc_final))
    dec_normed = low(rms_scale(dec_x, dec_norm1))
    dec_queries = split_heads(rounded_both(jnp.einsum('gmd,de->gme', dec_normed, dec_query, precision=highest)))
    dec_kv_rows = split_heads(rounded_both(jnp.einsum('gmd,cde->cgme', dec_normed, dec_kv, precision=highest)))

    def dec_row(packed):
        row_query, row_keys, row_values, row_segments = packed
        allowed = (row_segments[:, None] == row_segments[None, :]) & causal
        return attend(row_query, row_keys, row_values, dec_pos, allowed)
    self_mixed = lax.map(jax.checkpoint(dec_row), (dec_queries, dec_kv_rows[0], dec_kv_rows[1], dec_seg))
    self_mixed = self_mixed.reshape(group_rows, DEC_LEN, INNER)
    dec_x1 = dec_x + low_back(jnp.einsum('gme,ed->gmd', self_mixed, dec_out_proj, precision=highest))
    cross_normed = low(rms_scale(dec_x1, dec_norm2))
    cross_queries = split_heads(rounded_both(jnp.einsum('gmd,de->gme', cross_normed, cross_query, precision=highest)))
    cross_rows = split_heads(rounded_both(jnp.einsum('gld,cde->cgle', memory, cross_kv, precision=highest)))

    def cross_row(packed):
        row_query, row_keys, row_values, row_dec_seg, row_enc_seg, row_visible = packed
        allowed = (row_dec_seg[:, None] == row_enc_seg[None, :]) & row_visible[None, :]
        return attend(row_query, row_keys, row_values, 0.0, allowed)
    cross_mixed = lax.map(jax.checkpoint(cross_row), (cross_queries, cross_rows[0], cross_rows[1], dec_seg, enc_seg, visible))
    cross_mixed = cross_mixed.reshape(group_rows, DEC_LEN, INNER)
    dec_x2 = dec_x1 + low_back(jnp.einsum('gme,ed->gmd', cross_mixed, cross_out, precision=highest))
    ff_normed = low(rms_scale(dec_x2, dec_norm3))
    dec_hidden = low(jax.nn.gelu(low_back(jnp.einsum('gmd,df->gmf', ff_normed, dec_ff_in, precision=highest))))
    dec_x3 = dec_x2 + low_back(jnp.einsum('gmf,fd->gmd', dec_hidden, dec_ff_out, precision=highest))
    return (enc_y, dec_x3)

def reference(enc_in, enc_segments, enc_pad, enc_buckets, dec_in, dec_segments, dec_buckets, enc_cot, dec_cot, enc_norm1, enc_query, enc_kv, enc_out_proj, enc_bias, enc_norm2, enc_ff_in, enc_ff_out, enc_final, dec_norm1, dec_query, dec_kv, dec_out_proj, dec_bias, dec_norm2, cross_query, cross_kv, cross_out, dec_norm3, dec_ff_in, dec_ff_out):
    params = tuple((weight_item.astype(jnp.float32) for weight_item in (enc_norm1, enc_query, enc_kv, enc_out_proj, enc_bias, enc_norm2, enc_ff_in, enc_ff_out, enc_final, dec_norm1, dec_query, dec_kv, dec_out_proj, dec_bias, dec_norm2, cross_query, cross_kv, cross_out, dec_norm3, dec_ff_in, dec_ff_out)))
    group_rows = math.gcd(ROWS, max(1, 4096 // ENC_LEN))
    group_count = ROWS // group_rows

    def grouped(values):
        return values.reshape((group_count, group_rows) + values.shape[1:])
    inputs_grouped = (grouped(enc_in.astype(jnp.float32)), grouped(dec_in.astype(jnp.float32)), grouped(enc_segments), grouped(enc_pad), grouped(dec_segments), grouped(enc_cot.astype(jnp.float32)), grouped(dec_cot.astype(jnp.float32)))

    def group_step(totals, packed):
        enc_x, dec_x, enc_seg, pad_rows, dec_seg, enc_grad_out, dec_grad_out = packed

        def apply_layer(enc_inner, dec_inner, weight_set):
            return layer_forward(enc_inner, dec_inner, weight_set, enc_seg, pad_rows, dec_seg, enc_buckets, dec_buckets)
        outputs, pullback = jax.vjp(apply_layer, enc_x, dec_x, params)
        enc_grad, dec_grad, weight_grads = pullback((enc_grad_out, dec_grad_out))
        totals = jax.tree.map(lambda left, right: left + right, totals, weight_grads)
        return (totals, (outputs[0].astype(jnp.bfloat16), outputs[1].astype(jnp.bfloat16), enc_grad, dec_grad))
    zero_grads = jax.tree.map(jnp.zeros_like, params)
    totals, stacked = lax.scan(group_step, zero_grads, inputs_grouped)
    enc_out = stacked[0].reshape((ROWS,) + stacked[0].shape[2:])
    dec_out = stacked[1].reshape((ROWS,) + stacked[1].shape[2:])
    enc_grad = stacked[2].reshape((ROWS,) + stacked[2].shape[2:])
    dec_grad = stacked[3].reshape((ROWS,) + stacked[3].shape[2:])
    return (enc_out, dec_out, enc_grad, dec_grad, totals[0], totals[1], totals[2], totals[3], totals[4], totals[5], totals[6], totals[7], totals[8], totals[9], totals[10], totals[11], totals[12], totals[13], totals[14], totals[15], totals[16], totals[17], totals[18], totals[19], totals[20])
```

```python
import functools

import jax
import jax.numpy as jnp
from jax import lax
from jax.experimental import pallas as pl
from jax.experimental.pallas import tpu as pltpu
from jax.sharding import PartitionSpec as P

f32 = jnp.float32
bf16 = jnp.bfloat16
neg = -1e30
eps = 1e-06
LANE = 128
MIB = 1 << 20


def nn(a, b):
    return lax.dot_general(a, b, (((1,), (0,)), ((), ())), preferred_element_type=f32)


def nt(a, b):
    return lax.dot_general(a, b, (((1,), (1,)), ((), ())), preferred_element_type=f32)


def tn(a, b):
    return lax.dot_general(a, b, (((0,), (0,)), ((), ())), preferred_element_type=f32)


def total(terms):
    return functools.reduce(lambda a, b: a + b, terms)


def rms_parts(v):
    r = lax.rsqrt(jnp.mean(v * v, axis=-1, keepdims=True) + eps)
    return v * r, r


def rms(v, g):
    return (rms_parts(v)[0] * g).astype(bf16)


def rms_back(v, g, dn):
    vr, r = rms_parts(v)
    dg = jnp.sum(dn * vr, axis=0, keepdims=True)
    t = dn * g
    return r * (t - vr * jnp.mean(t * vr, axis=-1, keepdims=True)), dg


def gelu_both(u):
    c = 0.7978845608028654
    u2 = u * u
    t = jnp.tanh(u * (c + (c * 0.044715) * u2))
    half = 0.5 + 0.5 * t
    slope = half + (0.5 * u) * (1.0 - t * t) * (c + (3 * c * 0.044715) * u2)
    return u * half, slope


def params(vmem_mib=56, **kw):
    return pltpu.CompilerParams(vmem_limit_bytes=vmem_mib * MIB, **kw)


def cost(flops, nbytes):
    return pl.CostEstimate(flops=int(flops), bytes_accessed=int(nbytes), transcendentals=0)


def whole(a):
    return pl.BlockSpec(a.shape, lambda *_: (0,) * a.ndim, pipeline_mode=pl.Buffered(1))


def sds(shape, dtype):
    return jax.ShapeDtypeStruct(shape, dtype)


class Flat:
    def __init__(self, layout):
        self.at, row = {}, 0
        for name, kind in layout:
            self.at[name] = (row, kind)
            row += {"out": 256, "up": 1024, "down": 1024, "pair": 512, "one": 256, "tabs": 32}[kind]
        self.rows = row
        self.layout = layout

    def pack(self, arrays):
        parts = []
        for name, kind in self.layout:
            a = arrays[name]
            if kind in ("out", "down"):
                parts.append(a)
            elif kind == "up":
                parts += [a[:, :512], a[:, 512:]]
            elif kind == "pair":
                parts.append(jnp.concatenate([a[0], a[1]], axis=1))
            elif kind == "tabs":
                parts.append(
                    jnp.concatenate(
                        [jnp.pad(t, ((0, 0), (0, 256 - t.shape[1]))) for t in a], axis=1
                    )
                )
            else:
                parts.append(jnp.concatenate([a[:256], a[256:]], axis=1))
        return jnp.concatenate(parts, axis=0)


enc_qkv = Flat([("qk", "pair"), ("v", "one")])
enc_qkv_tabs = Flat([("qk", "pair"), ("v", "one"), ("tabs", "tabs")])
enc_mid = Flat([("ffo", "down"), ("ffi", "up"), ("ckv", "pair"), ("out", "out")])
dec_all = Flat(
    [
        ("ffo", "down"),
        ("ffi", "up"),
        ("cout", "out"),
        ("cq", "one"),
        ("out", "out"),
        ("qk", "pair"),
        ("v", "one"),
    ]
)


def bring(ids_ref, pieces, full, sems):
    n = len(pieces)
    size = full.shape[0] // n
    own = ids_ref[2] if n == 2 else ids_ref[3]
    copies = []
    for p, piece in enumerate(pieces):
        at = pl.multiple_of((p ^ own) * size, 16)
        copies.append(pltpu.make_async_copy(piece, full.at[pl.ds(at, size), :], sems.at[p]))
    for c in copies:
        c.start()
    for c in copies:
        c.wait()


def one_mul(a, w):
    return nn(a[:, :256], w[:, :256]) + nn(a[:, 256:], w[:, 256:])


def one_back(g, w):
    return jnp.concatenate([nt(g, w[:, :256]), nt(g, w[:, 256:])], axis=1)


def one_grad(a, g):
    full = tn(a, g)
    return jnp.concatenate([full[:256], full[256:]], axis=1)


def bucket_rows(rev_ref):
    rev = pltpu.roll(rev_ref[...], 1024 - 127, 1)
    return lax.broadcasted_iota(jnp.int32, (32, 1024), 0) == rev


def skew_rows(tab, rev_ref, skew_ref):
    w = tn(tab, bucket_rows(rev_ref).astype(bf16))
    for h in range(w.shape[0]):
        base = jnp.broadcast_to(w[h : h + 1], (LANE, 1024))
        skew_ref[h] = pltpu.roll(base, 0, 1, stride=1, stride_axis=0)


def diagonal_sums(a):
    rows, n = a.shape
    while rows > 1:
        rows //= 2
        a = a[:rows] + pltpu.roll(a[rows:], n - rows, 1)
    return a


def key_codes(seg, pad):
    start = (lax.broadcasted_iota(jnp.int32, seg.shape, 1) == 0) | (seg != pltpu.roll(seg, 1, 1))
    segf = seg.astype(f32)
    return segf, jnp.where((pad == 1) | start, segf, -1.0)


def as_column(row):
    return jnp.transpose(jnp.broadcast_to(row, (LANE, row.shape[1])))


def mask_add(seg, pad, out_ref):
    code, key = key_codes(seg, pad)
    keyc = as_column(key)
    for b in range(seg.shape[1] // LANE):
        out_ref[:, b * LANE : (b + 1) * LANE] = jnp.where(
            keyc == code[:, b * LANE : (b + 1) * LANE], 0.0, neg
        )


def pad_half(a_t, low):
    z = jnp.zeros_like(a_t)
    return jnp.concatenate([a_t, z] if low else [z, a_t], axis=0)


def skew_block(skew_ref, h, q0, width, keys=512):
    return jnp.concatenate(
        [
            skew_ref[h, :, 384 - LANE * b + q0 : 384 - LANE * b + q0 + width]
            for b in range(keys // LANE)
        ],
        axis=0,
    )


QB = 256


def enc_fwd_kernel(own, ids_ref, x_ref, g_ref, seg_ref, pad_ref, rev_ref, *rest):
    step = pl.program_id(0)
    if own:
        tab_ref, wq_ref, wkv_ref, qkv_ref, o_ref, lse_ref, skew, madd, o_t = rest
    else:
        p0, p1, qkv_ref, o_ref, lse_ref, w_ref, tab_ref, skew, madd, o_t, sems = rest

        @pl.when(step == 0)
        def _():
            bring(ids_ref, (p0, p1), w_ref, sems)
            tab_ref[...] = w_ref[768:800, :]

    @pl.when(step == 0)
    def _():
        skew_rows(tab_ref[:, 0:4], rev_ref, skew)

    row = pl.ds(ids_ref[1] + step, 1)
    mask_add(seg_ref[row, :], pad_ref[row, :], madd)
    n1 = rms(x_ref[0].astype(f32), g_ref[...])
    if own:
        q = nn(n1, wq_ref[...]).astype(bf16)
        k = nn(n1, wkv_ref[0]).astype(bf16)
        v = nn(n1, wkv_ref[1]).astype(bf16)
    else:
        qk = nn(n1, w_ref[0:512, :]).astype(bf16)
        q, k = qk[:, :256], qk[:, 256:]
        v = one_mul(n1, w_ref[512:768, :]).astype(bf16)
    qkv_ref[0, :, 0:256] = q
    qkv_ref[0, :, 256:512] = k
    qkv_ref[0, :, 512:768] = v
    q_t, v_t = jnp.transpose(q), jnp.transpose(v)
    for h in range(4):
        pair = slice(LANE * (h // 2), LANE * (h // 2) + LANE)
        rows = slice(64 * h, 64 * h + 64)
        k2 = k[:, pair]
        qz = pad_half(q_t[rows], h % 2 == 0)
        for b in range(0, 512, QB):
            s = nn(k2, qz[:, b : b + QB]) + skew_block(skew, h, b, QB) + madd[:, b : b + QB]
            m = jnp.max(s, axis=0, keepdims=True)
            e = jnp.exp(s - m)
            norm = jnp.sum(e, axis=0, keepdims=True)
            o_t[rows, b : b + QB] = nn(v_t[rows], e.astype(bf16)) * (1.0 / norm)
            lse_ref[0, h : h + 1, b : b + QB] = m + jnp.log(norm)
    o_ref[0] = jnp.transpose(o_t[...]).astype(bf16)


smem = pl.BlockSpec(memory_space=pltpu.SMEM)
anywhere = pl.BlockSpec(memory_space=pl.ANY)


def row_block(width, n=512, at=0):
    return pl.BlockSpec((1, n, width), lambda r: (r, 0, at))


def enc_fwd(ids, x, g, seg, pad, rev, ws):
    rows = x.shape[0]
    own = len(ws) == 3
    more = [] if own else [sds((enc_qkv_tabs.rows, 512), bf16), sds((32, 512), bf16)]
    return pl.pallas_call(
        functools.partial(enc_fwd_kernel, own),
        name="enc_attend_own" if own else "enc_attend_other",
        grid=(rows,),
        in_specs=[smem, row_block(512), whole(g), whole(seg), whole(pad), whole(rev)]
        + [whole(w) if own else anywhere for w in ws],
        out_specs=[row_block(768), row_block(256), row_block(512, 4)] + [whole(a) for a in more],
        out_shape=[
            sds((rows, 512, 768), bf16),
            sds((rows, 512, 256), bf16),
            sds((rows, 4, 512), f32),
        ]
        + more,
        scratch_shapes=[
            pltpu.VMEM((4, LANE, 1024), f32),
            pltpu.VMEM((512, 512), f32),
            pltpu.VMEM((256, 512), f32),
        ]
        + ([] if own else [pltpu.SemaphoreType.DMA((2,))]),
        compiler_params=params(),
        cost_estimate=cost(8e9, 4e6),
    )(ids, x, g, seg, pad, rev, *ws)


def enc_bwd_kernel(
    rows_n,
    ids_ref,
    x_ref,
    g_ref,
    seg_ref,
    pad_ref,
    rev_ref,
    tab_ref,
    qkv_ref,
    o_ref,
    do_ref,
    lse_ref,
    dqkv_ref,
    keep_ref,
    send_ref,
    dtab_ref,
    skew,
    dskew,
    madd,
    p_s,
    ds_s,
    dq_t,
    dv_acc,
    dk_acc,
    acc,
):
    step = pl.program_id(0)

    @pl.when(step == 0)
    def _():
        skew_rows(tab_ref[:, 0:4], rev_ref, skew)
        dskew[...] = jnp.zeros_like(dskew)

    row = pl.ds(ids_ref[1] + step, 1)
    mask_add(seg_ref[row, :], pad_ref[row, :], madd)
    q, k, v = qkv_ref[0, :, 0:256], qkv_ref[0, :, 256:512], qkv_ref[0, :, 512:768]
    do = do_ref[0]
    q_t, k_t, do_t = jnp.transpose(q), jnp.transpose(k), jnp.transpose(do)
    o_t = jnp.transpose(o_ref[0])
    lane = lax.broadcasted_iota(jnp.int32, (512, LANE), 1)
    for h in range(4):
        pair = slice(LANE * (h // 2), LANE * (h // 2) + LANE)
        rows = slice(64 * h, 64 * h + 64)
        low = h % 2 == 0
        k2, v2 = k[:, pair], v[:, pair]
        qz, doz = pad_half(q_t[rows], low), pad_half(do_t[rows], low)
        inner = jnp.sum(
            do_t[rows].astype(f32) * o_t[rows].astype(f32), axis=0, keepdims=True
        )
        for b in range(0, 512, QB):
            cols = slice(b, b + QB)
            s = nn(k2, qz[:, cols]) + skew_block(skew, h, b, QB) + madd[:, cols]
            p = jnp.exp(s - lse_ref[0, h : h + 1, cols])
            ds = p * (nn(v2, doz[:, cols]) - inner[:, cols])
            p_s[:, cols] = p.astype(bf16)
            ds_s[:, cols] = ds.astype(bf16)
            for kb in range(4):
                at = 384 - LANE * kb + b
                dskew[h, :, at : at + QB] += ds[LANE * kb : LANE * kb + LANE]
        mine = (lane < 64) if low else (lane >= 64)
        dv2 = nn(p_s[...], jnp.where(mine, do[:, pair], jnp.zeros((), bf16)))
        dk2 = nn(ds_s[...], jnp.where(mine, q[:, pair], jnp.zeros((), bf16)))
        if low:
            dv_acc[:, pair] = dv2
            dk_acc[:, pair] = dk2
        else:
            dv_acc[:, pair] += dv2
            dk_acc[:, pair] += dk2
        dq_t[rows] = nn(k_t[rows], ds_s[...])
    dqkv_ref[0, :, 0:256] = jnp.transpose(dq_t[...]).astype(bf16)
    dqkv_ref[0, :, 256:512] = dk_acc[...].astype(bf16)
    dqkv_ref[0, :, 512:768] = dv_acc[...].astype(bf16)
    n1_t = jnp.transpose(rms(x_ref[0].astype(f32), g_ref[...]))
    dqk = nn(n1_t, dqkv_ref[0, :, 0:512])
    dv = nn(n1_t, dqkv_ref[0, :, 512:768])
    dv = jnp.concatenate([dv[:256], dv[256:]], axis=1)

    @pl.when(step == 0)
    def _():
        acc[0:512] = dqk
        acc[512:768] = dv

    @pl.when(step > 0)
    def _():
        acc[0:512] += dqk
        acc[512:768] += dv

    @pl.when(step == rows_n - 1)
    def _():
        place(ids_ref, acc, keep_ref, send_ref)
        onehot = bucket_rows(rev_ref)
        out_lane = lax.broadcasted_iota(jnp.int32, (32, LANE), 1)
        dtab = jnp.zeros((32, LANE), f32)
        for h in range(4):
            diag = diagonal_sums(dskew[h])
            col = jnp.sum(jnp.where(onehot, diag, 0.0), axis=1, keepdims=True)
            dtab = dtab + jnp.where(out_lane == h, col, 0.0)
        dtab_ref[...] = dtab


def place(ids_ref, acc, keep_ref, send_ref):
    chunks = 16
    size = acc.shape[0] // chunks
    own = ids_ref[0]
    high = own // 8
    low = own % 8
    for j in range(chunks):
        at = pl.multiple_of(((j % 8) ^ low) * size, 16)
        piece = acc[j * size : (j + 1) * size].astype(bf16)

        @pl.when(high == j // 8)
        def _():
            keep_ref[pl.ds(at, size), :] = piece

        @pl.when(high != j // 8)
        def _():
            send_ref[pl.ds(at, size), :] = piece


def enc_bwd(half_at, ids, x, g, seg, pad, rev, tab, qkv, o, do, lse):
    rows = x.shape[0]
    half = enc_qkv.rows // 2
    return pl.pallas_call(
        functools.partial(enc_bwd_kernel, rows),
        name="enc_attend_other_back" if half_at else "enc_attend_own_back",
        grid=(rows,),
        in_specs=[
            smem,
            row_block(512),
            whole(g),
            whole(seg),
            whole(pad),
            whole(rev),
            whole(tab),
            row_block(768),
            row_block(256),
            row_block(256, at=half_at),
            row_block(512, 4),
        ],
        out_specs=[
            row_block(768),
            pl.BlockSpec((half, 512), lambda r: (0, 0)),
            pl.BlockSpec((half, 512), lambda r: (0, 0)),
            pl.BlockSpec((32, LANE), lambda r: (0, 0)),
        ],
        out_shape=[
            sds((rows, 512, 768), bf16),
            sds((half, 512), bf16),
            sds((half, 512), bf16),
            sds((32, LANE), f32),
        ],
        scratch_shapes=[
            pltpu.VMEM((4, LANE, 1024), f32),
            pltpu.VMEM((4, LANE, 1024), f32),
            pltpu.VMEM((512, 512), f32),
            pltpu.VMEM((512, 512), bf16),
            pltpu.VMEM((512, 512), bf16),
            pltpu.VMEM((256, 512), f32),
            pltpu.VMEM((512, 256), f32),
            pltpu.VMEM((512, 256), f32),
            pltpu.VMEM((enc_qkv.rows, 512), f32),
        ],
        compiler_params=params(),
        cost_estimate=cost(16e9, 8e6),
    )(ids, x, g, seg, pad, rev, tab, qkv, o, do, lse)


class Mid:
    def __init__(self, refs):
        if len(refs) == 1:
            (w,) = refs
            at = {n: r for n, (r, _) in enc_mid.at.items()}
            self.ffo = lambda c: w[at["ffo"] + 512 * c : at["ffo"] + 512 * c + 512, :]
            self.ffi = lambda c: w[at["ffi"] + 512 * c : at["ffi"] + 512 * c + 512, :]
            self.ckv = lambda c: w[at["ckv"] : at["ckv"] + 512, 256 * c : 256 * c + 256]
            self.out = lambda: w[at["out"] : at["out"] + 256, :]
        else:
            ffo, ffi, ckv, out = refs
            self.ffo = lambda c: ffo[512 * c : 512 * c + 512, :]
            self.ffi = lambda c: ffi[:, 512 * c : 512 * c + 512]
            self.ckv = lambda c: ckv[c]
            self.out = lambda: out[...]


def mid_fwd_kernel(ids_ref, x_ref, oa_ref, ob_ref, g2_ref, gf_ref, *rest):
    pieces = rest[4:8]
    x1_ref, y_ref, out_ref, h_ref, gp_ref, kv_ref, w_ref, sems = rest[8:]
    halves = (Mid(rest[:4]), Mid([w_ref]))

    @pl.when(pl.program_id(0) == 0)
    def _():
        bring(ids_ref, pieces, w_ref, sems)

    x1 = x_ref[...].astype(f32) + total(
        [nn(oa_ref[...], halves[0].out()), nn(ob_ref[...], halves[1].out())]
    )
    x1_ref[...] = x1
    m1 = rms(x1, g2_ref[...])
    terms = []
    for i, w in enumerate(halves):
        for c in range(2):
            u = nn(m1, w.ffi(c))
            h, slope = gelu_both(u)
            h = h.astype(bf16)
            cols = slice(1024 * i + 512 * c, 1024 * i + 512 * c + 512)
            h_ref[:, cols] = h
            gp_ref[:, cols] = slope.astype(bf16)
            terms.append(nn(h, w.ffo(c)))
    y = x1 + total(terms)
    y_ref[...] = y
    out_ref[...] = y.astype(bf16)
    mem = rms(y, gf_ref[...])
    for c in range(2):
        for i, w in enumerate(halves):
            at = 512 * c + 256 * i
            kv_ref[:, at : at + 256] = nn(mem, w.ckv(c)).astype(bf16)


def tile_block(tile, width):
    return pl.BlockSpec((tile, width), lambda t: (t, 0))


def mid_fwd(ids, x, oa, ob, g2, gf, own, pieces, tile=256):
    n = x.shape[0]
    return pl.pallas_call(
        mid_fwd_kernel,
        name="enc_middle",
        grid=(n // tile,),
        in_specs=[smem, tile_block(tile, 512), tile_block(tile, 256), tile_block(tile, 256), whole(g2), whole(gf)]
        + [whole(w) for w in own]
        + [anywhere] * len(pieces),
        out_specs=[
            tile_block(tile, 512),
            tile_block(tile, 512),
            tile_block(tile, 512),
            tile_block(tile, 2048),
            tile_block(tile, 2048),
            tile_block(tile, 1024),
            whole(sds((enc_mid.rows, 512), bf16)),
        ],
        out_shape=[
            sds((n, 512), f32),
            sds((n, 512), f32),
            sds((n, 512), bf16),
            sds((n, 2048), bf16),
            sds((n, 2048), bf16),
            sds((n, 1024), bf16),
            sds((enc_mid.rows, 512), bf16),
        ],
        scratch_shapes=[pltpu.SemaphoreType.DMA((len(pieces),))],
        compiler_params=params(),
        cost_estimate=cost(10e9, 2e7),
    )(ids, x, oa, ob, g2, gf, *own, *pieces)


def mid_bwd_kernel(steps, dkv_ref, y_ref, cot_ref, x1_ref, h_ref, gp_ref, oa_ref, ob_ref, g2_ref, gf_ref, ids_ref, *rest):
    halves = (Mid(rest[:4]), Mid(rest[4:5]))
    dx1_ref, do_ref, ka_ref, sa_ref, kb_ref, sb_ref, dg2_ref, dgf_ref, acc_a, acc_b = rest[5:]
    accs = (acc_a, acc_b)
    step = pl.program_id(0)
    at = {n: r for n, (r, _) in enc_mid.at.items()}

    def add(i, row, value, lanes=slice(None)):
        rows = slice(row, row + value.shape[0])

        @pl.when(step == 0)
        def _():
            accs[i][rows, lanes] = value

        @pl.when(step > 0)
        def _():
            accs[i][rows, lanes] += value

    y = y_ref[...]
    mem = rms(y, gf_ref[...])
    terms = []
    for i, w in enumerate(halves):
        for c in range(2):
            d = dkv_ref[:, 512 * c + 256 * i : 512 * c + 256 * i + 256]
            terms.append(nt(d, w.ckv(c)))
            add(i, at["ckv"], tn(mem, d), slice(256 * c, 256 * c + 256))
    part, dgf = rms_back(y, gf_ref[...], total(terms))
    dy = cot_ref[...].astype(f32) + part
    g = dy.astype(bf16)
    x1 = x1_ref[...]
    m1 = rms(x1, g2_ref[...])
    terms = []
    for i, w in enumerate(halves):
        for c in range(2):
            cols = slice(1024 * i + 512 * c, 1024 * i + 512 * c + 512)
            du = (nt(g, w.ffo(c)) * gp_ref[:, cols].astype(f32)).astype(bf16)
            add(i, at["ffo"] + 512 * c, tn(h_ref[:, cols], g))
            add(i, at["ffi"] + 512 * c, tn(m1, du))
            terms.append(nt(du, w.ffi(c)))
    part, dg2 = rms_back(x1, g2_ref[...], total(terms))
    dx1 = dy + part
    dx1_ref[...] = dx1
    g = dx1.astype(bf16)
    for i, (w, o_ref) in enumerate(zip(halves, (oa_ref, ob_ref))):
        do_ref[:, 256 * i : 256 * i + 256] = nt(g, w.out()).astype(bf16)
        add(i, at["out"], tn(o_ref[...], g))

    @pl.when(step == 0)
    def _():
        dg2_ref[...] = dg2
        dgf_ref[...] = dgf

    @pl.when(step > 0)
    def _():
        dg2_ref[...] += dg2
        dgf_ref[...] += dgf

    @pl.when(step == steps - 1)
    def _():
        place(ids_ref, acc_a, ka_ref, sa_ref)
        place(ids_ref, acc_b, kb_ref, sb_ref)


def mid_bwd(dkv, y, cot, x1, h, gp, oa, ob, g2, gf, pos, own, oth, tile=512):
    n = y.shape[0]
    ws = list(own) + [oth]
    half = enc_mid.rows // 2
    fixed = lambda shape: pl.BlockSpec(shape, lambda t: (0, 0), pipeline_mode=pl.Buffered(1))
    return pl.pallas_call(
        functools.partial(mid_bwd_kernel, n // tile),
        name="enc_middle_back",
        grid=(n // tile,),
        in_specs=[
            tile_block(tile, 1024),
            tile_block(tile, 512),
            tile_block(tile, 512),
            tile_block(tile, 512),
            tile_block(tile, 2048),
            tile_block(tile, 2048),
            tile_block(tile, 256),
            tile_block(tile, 256),
            whole(g2),
            whole(gf),
            pl.BlockSpec(memory_space=pltpu.SMEM),
        ]
        + [whole(w) for w in ws],
        out_specs=[tile_block(tile, 512), tile_block(tile, 512)]
        + [fixed((half, 512))] * 4
        + [fixed((1, 512))] * 2,
        out_shape=[sds((n, 512), f32), sds((n, 512), bf16)]
        + [sds((half, 512), bf16)] * 4
        + [sds((1, 512), f32)] * 2,
        scratch_shapes=[pltpu.VMEM((enc_mid.rows, 512), f32)] * 2,
        compiler_params=params(60),
        cost_estimate=cost(22e9, 3e7),
    )(dkv, y, cot, x1, h, gp, oa, ob, g2, gf, pos, *ws)


def enc_last_kernel(x_ref, dx1_ref, da_ref, db_ref, g_ref, wq_ref, wkv_ref, w_ref, out_ref, dg_ref):
    step = pl.program_id(0)
    da, db = da_ref[...], db_ref[...]
    dn = (
        nt(da[:, 0:256], wq_ref[...])
        + nt(da[:, 256:512], wkv_ref[0])
        + nt(da[:, 512:768], wkv_ref[1])
        + nt(db[:, 0:512], w_ref[0:512, :])
        + one_back(db[:, 512:768], w_ref[512:768, :])
    )
    part, dg = rms_back(x_ref[...].astype(f32), g_ref[...], dn)
    out_ref[...] = dx1_ref[...] + part

    @pl.when(step == 0)
    def _():
        dg_ref[...] = dg

    @pl.when(step > 0)
    def _():
        dg_ref[...] += dg


def enc_last(x, dx1, da, db, g, own, oth, tile=256):
    n = x.shape[0]
    ws = list(own) + [oth]
    return pl.pallas_call(
        enc_last_kernel,
        name="enc_input_back",
        grid=(n // tile,),
        in_specs=[
            tile_block(tile, 512),
            tile_block(tile, 512),
            tile_block(tile, 768),
            tile_block(tile, 768),
            whole(g),
        ]
        + [whole(w) for w in ws],
        out_specs=[tile_block(tile, 512), pl.BlockSpec((1, 512), lambda t: (0, 0))],
        out_shape=[sds((n, 512), f32), sds((1, 512), f32)],
        compiler_params=params(),
        cost_estimate=cost(4e9, 1e7),
    )(x, dx1, da, db, g, *ws)


class Dec:
    def __init__(self, refs):
        if len(refs) == 1:
            (w,) = refs
            at = {n: r for n, (r, _) in dec_all.at.items()}
            self.ffo = lambda c: w[at["ffo"] + 512 * c : at["ffo"] + 512 * c + 512, :]
            self.ffi = lambda c: w[at["ffi"] + 512 * c : at["ffi"] + 512 * c + 512, :]
            self.cout = lambda: w[at["cout"] : at["cout"] + 256, :]
            self.cq = lambda c: w[at["cq"] : at["cq"] + 256, 256 * c : 256 * c + 256]
            self.out = lambda: w[at["out"] : at["out"] + 256, :]
            self.qk = lambda c: w[at["qk"] : at["qk"] + 512, 256 * c : 256 * c + 256]
            self.v = lambda c: w[at["v"] : at["v"] + 256, 256 * c : 256 * c + 256]
        else:
            ffo, ffi, cout, cq, out, q, kv = refs
            self.ffo = lambda c: ffo[512 * c : 512 * c + 512, :]
            self.ffi = lambda c: ffi[:, 512 * c : 512 * c + 512]
            self.cout = lambda: cout[...]
            self.cq = lambda c: cq[256 * c : 256 * c + 256, :]
            self.out = lambda: out[...]
            self.qk = lambda c: q[...] if c == 0 else kv[0]
            self.v = lambda c: kv[1, 256 * c : 256 * c + 256, :]


def two_mul(a, w):
    return nn(a[:, :256], w(0)) + nn(a[:, 256:], w(1))


def two_back(g, w):
    return jnp.concatenate([nt(g, w(0)), nt(g, w(1))], axis=1)


def spread_t(a_t, width):
    tiled = jnp.concatenate([a_t] * 4, axis=1)
    head = lax.broadcasted_iota(jnp.int32, tiled.shape, 0) // 64
    block = lax.broadcasted_iota(jnp.int32, tiled.shape, 1) // width
    return jnp.where(head == block, tiled, jnp.zeros((), a_t.dtype))


def spread(a, height):
    tiled = jnp.concatenate([a] * 4, axis=0)
    block = lax.broadcasted_iota(jnp.int32, tiled.shape, 0) // height
    head = lax.broadcasted_iota(jnp.int32, tiled.shape, 1) // 64
    return jnp.where(head == block, tiled, jnp.zeros((), a.dtype))


def fold(full, height):
    head = lax.broadcasted_iota(jnp.int32, (height, 256), 1) // 64
    total = jnp.zeros((height, 256), f32)
    for h in range(4):
        total = total + jnp.where(head == h, full[height * h : height * h + height], 0.0)
    return total


def dec_bucket_rows(buckets_ref):
    b = buckets_ref[...]
    b = jnp.concatenate([b, jnp.full((1, LANE - b.shape[1]), -1, jnp.int32)], axis=1)
    return lax.broadcasted_iota(jnp.int32, (32, LANE), 0) == b


def dec_bias_rows(tab, buckets_ref):
    w = tn(tab, dec_bucket_rows(buckets_ref).astype(bf16))
    return jnp.concatenate(
        [
            pltpu.roll(jnp.broadcast_to(w[h : h + 1], (LANE, LANE)), 0, 1, stride=1, stride_axis=0)
            for h in range(4)
        ],
        axis=1,
    )


def dec_self_mask(ids_ref, dseg_ref, rows):
    code = jnp.concatenate(
        [(dseg_ref[pl.ds(ids_ref[1] + r, 1), :] + 8 * r).astype(f32) for r in range(rows)], axis=1
    )
    key = as_column(code)
    j = lax.broadcasted_iota(jnp.int32, (LANE, LANE), 0)
    i = lax.broadcasted_iota(jnp.int32, (LANE, LANE), 1)
    one = jnp.where((key == code) & (j <= i), 0.0, neg)
    return jnp.concatenate([one] * 4, axis=1)


def dec_first_kernel(ids_ref, x_ref, g1_ref, g2_ref, dseg_ref, buckets_ref, taba_ref, tabb_ref, *rest):
    pieces = rest[7:11]
    qkv_ref, o_ref, lse_ref, z1_ref, q3_ref, w_ref, sems = rest[11:]
    halves = (Dec(rest[:7]), Dec([w_ref]))
    bring(ids_ref, pieces, w_ref, sems)
    z = x_ref[...].astype(f32)
    n2 = rms(z, g1_ref[...])
    mask = dec_self_mask(ids_ref, dseg_ref, x_ref.shape[0] // 64)
    terms = []
    for i, (w, tab) in enumerate(zip(halves, (taba_ref[...], tabb_ref[:, 256:260]))):
        q = nn(n2, w.qk(0)).astype(bf16)
        k = nn(n2, w.qk(1)).astype(bf16)
        v = two_mul(n2, w.v).astype(bf16)
        for c, a in enumerate((q, k, v)):
            qkv_ref[:, 512 * c + 256 * i : 512 * c + 256 * i + 256] = a
        s = nn(k, spread_t(jnp.transpose(q), LANE)) + dec_bias_rows(tab, buckets_ref) + mask
        m = jnp.max(s, axis=0, keepdims=True)
        e = jnp.exp(s - m)
        norm = jnp.sum(e, axis=0, keepdims=True)
        p = (e * (1.0 / norm)).astype(bf16)
        lse_ref[i : i + 1, :] = m + jnp.log(norm)
        o = fold(tn(p, v), LANE).astype(bf16)
        o_ref[:, 256 * i : 256 * i + 256] = o
        terms.append(nn(o, w.out()))
    z1 = z + total(terms)
    z1_ref[...] = z1
    n3 = rms(z1, g2_ref[...])
    for i, w in enumerate(halves):
        q3_ref[:, 256 * i : 256 * i + 256] = two_mul(n3, w.cq).astype(bf16)


def dec_first(ids, x, g1, g2, dseg, buckets, taba, tabb, own, pieces):
    n = x.shape[0]
    ins = [x, g1, g2, dseg, buckets, taba, tabb, *own]
    return pl.pallas_call(
        dec_first_kernel,
        name="dec_self",
        grid=(1,),
        in_specs=[smem] + [whole(a) for a in ins] + [anywhere] * len(pieces),
        out_specs=[
            pl.BlockSpec(s, lambda t: (0, 0))
            for s in ((n, 1536), (n, 512), (2, 512), (n, 512), (n, 512), (dec_all.rows, 512))
        ],
        out_shape=[
            sds((n, 1536), bf16),
            sds((n, 512), bf16),
            sds((2, 512), f32),
            sds((n, 512), f32),
            sds((n, 512), bf16),
            sds((dec_all.rows, 512), bf16),
        ],
        scratch_shapes=[pltpu.SemaphoreType.DMA((len(pieces),))],
        compiler_params=params(),
        cost_estimate=cost(1e9, 8e6),
    )(ids, *ins, *pieces)


def dec_main_kernel(
    x_ref,
    cot_ref,
    g1_ref,
    g2_ref,
    g3_ref,
    buckets_ref,
    dseg_ref,
    seg_ref,
    pad_ref,
    ids_ref,
    qkv_ref,
    o2_ref,
    lse_ref,
    z1_ref,
    q3_ref,
    kv_ref,
    taba_ref,
    tabb_ref,
    *rest,
):
    halves = (Dec(rest[:7]), Dec(rest[7:8]))
    out_ref, dx_ref, dkv_ref, ka_ref, sa_ref, kb_ref, sb_ref, dg_ref, dtab_ref = rest[8:17]
    madd, p_s, acc_a, acc_b = rest[17:]
    accs = (acc_a, acc_b)
    at = {n: r for n, (r, _) in dec_all.at.items()}
    rows_n = x_ref.shape[0] // 64
    z1 = z1_ref[...]
    mixed = [[None] * rows_n, [None] * rows_n]
    for r in range(rows_n):
        row = pl.ds(ids_ref[1] + r, 1)
        keyc = as_column(key_codes(seg_ref[row, :], pad_ref[row, :])[1])
        code = dseg_ref[row, :].astype(f32)
        madd[...] = jnp.where(keyc == jnp.concatenate([code, code], axis=1), 0.0, neg)
        both = jnp.concatenate([madd[...]] * 2, axis=1)
        for i in range(2):
            cols = slice(256 * i, 256 * i + 256)
            k3 = kv_ref[512 * r : 512 * r + 512, 256 * i : 256 * i + 256]
            v3 = kv_ref[512 * r : 512 * r + 512, 512 + 256 * i : 512 + 256 * i + 256]
            q_t = jnp.transpose(q3_ref[64 * r : 64 * r + 64, cols])
            s = nn(k3, spread_t(q_t, 64)) + both
            m = jnp.max(s, axis=0, keepdims=True)
            e = jnp.exp(s - m)
            p = e * (1.0 / jnp.sum(e, axis=0, keepdims=True))
            p_s[2 * r + i] = p
            mixed[i][r] = fold(tn(p.astype(bf16), v3), 64).astype(bf16)
    o3 = [jnp.concatenate(m, axis=0) for m in mixed]
    z2 = z1 + total([nn(o, w.cout()) for o, w in zip(o3, halves)])
    n4 = rms(z2, g3_ref[...])
    terms, kept = [], []
    for i, w in enumerate(halves):
        for c in range(2):
            h, slope = gelu_both(nn(n4, w.ffi(c)))
            h = h.astype(bf16)
            kept.append((h, slope))
            terms.append(nn(h, w.ffo(c)))
    out_ref[...] = (z2 + total(terms)).astype(bf16)
    g = cot_ref[...]
    terms = []
    for i, w in enumerate(halves):
        for c in range(2):
            h, slope = kept[2 * i + c]
            accs[i][at["ffo"] + 512 * c : at["ffo"] + 512 * c + 512] = tn(h, g)
            du = (nt(g, w.ffo(c)) * slope).astype(bf16)
            accs[i][at["ffi"] + 512 * c : at["ffi"] + 512 * c + 512] = tn(n4, du)
            terms.append(nt(du, w.ffi(c)))
    part, dg3 = rms_back(z2, g3_ref[...], total(terms))
    dz2 = g.astype(f32) + part
    g = dz2.astype(bf16)
    n3 = rms(z1, g2_ref[...])
    terms = []
    for i, w in enumerate(halves):
        cols = slice(256 * i, 256 * i + 256)
        accs[i][at["cout"] : at["cout"] + 256] = tn(o3[i], g)
        do = nt(g, w.cout()).astype(bf16)
        dq = []
        for r in range(rows_n):
            k3 = kv_ref[512 * r : 512 * r + 512, 256 * i : 256 * i + 256]
            v3 = kv_ref[512 * r : 512 * r + 512, 512 + 256 * i : 512 + 256 * i + 256]
            do_r = do[64 * r : 64 * r + 64]
            p = p_s[2 * r + i]
            dp = nn(v3, spread_t(jnp.transpose(do_r), 64))
            ds = (p * (dp - jnp.sum(p * dp, axis=0, keepdims=True))).astype(bf16)
            rows = slice(512 * r, 512 * r + 512)
            dkv_ref[rows, 256 * i : 256 * i + 256] = nn(
                ds, spread(q3_ref[64 * r : 64 * r + 64, cols], 64)
            ).astype(bf16)
            dkv_ref[rows, 512 + 256 * i : 512 + 256 * i + 256] = nn(
                p.astype(bf16), spread(do_r, 64)
            ).astype(bf16)
            dq.append(fold(tn(ds, k3), 64).astype(bf16))
        dq = jnp.concatenate(dq, axis=0)
        accs[i][at["cq"] : at["cq"] + 256] = one_grad(n3, dq)
        terms.append(two_back(dq, w.cq))
    part, dg2 = rms_back(z1, g2_ref[...], total(terms))
    dz1 = dz2 + part
    g = dz1.astype(bf16)
    z = x_ref[...].astype(f32)
    n2 = rms(z, g1_ref[...])
    mask = dec_self_mask(ids_ref, dseg_ref, rows_n)
    terms = []
    dtab = jnp.zeros((32, LANE), f32)
    out_lane = lax.broadcasted_iota(jnp.int32, (32, LANE), 1)
    onehot = dec_bucket_rows(buckets_ref)
    for i, (w, tab) in enumerate(zip(halves, (taba_ref[...], tabb_ref[:, 256:260]))):
        q, k, v = (qkv_ref[:, 512 * c + 256 * i : 512 * c + 256 * i + 256] for c in range(3))
        accs[i][at["out"] : at["out"] + 256] = tn(o2_ref[:, 256 * i : 256 * i + 256], g)
        do = nt(g, w.out()).astype(bf16)
        s = nn(k, spread_t(jnp.transpose(q), LANE)) + dec_bias_rows(tab, buckets_ref) + mask
        p = jnp.exp(s - lse_ref[i : i + 1, :])
        dp = nn(v, spread_t(jnp.transpose(do), LANE))
        ds = p * (dp - jnp.sum(p * dp, axis=0, keepdims=True))
        for h in range(4):
            diag = diagonal_sums(ds[:, LANE * h : LANE * h + LANE])
            col = jnp.sum(jnp.where(onehot, diag, 0.0), axis=1, keepdims=True)
            dtab = dtab + jnp.where(out_lane == 4 * i + h, col, 0.0)
        ds = ds.astype(bf16)
        dk = nn(ds, spread(q, LANE)).astype(bf16)
        dv = nn(p.astype(bf16), spread(do, LANE)).astype(bf16)
        dq = fold(tn(ds, k), LANE).astype(bf16)
        accs[i][at["qk"] : at["qk"] + 512, 0:256] = tn(n2, dq)
        accs[i][at["qk"] : at["qk"] + 512, 256:512] = tn(n2, dk)
        accs[i][at["v"] : at["v"] + 256] = one_grad(n2, dv)
        terms += [nt(dq, w.qk(0)), nt(dk, w.qk(1)), two_back(dv, w.v)]
    part, dg1 = rms_back(z, g1_ref[...], total(terms))
    dx_ref[...] = dz1 + part
    dg_ref[...] = jnp.concatenate([dg1, dg2, dg3], axis=0)
    dtab_ref[...] = dtab
    place(ids_ref, acc_a, ka_ref, sa_ref)
    place(ids_ref, acc_b, kb_ref, sb_ref)


def dec_main(x, cot, g1, g2, g3, buckets, dseg, seg, pad, ids, qkv, o2, lse, z1, q3, kv, taba, tabb, own, oth):
    n = x.shape[0]
    ins = [x, cot, g1, g2, g3, buckets, dseg, seg, pad, ids, qkv, o2, lse, z1, q3, kv, taba, tabb, *own, oth]
    half = dec_all.rows // 2
    outs = [
        sds((n, 512), bf16),
        sds((n, 512), f32),
        sds((kv.shape[0], 1024), bf16),
        sds((half, 512), bf16),
        sds((half, 512), bf16),
        sds((half, 512), bf16),
        sds((half, 512), bf16),
        sds((3, 512), f32),
        sds((32, LANE), f32),
    ]
    specs = [whole(a) for a in ins]
    specs[9] = smem
    return pl.pallas_call(
        dec_main_kernel,
        name="dec_cross_ff_back",
        grid=(1,),
        in_specs=specs,
        out_specs=[whole(a) for a in outs],
        out_shape=outs,
        scratch_shapes=[
            pltpu.VMEM((512, LANE), f32),
            pltpu.VMEM((4, 512, 256), f32),
            pltpu.VMEM((dec_all.rows, 512), f32),
            pltpu.VMEM((dec_all.rows, 512), f32),
        ],
        compiler_params=params(60),
        cost_estimate=cost(6e9, 2e7),
    )(*ins)


def natural(flat):
    shapes = {"out": (256, 512), "down": (1024, 512), "up": (512, 1024), "pair": (2, 512, 256), "one": (512, 256)}
    res = []
    for name, kind in flat.layout:
        if name == "qk":
            res.append(("q", (512, 256)))
        elif name == "v":
            res.append(("kv", (2, 512, 256)))
        else:
            res.append((name, shapes[kind]))
    return res


def finish_kernel(flat, ids_ref, a_ref, b_ref, *rest):
    outs, full = dict(zip([n for n, _ in natural(flat)], rest[:-1])), rest[-1]
    size = flat.rows // 16
    own = ids_ref[0]
    high = own // 8
    low = own % 8
    for j in range(16):
        at = pl.multiple_of(((j % 8) ^ low) * size, 16)

        @pl.when(high == j // 8)
        def _():
            full[j * size : (j + 1) * size] = a_ref[pl.ds(at, size), :].astype(f32)

        @pl.when(high != j // 8)
        def _():
            full[j * size : (j + 1) * size] = b_ref[pl.ds(at, size), :].astype(f32)

    for name, kind in flat.layout:
        row = flat.at[name][0]
        if name == "qk":
            outs["q"][...] = full[row : row + 512, :256]
            outs["kv"][0] = full[row : row + 512, 256:]
        elif name == "v":
            outs["kv"][1, :256] = full[row : row + 256, :256]
            outs["kv"][1, 256:] = full[row : row + 256, 256:]
        elif kind in ("out", "down"):
            outs[name][...] = full[row : row + outs[name].shape[0]]
        elif kind == "up":
            outs[name][:, :512] = full[row : row + 512]
            outs[name][:, 512:] = full[row + 512 : row + 1024]
        elif kind == "pair":
            outs[name][0] = full[row : row + 512, :256]
            outs[name][1] = full[row : row + 512, 256:]
        else:
            outs[name][:256] = full[row : row + 256, :256]
            outs[name][256:] = full[row : row + 256, 256:]


def finish(flat, ids, a, b):
    names = natural(flat)
    outs = [sds(shape, f32) for _, shape in names]
    res = pl.pallas_call(
        functools.partial(finish_kernel, flat),
        name="grads_out",
        grid=(1,),
        in_specs=[smem, whole(a), whole(b)],
        out_specs=[whole(o) for o in outs],
        out_shape=outs,
        scratch_shapes=[pltpu.VMEM((flat.rows, 512), f32)],
        compiler_params=params(),
        cost_estimate=cost(1e6, 6 * flat.rows * 512),
    )(ids, a, b)
    return {name: r for (name, _), r in zip(names, res)}


place_bits = 4


def swap_dp(a, bit):
    n = lax.axis_size("dp")
    return lax.ppermute(a, "dp", [(i, i ^ bit) for i in range(n)])


def swap_mp(a):
    return lax.ppermute(a, "mp", [(0, 1), (1, 0)])


def after(a, *others):
    return lax.optimization_barrier((a,) + others)[0]


def add_low(*terms):
    return total([t.astype(f32) for t in terms]).astype(bf16)


def reduce_other(pair_b):
    keep, send = pair_b
    return swap_mp(add_low(keep, swap_dp(send, 1)))


def reduce_own(pair_a, came):
    keep, send = pair_a
    cur = add_low(keep, swap_dp(send, 1), came)
    bits = [2, 4, 8]
    for bit in bits:
        n = cur.shape[0] // 2
        cur = add_low(cur[:n], swap_dp(cur[n:], bit))
    bit = 16
    while bit < lax.axis_size("dp"):
        cur = add_low(cur, swap_dp(cur, bit))
        bit *= 2
    for bit in bits[::-1]:
        cur = jnp.concatenate([cur, swap_dp(cur, bit)], axis=0)
    return cur, swap_dp(cur, 1)


def reduce_small(same, own, other):
    n = same.shape[0]
    cur = jnp.concatenate([same, own], axis=0) + swap_mp(jnp.concatenate([same, other], axis=0))
    bit = 1
    while bit < lax.axis_size("dp"):
        cur = cur + swap_dp(cur, bit)
        bit *= 2
    return cur[:n], cur[n:]


def on_device(
    enc_in,
    enc_segments,
    enc_pad,
    enc_buckets,
    dec_in,
    dec_segments,
    dec_buckets,
    enc_cot,
    dec_cot,
    enc_norm1,
    enc_query,
    enc_kv,
    enc_out_proj,
    enc_bias,
    enc_norm2,
    enc_ff_in,
    enc_ff_out,
    enc_final,
    dec_norm1,
    dec_query,
    dec_kv,
    dec_out_proj,
    dec_bias,
    dec_norm2,
    cross_query,
    cross_kv,
    cross_out,
    dec_norm3,
    dec_ff_in,
    dec_ff_out,
):
    rows, length, width = enc_in.shape
    dp = lax.axis_index("dp")
    core, y_at = dp % 2, dp // 2 % 2
    place_at = core * 8 + y_at * 4 + dp // 4 % 2 * 2 + dp // 8 % 2
    ids = jnp.stack([place_at, lax.axis_index("mp") * rows, core, core * 2 + y_at]).astype(jnp.int32)

    flat_qkv = enc_qkv_tabs.pack(
        {"qk": [enc_query, enc_kv[0]], "v": enc_kv[1], "tabs": [enc_bias, dec_bias]}
    )
    flat_mid = enc_mid.pack({"ffo": enc_ff_out, "ffi": enc_ff_in, "ckv": cross_kv, "out": enc_out_proj})
    flat_dec = dec_all.pack(
        {
            "ffo": dec_ff_out,
            "ffi": dec_ff_in,
            "cout": cross_out,
            "cq": cross_query,
            "out": dec_out_proj,
            "qk": [dec_query, dec_kv[0]],
            "v": dec_kv[1],
        }
    )

    def chunk(flat, at, n):
        size = flat.shape[0] // n
        return lax.dynamic_slice_in_dim(flat, at * size, size, 0)

    q0 = swap_mp(chunk(flat_qkv, core, 2))
    q1 = swap_dp(q0, 1)
    m0 = swap_mp(after(chunk(flat_mid, core * 2 + y_at, 4), q0))
    m1 = swap_dp(m0, 2)
    m2, m3 = swap_dp(m0, 1), swap_dp(m1, 1)
    d0 = swap_mp(after(chunk(flat_dec, core * 2 + y_at, 4), m0))
    d1 = swap_dp(after(d0, m1), 2)
    d2, d3 = swap_dp(d0, 1), swap_dp(d1, 1)

    n1g, n2g, nfg = enc_norm1[None, :], enc_norm2[None, :], enc_final[None, :]
    d1g, d2g, d3g = dec_norm1[None, :], dec_norm2[None, :], dec_norm3[None, :]
    rev = jnp.pad(enc_buckets[::-1], (0, 1), constant_values=-1)[None, :]
    places = dec_buckets[None, :]
    x = enc_in.reshape(rows * length, width)
    xc = enc_cot.reshape(rows * length, width)
    z = dec_in.reshape(-1, width)
    zc = dec_cot.reshape(-1, width)

    def flat2(a):
        return a.reshape(rows * length, a.shape[-1])

    qkv_a, o_a, lse_a = enc_fwd(
        ids, enc_in, n1g, enc_segments, enc_pad, rev, [enc_bias, enc_query, enc_kv]
    )
    qkv_b, o_b, lse_b, w_qkv, tabs = enc_fwd(ids, enc_in, n1g, enc_segments, enc_pad, rev, [q0, q1])
    own_mid = [enc_ff_out, enc_ff_in, cross_kv, enc_out_proj]
    x1, y, enc_out, h, slope, kv3, w_mid = mid_fwd(
        ids, x, flat2(o_a), flat2(o_b), n2g, nfg, own_mid, [m0, m1, m2, m3]
    )
    own_dec = [dec_ff_out, dec_ff_in, cross_out, cross_query, dec_out_proj, dec_query, dec_kv]
    dqkv, o2, lse2, z1, q3, w_dec = dec_first(
        ids, z, d1g, d2g, dec_segments, places, dec_bias, tabs, own_dec, [d0, d1, d2, d3]
    )
    dec_out, dec_grad, dkv3, dka, dsa, dkb, dsb, dgd, ddtab = dec_main(
        z, zc, d1g, d2g, d3g, places, dec_segments, enc_segments, enc_pad, ids,
        dqkv, o2, lse2, z1, q3, kv3, dec_bias, tabs, own_dec, w_dec,
    )
    came_dec = reduce_other((dkb, dsb))
    dec_a, dec_b = reduce_own((dka, dsa), came_dec)
    dx1, do, mka, msa, mkb, msb, dg2, dgf = mid_bwd(
        dkv3, y, xc, x1, h, slope, flat2(o_a), flat2(o_b), n2g, nfg, ids, own_mid, w_mid
    )
    came_mid = reduce_other((mkb, msb))
    mid_a, mid_b = reduce_own((mka, msa), came_mid)
    do = do.reshape(rows, length, width)
    dqkv_b, tkb, tsb, dtab_b = enc_bwd(
        1, ids, enc_in, n1g, enc_segments, enc_pad, rev, tabs, qkv_b, o_b, do, lse_b
    )
    came_qkv = reduce_other((tkb, tsb))
    dqkv_a, tka, tsa, dtab_a = enc_bwd(
        0, ids, enc_in, n1g, enc_segments, enc_pad, rev, enc_bias, qkv_a, o_a, do, lse_a
    )
    qkv_c, qkv_d = reduce_own((tka, tsa), came_qkv)
    enc_grad, dg1 = enc_last(x, dx1, flat2(dqkv_a), flat2(dqkv_b), n1g, [enc_query, enc_kv], w_qkv)
    same = jnp.concatenate([dg1, dg2, dgf, dgd], axis=0)
    tab_a = jnp.concatenate([dtab_a[:, 0:4], ddtab[:, 0:4]], axis=1)
    tab_b = jnp.concatenate([dtab_b[:, 0:4], ddtab[:, 4:8]], axis=1)
    same, tab = reduce_small(
        jnp.concatenate([same, jnp.zeros((2, width), f32)], axis=0),
        jnp.pad(tab_a, ((0, 0), (0, width - 8))),
        jnp.pad(tab_b, ((0, 0), (0, width - 8))),
    )
    dec_g = finish(dec_all, ids, dec_a, dec_b)
    mid_g = finish(enc_mid, ids, mid_a, mid_b)
    qkv_g = finish(enc_qkv, ids, qkv_c, qkv_d)
    return (
        enc_out.reshape(enc_in.shape),
        dec_out.reshape(dec_in.shape),
        enc_grad.reshape(enc_in.shape),
        dec_grad.reshape(dec_in.shape),
        same[0],
        qkv_g["q"],
        qkv_g["kv"],
        mid_g["out"],
        tab[:, 0:4],
        same[1],
        mid_g["ffi"],
        mid_g["ffo"],
        same[2],
        same[3],
        dec_g["q"],
        dec_g["kv"],
        dec_g["out"],
        tab[:, 4:8],
        same[4],
        dec_g["cq"],
        mid_g["ckv"],
        dec_g["cout"],
        same[5],
        dec_g["ffi"],
        dec_g["ffo"],
    )


def solution(mesh):
    in_specs = (
        P(("dp", "mp"), None, None),
        P("dp", None),
        P("dp", None),
        P(),
        P(("dp", "mp"), None, None),
        P("dp", None),
        P(),
        P(("dp", "mp"), None, None),
        P(("dp", "mp"), None, None),
        P(),
        P(None, "mp"),
        P(None, None, "mp"),
        P("mp", None),
        P(None, "mp"),
        P(),
        P(None, "mp"),
        P("mp", None),
        P(),
        P(),
        P(None, "mp"),
        P(None, None, "mp"),
        P("mp", None),
        P(None, "mp"),
        P(),
        P(None, "mp"),
        P(None, None, "mp"),
        P("mp", None),
        P(),
        P(None, "mp"),
        P("mp", None),
    )
    out_specs = (
        P(("dp", "mp"), None, None),
        P(("dp", "mp"), None, None),
        P(("dp", "mp"), None, None),
        P(("dp", "mp"), None, None),
        P(),
        P(None, "mp"),
        P(None, None, "mp"),
        P("mp", None),
        P(None, "mp"),
        P(),
        P(None, "mp"),
        P("mp", None),
        P(),
        P(),
        P(None, "mp"),
        P(None, None, "mp"),
        P("mp", None),
        P(None, "mp"),
        P(),
        P(None, "mp"),
        P(None, None, "mp"),
        P("mp", None),
        P(),
        P(None, "mp"),
        P("mp", None),
    )
    return jax.shard_map(
        on_device, mesh=mesh, in_specs=in_specs, out_specs=out_specs, check_vma=False
    )
```

```python
import functools

import jax
import jax.numpy as jnp
from jax import lax
from jax.experimental import pallas as pl
from jax.experimental.pallas import tpu as pltpu
from jax.sharding import PartitionSpec as P

f32 = jnp.float32
bf16 = jnp.bfloat16
neg = -1e30
eps = 1e-06
LANE = 128
MIB = 1 << 20


def nn(a, b):
    return lax.dot_general(a, b, (((1,), (0,)), ((), ())), preferred_element_type=f32)


def nt(a, b):
    return lax.dot_general(a, b, (((1,), (1,)), ((), ())), preferred_element_type=f32)


def tn(a, b):
    return lax.dot_general(a, b, (((0,), (0,)), ((), ())), preferred_element_type=f32)


def total(terms):
    return functools.reduce(lambda a, b: a + b, terms)


def rms_parts(v):
    r = lax.rsqrt(jnp.mean(v * v, axis=-1, keepdims=True) + eps)
    return v * r, r


def rms(v, g):
    return (rms_parts(v)[0] * g).astype(bf16)


def rms_back(v, g, dn):
    vr, r = rms_parts(v)
    dg = jnp.sum(dn * vr, axis=0, keepdims=True)
    t = dn * g
    return r * (t - vr * jnp.mean(t * vr, axis=-1, keepdims=True)), dg


def gelu_both(u):
    c = 0.7978845608028654
    u2 = u * u
    t = jnp.tanh(u * (c + (c * 0.044715) * u2))
    half = 0.5 + 0.5 * t
    slope = half + (0.5 * u) * (1.0 - t * t) * (c + (3 * c * 0.044715) * u2)
    return u * half, slope


def params(vmem_mib=56, **kw):
    return pltpu.CompilerParams(vmem_limit_bytes=vmem_mib * MIB, **kw)


def cost(flops, nbytes):
    return pl.CostEstimate(flops=int(flops * 4), bytes_accessed=int(nbytes * 4), transcendentals=0)


smem = pl.BlockSpec(memory_space=pltpu.SMEM)
anywhere = pl.BlockSpec(memory_space=pltpu.HBM)


def ordered(kernel, ins, after):
    n, k = len(ins), len(after)
    return lambda *refs: kernel(*refs[:n], *refs[n + k :])


unused = pl.BlockSpec(memory_space=pl.ANY)


def whole(a):
    return pl.BlockSpec(a.shape, lambda *_: (0,) * a.ndim, pipeline_mode=pl.Buffered(1))


def sds(shape, dtype):
    return jax.ShapeDtypeStruct(shape, dtype)


class Flat:
    sizes = {"out": 256, "up": 1024, "down": 1024, "pair": 512, "one": 256, "tabs": 32}

    def __init__(self, *layout):
        self.at, row = {}, 0
        for name, kind in layout:
            self.at[name] = row
            row += self.sizes[kind]
        self.rows = row
        self.layout = layout

    def blocks(self, n):
        res, row = [], 0
        for name, kind in self.layout:
            runs = 2 if kind == "up" else 1
            size = self.sizes[kind] // runs
            for run in range(runs):
                res.append((self.at[name] + run * size, size // n, row))
                row += size // n
        return res


enc_first = Flat(("out", "out"), ("qk", "pair"), ("v", "one"), ("tabs", "tabs"))
enc_qkv = Flat(("qk", "pair"), ("v", "one"))
enc_mid = Flat(("ckv", "pair"), ("ffo", "down"), ("ffi", "up"))
dec_early = Flat(("out", "out"), ("cq", "one"), ("qk", "pair"), ("v", "one"))
dec_late = Flat(("ffo", "down"), ("ffi", "up"), ("cout", "out"))
enc_grads = Flat(("ckv", "pair"), ("ffo", "down"), ("ffi", "up"), ("out", "out"))
dec_all = Flat(
    ("ffo", "down"),
    ("ffi", "up"),
    ("cout", "out"),
    ("cq", "one"),
    ("out", "out"),
    ("qk", "pair"),
    ("v", "one"),
)


def chunk_ids(ids_ref, n):
    core, y, z0 = ids_ref[1], ids_ref[2], ids_ref[3]
    if n == 2:
        return [core, 1 - core]
    a = core * 2 + y * (1 - core) + z0 * core
    b = (1 - core) * 2 + z0 * (1 - core) + y * core
    return [a, a ^ 1, b, b ^ 1]


def run_all(copies, sems):
    copies = [pltpu.make_async_copy(a, b, sems.at[i]) for i, (a, b) in enumerate(copies)]
    for c in copies:
        c.start()
    for c in copies:
        c.wait()


def bring(ids_ref, flat, pieces, full, sems):
    n = len(pieces)
    copies = []
    for j, piece in zip(chunk_ids(ids_ref, n), pieces):
        for row, size, at in flat.blocks(n):
            to = pl.multiple_of(row + j * size, 16)
            copies.append((piece.at[at : at + size, :], full.at[pl.ds(to, size), :]))
    run_all(copies, sems)


def bring_sems(flat, n):
    return pltpu.SemaphoreType.DMA((n * len(flat.blocks(n)),))


def chunk_copies(flat, n, j, refs, out):
    copies, row = [], 0

    def add(src, start, rows, lanes=None):
        part = pl.ds(pl.multiple_of(start, 16), rows)
        to = out.at[row : row + rows, :] if lanes is None else out.at[row : row + rows, lanes]
        copies.append((src(part), to))

    left, right = slice(0, 256), slice(256, 512)
    for name, kind in flat.layout:
        ref = refs[name]
        size = flat.sizes[kind] // n
        if kind == "up":
            size //= 2
            add(lambda part: ref.at[part, 0:512], j * size, size)
            row += size
            add(lambda part: ref.at[part, 512:1024], j * size, size)
        elif kind == "pair":
            add(ref[0], j * size, size, left)
            add(ref[1], j * size, size, right)
        elif kind == "one":
            add(ref, j * size, size, left)
            add(ref, 256 + j * size, size, right)
        else:
            add(lambda part: ref.at[part, :], j * size, size)
        row += size
    return copies


def rows_at(ref, *lead):
    return lambda part: ref.at[lead + (part, slice(None))]


def pack_first_kernel(ids_ref, ebias, dbias, eq, ekv, eo, out, tabs, sems):
    tabs[...] = jnp.zeros_like(tabs)
    tabs[0:4, 0:32] = ebias[...]
    tabs[0:4, 256:288] = dbias[...]
    refs = {"qk": (rows_at(eq), rows_at(ekv, 0)), "v": rows_at(ekv, 1), "tabs": tabs, "out": eo}
    run_all(chunk_copies(enc_first, 2, chunk_ids(ids_ref, 2)[0], refs, out), sems)


def pack_rest_kernel(ids_ref, ffo, ffi, ckv, dffo, dffi, cout, cq, do, dq, dkv, sm, se, sl, sems):
    c = chunk_ids(ids_ref, 4)[0]
    mid = {"ckv": (rows_at(ckv, 0), rows_at(ckv, 1)), "ffo": ffo, "ffi": ffi}
    early = {"out": do, "cq": rows_at(cq), "qk": (rows_at(dq), rows_at(dkv, 0)), "v": rows_at(dkv, 1)}
    late = {"ffo": dffo, "ffi": dffi, "cout": cout}
    run_all(
        chunk_copies(enc_mid, 4, c, mid, sm)
        + chunk_copies(dec_early, 4, c, early, se)
        + chunk_copies(dec_late, 4, c, late, sl),
        sems,
    )


def pack_first(ids, ebias, dbias, *weights):
    out = sds((enc_first.rows // 2, 512), bf16)
    return pl.pallas_call(
        pack_first_kernel,
        name="pack_first",
        in_specs=[smem, whole(ebias), whole(dbias)] + [anywhere] * len(weights),
        out_specs=whole(out),
        out_shape=out,
        scratch_shapes=[pltpu.VMEM((32, 512), bf16), pltpu.SemaphoreType.DMA((6,))],
        compiler_params=params(60),
        cost_estimate=cost(1e6, 5e6),
    )(ids, ebias, dbias, *weights)


def pack_rest(ids, *weights):
    outs = [sds((flat.rows // 4, 512), bf16) for flat in (enc_mid, dec_early, dec_late)]
    return pl.pallas_call(
        pack_rest_kernel,
        name="pack_rest",
        in_specs=[smem] + [anywhere] * len(weights),
        out_specs=[whole(a) for a in outs],
        out_shape=outs,
        scratch_shapes=[pltpu.SemaphoreType.DMA((17,))],
        compiler_params=params(60),
        cost_estimate=cost(1e6, 5e6),
    )(ids, *weights)


def one_mul(a, w):
    return nn(a[:, :256], w[:, :256]) + nn(a[:, 256:], w[:, 256:])


def one_back(g, w):
    return jnp.concatenate([nt(g, w[:, :256]), nt(g, w[:, 256:])], axis=1)


def one_grad(a, g):
    full = tn(a, g)
    return jnp.concatenate([full[:256], full[256:]], axis=1)


def bucket_rows(rev_ref):
    rev = pltpu.roll(rev_ref[...], 1024 - 127, 1)
    return lax.broadcasted_iota(jnp.int32, (32, 1024), 0) == rev


def skew_rows(tab, rev_ref, skew_ref):
    w = nn(tab, bucket_rows(rev_ref).astype(bf16))
    for h in range(w.shape[0]):
        base = jnp.broadcast_to(w[h : h + 1], (LANE, 1024))
        skew_ref[h] = pltpu.roll(base, 0, 1, stride=1, stride_axis=0)


def diagonal_sums(a):
    rows, n = a.shape
    while rows > 1:
        rows //= 2
        a = a[:rows] + pltpu.roll(a[rows:], n - rows, 1)
    return a


def bucket_sums(diags, onehot):
    return lax.dot_general(
        diags,
        onehot.astype(f32),
        (((1,), (1,)), ((), ())),
        precision=lax.Precision.HIGHEST,
        preferred_element_type=f32,
    )


def key_codes(seg, pad):
    start = (lax.broadcasted_iota(jnp.int32, seg.shape, 1) == 0) | (seg != pltpu.roll(seg, 1, 1))
    segf = seg.astype(f32)
    return segf, jnp.where((pad == 1) | start, segf, -1.0)


def as_column(row):
    return jnp.transpose(jnp.broadcast_to(row, (LANE, row.shape[1])))


def mask_add(seg, pad, out_ref):
    code, key = key_codes(seg, pad)
    keyc = as_column(key)
    for b in range(seg.shape[1] // LANE):
        out_ref[:, b * LANE : (b + 1) * LANE] = jnp.where(
            keyc == code[:, b * LANE : (b + 1) * LANE], 0.0, neg
        )


def pad_half(a_t, low):
    z = jnp.zeros_like(a_t)
    return jnp.concatenate([a_t, z] if low else [z, a_t], axis=0)


def skew_block(skew_ref, h, q0, width, keys=512):
    return jnp.concatenate(
        [
            skew_ref[h, :, 384 - LANE * b + q0 : 384 - LANE * b + q0 + width]
            for b in range(keys // LANE)
        ],
        axis=0,
    )


QB = 256


def enc_fwd_kernel(own, ids_ref, x_ref, g_ref, seg_ref, pad_ref, rev_ref, *rest):
    step = pl.program_id(0)
    if own:
        tab_ref, wq_ref, wkv_ref, qkv_ref, o_ref, lse_ref, skew, madd, o_t = rest
    else:
        p0, p1, qkv_ref, o_ref, lse_ref, w_ref, tab_ref, skew, madd, o_t, sems = rest

        @pl.when(step == 0)
        def _():
            bring(ids_ref, enc_first, (p0, p1), w_ref, sems)
            tab_ref[...] = w_ref[1024:1056, :]

    @pl.when(step == 0)
    def _():
        skew_rows(tab_ref[0:4, 0:32], rev_ref, skew)

    row = pl.ds(ids_ref[0] + step, 1)
    mask_add(seg_ref[row, :], pad_ref[row, :], madd)
    n1 = rms(x_ref[0].astype(f32), g_ref[...])
    if own:
        q = nn(n1, wq_ref[...]).astype(bf16)
        k = nn(n1, wkv_ref[0]).astype(bf16)
        v = nn(n1, wkv_ref[1]).astype(bf16)
    else:
        qk = nn(n1, w_ref[256:768, :]).astype(bf16)
        q, k = qk[:, :256], qk[:, 256:]
        v = one_mul(n1, w_ref[768:1024, :]).astype(bf16)
    qkv_ref[0, :, 0:256] = q
    qkv_ref[0, :, 256:512] = k
    qkv_ref[0, :, 512:768] = v
    q_t, v_t = jnp.transpose(q), jnp.transpose(v)
    for h in range(4):
        pair = slice(LANE * (h // 2), LANE * (h // 2) + LANE)
        rows = slice(64 * h, 64 * h + 64)
        k2 = k[:, pair]
        qz = pad_half(q_t[rows], h % 2 == 0)
        for b in range(0, 512, QB):
            s = nn(k2, qz[:, b : b + QB]) + skew_block(skew, h, b, QB) + madd[:, b : b + QB]
            m = jnp.max(s, axis=0, keepdims=True)
            e = jnp.exp(s - m)
            norm = jnp.sum(e, axis=0, keepdims=True)
            o_t[rows, b : b + QB] = nn(v_t[rows], e.astype(bf16)) * (1.0 / norm)
            lse_ref[0, h : h + 1, b : b + QB] = m + jnp.log(norm)
    o_ref[0] = jnp.transpose(o_t[...]).astype(bf16)


def row_block(width, n=512, at=0):
    return pl.BlockSpec((1, n, width), lambda r: (r, 0, at))


def enc_fwd(ids, x, g, seg, pad, rev, ws):
    rows = x.shape[0]
    own = len(ws) == 3
    more = [] if own else [sds((enc_first.rows, 512), bf16), sds((32, 512), bf16)]
    return pl.pallas_call(
        functools.partial(enc_fwd_kernel, own),
        name="enc_attend_own" if own else "enc_attend_other",
        grid=(rows,),
        in_specs=[smem, row_block(512), whole(g), whole(seg), whole(pad), whole(rev)]
        + [whole(w) if own else anywhere for w in ws],
        out_specs=[row_block(768), row_block(256), row_block(512, 4)] + [whole(a) for a in more],
        out_shape=[
            sds((rows, 512, 768), bf16),
            sds((rows, 512, 256), bf16),
            sds((rows, 4, 512), f32),
        ]
        + more,
        scratch_shapes=[
            pltpu.VMEM((4, LANE, 1024), f32),
            pltpu.VMEM((512, 512), f32),
            pltpu.VMEM((256, 512), f32),
        ]
        + ([] if own else [bring_sems(enc_first, 2)]),
        compiler_params=params(),
        cost_estimate=cost(8e9, 4e6),
    )(ids, x, g, seg, pad, rev, *ws)


def enc_bwd_kernel(
    rows_n,
    ids_ref,
    x_ref,
    g_ref,
    seg_ref,
    pad_ref,
    rev_ref,
    tab_ref,
    qkv_ref,
    o_ref,
    do_ref,
    lse_ref,
    *rest,
):
    if len(rest) == 12:
        other_ref, (dqkv_ref, *grads, dtab_ref) = None, rest[:3]
        skew, dskew, madd, p_s, ds_s, dq_t, dv_acc, dk_acc, acc = rest[3:]
    else:
        other_ref, (dqkv_ref, *grads, dtab_ref) = rest[0], rest[1:5]
        skew, dskew, madd, p_s, ds_s, dq_t, dv_acc, dk_acc, acc, rounded, sems = rest[5:]
    step = pl.program_id(0)

    @pl.when(step == 0)
    def _():
        skew_rows(tab_ref[0:4, 0:32], rev_ref, skew)
        dskew[...] = jnp.zeros_like(dskew)

    row = pl.ds(ids_ref[0] + step, 1)
    mask_add(seg_ref[row, :], pad_ref[row, :], madd)
    q, k, v = qkv_ref[0, :, 0:256], qkv_ref[0, :, 256:512], qkv_ref[0, :, 512:768]
    do = do_ref[0]
    q_t, k_t, do_t = jnp.transpose(q), jnp.transpose(k), jnp.transpose(do)
    o_t = jnp.transpose(o_ref[0])
    lane = lax.broadcasted_iota(jnp.int32, (512, LANE), 1)
    for h in range(4):
        pair = slice(LANE * (h // 2), LANE * (h // 2) + LANE)
        rows = slice(64 * h, 64 * h + 64)
        low = h % 2 == 0
        k2, v2 = k[:, pair], v[:, pair]
        qz, doz = pad_half(q_t[rows], low), pad_half(do_t[rows], low)
        inner = jnp.sum(
            do_t[rows].astype(f32) * o_t[rows].astype(f32), axis=0, keepdims=True
        )
        for b in range(0, 512, QB):
            cols = slice(b, b + QB)
            s = nn(k2, qz[:, cols]) + skew_block(skew, h, b, QB) + madd[:, cols]
            p = jnp.exp(s - lse_ref[0, h : h + 1, cols])
            ds = p * (nn(v2, doz[:, cols]) - inner[:, cols])
            p_s[:, cols] = p.astype(bf16)
            ds_s[:, cols] = ds.astype(bf16)
            for kb in range(4):
                at = 384 - LANE * kb + b
                dskew[h, :, at : at + QB] += ds[LANE * kb : LANE * kb + LANE]
        mine = (lane < 64) if low else (lane >= 64)
        dv2 = nn(p_s[...], jnp.where(mine, do[:, pair], jnp.zeros((), bf16)))
        dk2 = nn(ds_s[...], jnp.where(mine, q[:, pair], jnp.zeros((), bf16)))
        if low:
            dv_acc[:, pair] = dv2
            dk_acc[:, pair] = dk2
        else:
            dv_acc[:, pair] += dv2
            dk_acc[:, pair] += dk2
        dq_t[rows] = nn(k_t[rows], ds_s[...])
    dqkv_ref[0, :, 0:256] = jnp.transpose(dq_t[...]).astype(bf16)
    dqkv_ref[0, :, 256:512] = dk_acc[...].astype(bf16)
    dqkv_ref[0, :, 512:768] = dv_acc[...].astype(bf16)
    n1_t = jnp.transpose(rms(x_ref[0].astype(f32), g_ref[...]))
    dqk = nn(n1_t, dqkv_ref[0, :, 0:512])
    dv = nn(n1_t, dqkv_ref[0, :, 512:768])
    dv = jnp.concatenate([dv[:256], dv[256:]], axis=1)

    @pl.when(step == 0)
    def _():
        acc[0:512] = dqk
        acc[512:768] = dv

    @pl.when(step > 0)
    def _():
        acc[0:512] += dqk
        acc[512:768] += dv

    @pl.when(step == rows_n - 1)
    def _():
        if other_ref is None:
            grads[0][...] = acc[...].astype(bf16)
        else:
            rounded[...] = acc[...].astype(bf16)
            move = Place(ids_ref, (rounded, other_ref), *grads, sems)
            move.start()
        diags = jnp.concatenate([diagonal_sums(dskew[h]) for h in range(4)], axis=0)
        dtab_ref[0:4, 0:32] = bucket_sums(diags, bucket_rows(rev_ref))
        if other_ref is not None:
            move.wait()


def place_of(ids_ref, j, m):
    yb = (j // 4 % 2) ^ ids_ref[2]
    b0 = (j // 2 % 2) ^ ids_ref[3]
    b1 = j % 2
    return m * 8 + yb * 4 + b0 * 2 + b1 if j < 8 else b0 * 8 + m * 4 + yb * 2 + b1


class Place:
    def __init__(self, ids_ref, accs, keep_ref, send_ref, sems):
        self.ids_ref, self.accs, self.outs, self.sems = ids_ref, accs, (keep_ref, send_ref), sems
        self.copies = []

    def start(self, first=0, last=16):
        size = self.accs[0].shape[0] // 16
        for j in range(first, last):
            for m in range(2):
                at = pl.multiple_of(place_of(self.ids_ref, j, m) * size, 16)
                src = self.accs[m].at[j * size : (j + 1) * size, :]
                keep, send = [
                    pltpu.make_async_copy(src, out.at[pl.ds(at, size), :], self.sems.at[2 * j + m])
                    for out in self.outs
                ]
                pl.when(self.ids_ref[1] == j // 8)(keep.start)
                pl.when(self.ids_ref[1] != j // 8)(send.start)
                self.copies.append(keep)

    def wait(self):
        for c in self.copies:
            c.wait()


place_sems = pltpu.SemaphoreType.DMA((32,))


def enc_bwd(half_at, ids, x, g, seg, pad, rev, tab, qkv, o, do, lse, other=None, after=()):
    rows = x.shape[0]
    n = enc_qkv.rows
    ins = [ids, x, g, seg, pad, rev, tab, qkv, o, do, lse] + ([] if other is None else [other])
    grads = [sds((n, 512), bf16)] * (1 if other is None else 2)
    return pl.pallas_call(
        ordered(functools.partial(enc_bwd_kernel, rows), ins, after),
        name="enc_attend_other_back" if half_at else "enc_attend_own_back",
        grid=(rows,),
        in_specs=[
            smem,
            row_block(512),
            whole(g),
            whole(seg),
            whole(pad),
            whole(rev),
            whole(tab),
            row_block(768),
            row_block(256),
            row_block(256, at=half_at),
            row_block(512, 4),
        ]
        + [whole(a) for a in ins[11:]]
        + [unused] * len(after),
        out_specs=[row_block(768)]
        + [whole(a) if other is None else anywhere for a in grads]
        + [pl.BlockSpec((8, LANE), lambda r: (0, 0))],
        out_shape=[sds((rows, 512, 768), bf16)] + grads + [sds((8, LANE), f32)],
        scratch_shapes=[
            pltpu.VMEM((4, LANE, 1024), f32),
            pltpu.VMEM((4, LANE, 1024), f32),
            pltpu.VMEM((512, 512), f32),
            pltpu.VMEM((512, 512), bf16),
            pltpu.VMEM((512, 512), bf16),
            pltpu.VMEM((256, 512), f32),
            pltpu.VMEM((512, 256), f32),
            pltpu.VMEM((512, 256), f32),
            pltpu.VMEM((n, 512), f32),
        ]
        + ([] if other is None else [pltpu.VMEM((n, 512), bf16), place_sems]),
        compiler_params=params(),
        cost_estimate=cost(16e9, 8e6),
    )(*ins, *after)


class Mid:
    def __init__(self, ffo=None, ffi=None, ckv=None, flat=None):
        if flat is not None:
            at = enc_mid.at
            self.ffo = lambda c: flat[at["ffo"] + 512 * c : at["ffo"] + 512 * c + 512, :]
            self.ffi = lambda c: flat[at["ffi"] + 512 * c : at["ffi"] + 512 * c + 512, :]
            self.ckv = lambda c: flat[at["ckv"] : at["ckv"] + 512, 256 * c : 256 * c + 256]
        else:
            self.ffo = lambda c: ffo[512 * c : 512 * c + 512, :]
            self.ffi = lambda c: ffi[:, 512 * c : 512 * c + 512]
            self.ckv = lambda c: ckv[c]


def tile_block(tile, width, at=0):
    return pl.BlockSpec((tile, width), lambda t: (t, at))


def rows_of(a, first, n):
    return pl.BlockSpec((n, a.shape[1]), lambda *_: (first // n, 0), pipeline_mode=pl.Buffered(1))


def feed_forward(m1, w, h_ref, slope_ref):
    terms = []
    for c in range(2):
        h, slope = gelu_both(nn(m1, w.ffi(c)))
        h = h.astype(bf16)
        cols = slice(512 * c, 512 * c + 512)
        h_ref[:, cols] = h
        slope_ref[:, cols] = slope.astype(bf16)
        terms.append(nn(h, w.ffo(c)))
    return total(terms)


def mid_own_kernel(x_ref, oa_ref, ob_ref, g2_ref, outa_ref, outb_ref, ffo_ref, ffi_ref, x1_ref, part_ref, h_ref, slope_ref):
    x1 = x_ref[...].astype(f32) + total([nn(oa_ref[...], outa_ref[...]), nn(ob_ref[...], outb_ref[...])])
    x1_ref[...] = x1
    m1 = rms(x1, g2_ref[...])
    part_ref[...] = x1 + feed_forward(m1, Mid(ffo_ref, ffi_ref), h_ref, slope_ref)


def mid_own(x, oa, ob, g2, out_a, w_first, ffo, ffi, tile=256):
    n = x.shape[0]
    return pl.pallas_call(
        mid_own_kernel,
        name="enc_middle_own",
        grid=(n // tile,),
        in_specs=[
            tile_block(tile, 512),
            tile_block(tile, 256),
            tile_block(tile, 256),
            whole(g2),
            whole(out_a),
            pl.BlockSpec((256, 512), lambda t: (0, 0), pipeline_mode=pl.Buffered(1)),
            whole(ffo),
            whole(ffi),
        ],
        out_specs=[tile_block(tile, 512), tile_block(tile, 512), tile_block(tile, 1024), tile_block(tile, 1024)],
        out_shape=[sds((n, 512), f32), sds((n, 512), f32), sds((n, 1024), bf16), sds((n, 1024), bf16)],
        compiler_params=params(),
        cost_estimate=cost(6e9, 1.2e7),
    )(x, oa, ob, g2, out_a, w_first, ffo, ffi)


def mid_other_kernel(ids_ref, x1_ref, part_ref, g2_ref, gf_ref, ckv_ref, p0, p1, p2, p3, y_ref, out_ref, mem_ref, h_ref, slope_ref, kv_ref, w_ref, sems):
    @pl.when(pl.program_id(0) == 0)
    def _():
        bring(ids_ref, enc_mid, (p0, p1, p2, p3), w_ref, sems)

    w = Mid(flat=w_ref)
    m1 = rms(x1_ref[...], g2_ref[...])
    y = part_ref[...] + feed_forward(m1, w, h_ref, slope_ref)
    y_ref[...] = y
    out_ref[...] = y.astype(bf16)
    mem = rms(y, gf_ref[...])
    mem_ref[...] = mem
    for c in range(2):
        for i, half in enumerate((Mid(ckv=ckv_ref), w)):
            at = 512 * c + 256 * i
            kv_ref[:, at : at + 256] = nn(mem, half.ckv(c)).astype(bf16)


def mid_other(ids, x1, part, g2, gf, ckv, pieces, tile=256):
    n = x1.shape[0]
    return pl.pallas_call(
        mid_other_kernel,
        name="enc_middle_other",
        grid=(n // tile,),
        in_specs=[smem, tile_block(tile, 512), tile_block(tile, 512), whole(g2), whole(gf), whole(ckv)]
        + [anywhere] * len(pieces),
        out_specs=[
            tile_block(tile, 512),
            tile_block(tile, 512),
            tile_block(tile, 512),
            tile_block(tile, 1024),
            tile_block(tile, 1024),
            tile_block(tile, 1024),
            whole(sds((enc_mid.rows, 512), bf16)),
        ],
        out_shape=[
            sds((n, 512), f32),
            sds((n, 512), bf16),
            sds((n, 512), bf16),
            sds((n, 1024), bf16),
            sds((n, 1024), bf16),
            sds((n, 1024), bf16),
            sds((enc_mid.rows, 512), bf16),
        ],
        scratch_shapes=[bring_sems(enc_mid, len(pieces))],
        compiler_params=params(),
        cost_estimate=cost(7e9, 1.5e7),
    )(ids, x1, part, g2, gf, ckv, *pieces)


def out_grad_kernel(dkv_ref, y_ref, cot_ref, gf_ref, ckva_ref, ckvb_ref, dy_ref, dgf_ref):
    step = pl.program_id(0)
    terms = []
    for c in range(2):
        for i in range(2):
            d = dkv_ref[:, 512 * c + 256 * i : 512 * c + 256 * i + 256]
            terms.append(nt(d, ckvb_ref[:, 256 * c : 256 * c + 256] if i else ckva_ref[c]))
    part, dgf = rms_back(y_ref[...], gf_ref[...], total(terms))
    dy_ref[...] = cot_ref[...].astype(f32) + part

    @pl.when(step == 0)
    def _():
        dgf_ref[...] = dgf

    @pl.when(step > 0)
    def _():
        dgf_ref[...] += dgf


def out_grad(dkv, y, cot, gf, ckv, w_mid, after=(), tile=256):
    n = y.shape[0]
    ins = [dkv, y, cot, gf, ckv, w_mid]
    return pl.pallas_call(
        ordered(out_grad_kernel, ins, after),
        name="enc_output_back",
        grid=(n // tile,),
        in_specs=[
            tile_block(tile, 1024),
            tile_block(tile, 512),
            tile_block(tile, 512),
            whole(gf),
            whole(ckv),
            rows_of(w_mid, enc_mid.at["ckv"], 512),
        ]
        + [unused] * len(after),
        out_specs=[tile_block(tile, 512), pl.BlockSpec((1, 512), lambda t: (0, 0))],
        out_shape=[sds((n, 512), f32), sds((1, 512), f32)],
        compiler_params=params(),
        cost_estimate=cost(2e9, 8e6),
    )(*ins, *after)


def mid_bwd_kernel(
    ids_ref, dy_ref, dkv_ref, mem_ref, x1_ref, oa_ref, ob_ref, g2_ref, outa_ref, outb_ref,
    ha_ref, hb_ref, sa_ref, sb_ref, ffoa_ref, ffob_ref, ffia_ref, ffib_ref,
    dx1_ref, do_ref, keep_ref, send_ref, dg2_ref, g_s, m1_s, dm1, acc_a, acc_b, sems,
):
    accs = (acc_a, acc_b)
    step = pl.program_id(0)
    at = enc_grads.at

    @pl.when(step == 0)
    def _():
        g_s[...] = dy_ref[...].astype(bf16)
        m1_s[...] = rms(x1_ref[...], g2_ref[...])

    out_row = pl.ds(pl.multiple_of(at["ffo"] + 256 * step, 256), 256)
    in_row = pl.ds(pl.multiple_of(at["ffi"] + 512 * (step // 2), 512), 512)
    in_lane = pl.ds(pl.multiple_of(256 * (step % 2), 256), 256)
    terms = []
    for acc, h_ref, slope_ref, ffo_ref, ffi_ref in (
        (acc_a, ha_ref, sa_ref, ffoa_ref, ffia_ref),
        (acc_b, hb_ref, sb_ref, ffob_ref, ffib_ref),
    ):
        g = g_s[...]
        du = (nt(g, ffo_ref[...]) * slope_ref[...].astype(f32)).astype(bf16)
        acc[out_row, :] = tn(h_ref[...], g).astype(bf16)
        acc[in_row, in_lane] = tn(m1_s[...], du).astype(bf16)
        terms.append(nt(du, ffi_ref[...]))

    @pl.when(step == 0)
    def _():
        dm1[...] = total(terms)

    @pl.when(step > 0)
    def _():
        dm1[...] += total(terms)

    @pl.when(step == 3)
    def _():
        part, dg2_ref[...] = rms_back(x1_ref[...], g2_ref[...], dm1[...])
        dx1 = dy_ref[...] + part
        dx1_ref[...] = dx1
        g_s[...] = dx1.astype(bf16)
        for i, (o_ref, out_ref) in enumerate(((oa_ref, outa_ref), (ob_ref, outb_ref))):
            do_ref[:, 256 * i : 256 * i + 256] = nt(g_s[...], out_ref[...]).astype(bf16)
            accs[i][at["out"] : at["out"] + 256, :] = tn(o_ref[...], g_s[...]).astype(bf16)
            for c in range(2):
                d = dkv_ref[:, 512 * c + 256 * i : 512 * c + 256 * i + 256]
                rows = slice(at["ckv"], at["ckv"] + 512)
                accs[i][rows, 256 * c : 256 * c + 256] = tn(mem_ref[...], d).astype(bf16)
        move = Place(ids_ref, accs, keep_ref, send_ref, sems)
        move.start()
        move.wait()


def mid_bwd(ids, dy, dkv, mem, x1, ha, hb, sa, sb, oa, ob, g2, out_a, w_first, ffo, ffi, w_mid, after=()):
    n = dy.shape[0]
    grads = sds((enc_grads.rows, 512), bf16)
    hidden = pl.BlockSpec((n, 256), lambda t: (0, t))
    down, up = enc_mid.at["ffo"] // 256, enc_mid.at["ffi"] // 512
    outs = [sds((n, 512), f32), sds((n, 512), bf16), grads, grads, sds((1, 512), f32)]
    ins = [ids, dy, dkv, mem, x1, oa, ob, g2, out_a, w_first, ha, hb, sa, sb, ffo, w_mid, ffi, w_mid]
    return pl.pallas_call(
        ordered(mid_bwd_kernel, ins, after),
        name="enc_middle_back",
        grid=(4,),
        in_specs=[smem]
        + [whole(a) for a in (dy, dkv, mem, x1, oa, ob, g2, out_a)]
        + [
            pl.BlockSpec((256, 512), lambda t: (0, 0), pipeline_mode=pl.Buffered(1)),
            hidden,
            hidden,
            hidden,
            hidden,
            pl.BlockSpec((256, 512), lambda t: (t, 0)),
            pl.BlockSpec((256, 512), lambda t: (down + t, 0)),
            pl.BlockSpec((512, 256), lambda t: (0, t)),
            pl.BlockSpec((512, 256), lambda t: (up + t // 2, t % 2)),
        ]
        + [unused] * len(after),
        out_specs=[anywhere if a is grads else whole(a) for a in outs],
        out_shape=outs,
        scratch_shapes=[
            pltpu.VMEM((n, 512), bf16),
            pltpu.VMEM((n, 512), bf16),
            pltpu.VMEM((n, 512), f32),
            pltpu.VMEM((enc_grads.rows, 512), bf16),
            pltpu.VMEM((enc_grads.rows, 512), bf16),
            place_sems,
        ],
        compiler_params=params(56),
        cost_estimate=cost(20e9, 3e7),
    )(*ins, *after)


def enc_last_kernel(
    x_ref, dx1_ref, da_ref, db_ref, g_ref, wq_ref, wkv_ref, w_ref, dg2_ref, dgf_ref, dgd_ref, taba_ref, tabb_ref,
    tabd_ref, ids_ref, out_ref, small_ref,
):
    step = pl.program_id(0)
    da, db = da_ref[...], db_ref[...]
    dn = total(
        [
            nt(da[:, 0:256], wq_ref[...]),
            nt(da[:, 256:512], wkv_ref[0]),
            nt(da[:, 512:768], wkv_ref[1]),
            nt(db[:, 0:512], w_ref[256:768, :]),
            one_back(db[:, 512:768], w_ref[768:1024, :]),
        ]
    )
    part, dg = rms_back(x_ref[...].astype(f32), g_ref[...], dn)
    out_ref[...] = dx1_ref[...] + part

    @pl.when(step == 0)
    def _():
        zero = jnp.zeros((2, 512), f32)
        small_ref[0:8] = jnp.concatenate([dg, dg2_ref[...], dgf_ref[...], dgd_ref[...], zero], axis=0)
        small_ref[8:16] = jnp.zeros((8, 512), f32)
        for at, (enc, first) in enumerate(((taba_ref, 0), (tabb_ref, 4))):
            dec = tabd_ref[first : first + 4, :]
            rows = jnp.concatenate([enc[0:4, :], dec], axis=1)

            @pl.when(ids_ref[5] == at)
            def _():
                small_ref[8:12, 0 : 2 * LANE] = rows

            @pl.when(ids_ref[5] != at)
            def _():
                small_ref[12:16, 0 : 2 * LANE] = rows

    @pl.when(step > 0)
    def _():
        small_ref[0:1] += dg


def enc_last(ids, x, dx1, da, db, g, wq, wkv, w_first, smalls, after=(), tile=256):
    n = x.shape[0]
    small = sds((16, 512), f32)
    ins = [x, dx1, da, db, g, wq, wkv, w_first, *smalls, ids]
    return pl.pallas_call(
        ordered(enc_last_kernel, ins, after),
        name="enc_input_back",
        grid=(n // tile,),
        in_specs=[
            tile_block(tile, 512),
            tile_block(tile, 512),
            tile_block(tile, 768),
            tile_block(tile, 768),
            whole(g),
            whole(wq),
            whole(wkv),
            whole(w_first),
        ]
        + [whole(a) for a in smalls]
        + [smem]
        + [unused] * len(after),
        out_specs=[tile_block(tile, 512), whole(small)],
        out_shape=[sds((n, 512), f32), small],
        compiler_params=params(),
        cost_estimate=cost(4e9, 1e7),
    )(*ins, *after)


class Dec:
    def __init__(self, natural=None, early=None, late=None):
        if natural is not None:
            ffo, ffi, cout, cq, out, q, kv = natural
            self.ffo = lambda c: ffo[512 * c : 512 * c + 512, :]
            self.ffi = lambda c: ffi[:, 512 * c : 512 * c + 512]
            self.cout = lambda: cout[...]
            self.cq = lambda c: cq[256 * c : 256 * c + 256, :]
            self.out = lambda: out[...]
            self.qk = lambda c: q[...] if c == 0 else kv[0]
            self.v = lambda c: kv[1, 256 * c : 256 * c + 256, :]
        else:
            at = {**dec_early.at, **dec_late.at}
            self.ffo = lambda c: late[at["ffo"] + 512 * c : at["ffo"] + 512 * c + 512, :]
            self.ffi = lambda c: late[at["ffi"] + 512 * c : at["ffi"] + 512 * c + 512, :]
            self.cout = lambda: late[at["cout"] : at["cout"] + 256, :]
            self.cq = lambda c: early[at["cq"] : at["cq"] + 256, 256 * c : 256 * c + 256]
            self.out = lambda: early[at["out"] : at["out"] + 256, :]
            self.qk = lambda c: early[at["qk"] : at["qk"] + 512, 256 * c : 256 * c + 256]
            self.v = lambda c: early[at["v"] : at["v"] + 256, 256 * c : 256 * c + 256]


def two_mul(a, w):
    return nn(a[:, :256], w(0)) + nn(a[:, 256:], w(1))


def two_back(g, w):
    return jnp.concatenate([nt(g, w(0)), nt(g, w(1))], axis=1)


def spread_t(a_t, width):
    tiled = jnp.concatenate([a_t] * 4, axis=1)
    head = lax.broadcasted_iota(jnp.int32, tiled.shape, 0) // 64
    block = lax.broadcasted_iota(jnp.int32, tiled.shape, 1) // width
    return jnp.where(head == block, tiled, jnp.zeros((), a_t.dtype))


def spread(a, height):
    tiled = jnp.concatenate([a] * 4, axis=0)
    block = lax.broadcasted_iota(jnp.int32, tiled.shape, 0) // height
    head = lax.broadcasted_iota(jnp.int32, tiled.shape, 1) // 64
    return jnp.where(head == block, tiled, jnp.zeros((), a.dtype))


def fold(full, height):
    head = lax.broadcasted_iota(jnp.int32, (height, 256), 1) // 64
    total = jnp.zeros((height, 256), f32)
    for h in range(4):
        total = total + jnp.where(head == h, full[height * h : height * h + height], 0.0)
    return total


def dec_bucket_rows(buckets_ref):
    b = buckets_ref[...]
    b = jnp.concatenate([b, jnp.full((1, LANE - b.shape[1]), -1, jnp.int32)], axis=1)
    return lax.broadcasted_iota(jnp.int32, (32, LANE), 0) == b


def dec_bias_rows(tab, buckets_ref):
    w = nn(tab, dec_bucket_rows(buckets_ref).astype(bf16))
    return jnp.concatenate(
        [
            pltpu.roll(jnp.broadcast_to(w[h : h + 1], (LANE, LANE)), 0, 1, stride=1, stride_axis=0)
            for h in range(4)
        ],
        axis=1,
    )


def dec_self_mask(ids_ref, dseg_ref, rows):
    code = jnp.concatenate(
        [(dseg_ref[pl.ds(ids_ref[0] + r, 1), :] + 8 * r).astype(f32) for r in range(rows)], axis=1
    )
    key = as_column(code)
    j = lax.broadcasted_iota(jnp.int32, (LANE, LANE), 0)
    i = lax.broadcasted_iota(jnp.int32, (LANE, LANE), 1)
    one = jnp.where((key == code) & (j <= i), 0.0, neg)
    return jnp.concatenate([one] * 4, axis=1)


def dec_first_kernel(ids_ref, x_ref, g1_ref, g2_ref, dseg_ref, buckets_ref, taba_ref, tabb_ref, *rest):
    pieces = rest[7:11]
    qkv_ref, o_ref, lse_ref, z1_ref, q3_ref, w_ref, sems = rest[11:]
    halves = (Dec(rest[:7]), Dec(early=w_ref))
    bring(ids_ref, dec_early, pieces, w_ref, sems)
    z = x_ref[...].astype(f32)
    n2 = rms(z, g1_ref[...])
    mask = dec_self_mask(ids_ref, dseg_ref, x_ref.shape[0] // 64)
    terms = []
    for i, (w, tab) in enumerate(zip(halves, (taba_ref[...], tabb_ref[0:4, 256:288]))):
        q = nn(n2, w.qk(0)).astype(bf16)
        k = nn(n2, w.qk(1)).astype(bf16)
        v = two_mul(n2, w.v).astype(bf16)
        for c, a in enumerate((q, k, v)):
            qkv_ref[:, 512 * c + 256 * i : 512 * c + 256 * i + 256] = a
        s = nn(k, spread_t(jnp.transpose(q), LANE)) + dec_bias_rows(tab, buckets_ref) + mask
        m = jnp.max(s, axis=0, keepdims=True)
        e = jnp.exp(s - m)
        norm = jnp.sum(e, axis=0, keepdims=True)
        p = (e * (1.0 / norm)).astype(bf16)
        lse_ref[i : i + 1, :] = m + jnp.log(norm)
        o = fold(tn(p, v), LANE).astype(bf16)
        o_ref[:, 256 * i : 256 * i + 256] = o
        terms.append(nn(o, w.out()))
    z1 = z + total(terms)
    z1_ref[...] = z1
    n3 = rms(z1, g2_ref[...])
    for i, w in enumerate(halves):
        q3_ref[:, 256 * i : 256 * i + 256] = two_mul(n3, w.cq).astype(bf16)


def dec_first(ids, x, g1, g2, dseg, buckets, taba, tabb, own, pieces):
    n = x.shape[0]
    ins = [x, g1, g2, dseg, buckets, taba, tabb, *own]
    return pl.pallas_call(
        dec_first_kernel,
        name="dec_self",
        grid=(1,),
        in_specs=[smem] + [whole(a) for a in ins] + [anywhere] * len(pieces),
        out_specs=[
            pl.BlockSpec(s, lambda t: (0, 0))
            for s in ((n, 1536), (n, 512), (2, 512), (n, 512), (n, 512), (dec_early.rows, 512))
        ],
        out_shape=[
            sds((n, 1536), bf16),
            sds((n, 512), bf16),
            sds((2, 512), f32),
            sds((n, 512), f32),
            sds((n, 512), bf16),
            sds((dec_early.rows, 512), bf16),
        ],
        scratch_shapes=[bring_sems(dec_early, len(pieces))],
        compiler_params=params(),
        cost_estimate=cost(1e9, 8e6),
    )(ids, *ins, *pieces)


def dec_main_kernel(
    x_ref,
    cot_ref,
    g1_ref,
    g2_ref,
    g3_ref,
    buckets_ref,
    dseg_ref,
    seg_ref,
    pad_ref,
    ids_ref,
    qkv_ref,
    o2_ref,
    lse_ref,
    z1_ref,
    q3_ref,
    kv_ref,
    taba_ref,
    tabb_ref,
    *rest,
):
    early, pieces = rest[7], rest[8:12]
    out_ref, dx_ref, dkv_ref, keep_ref, send_ref, dg_ref, dtab_ref = rest[12:19]
    madd, p_s, acc_a, acc_b, late, sems, move_sems = rest[19:]
    halves = (Dec(rest[:7]), Dec(early=early, late=late))
    bring(ids_ref, dec_late, pieces, late, sems)
    accs = (acc_a, acc_b)
    at = dec_all.at
    rows_n = x_ref.shape[0] // 64
    z1 = z1_ref[...]
    mixed = [[None] * rows_n, [None] * rows_n]
    for r in range(rows_n):
        row = pl.ds(ids_ref[0] + r, 1)
        keyc = as_column(key_codes(seg_ref[row, :], pad_ref[row, :])[1])
        code = dseg_ref[row, :].astype(f32)
        madd[...] = jnp.where(keyc == jnp.concatenate([code, code], axis=1), 0.0, neg)
        both = jnp.concatenate([madd[...]] * 2, axis=1)
        for i in range(2):
            cols = slice(256 * i, 256 * i + 256)
            k3 = kv_ref[512 * r : 512 * r + 512, 256 * i : 256 * i + 256]
            v3 = kv_ref[512 * r : 512 * r + 512, 512 + 256 * i : 512 + 256 * i + 256]
            q_t = jnp.transpose(q3_ref[64 * r : 64 * r + 64, cols])
            s = nn(k3, spread_t(q_t, 64)) + both
            m = jnp.max(s, axis=0, keepdims=True)
            e = jnp.exp(s - m)
            p = e * (1.0 / jnp.sum(e, axis=0, keepdims=True))
            p_s[2 * r + i] = p
            mixed[i][r] = fold(tn(p.astype(bf16), v3), 64).astype(bf16)
    o3 = [jnp.concatenate(m, axis=0) for m in mixed]
    z2 = z1 + total([nn(o, w.cout()) for o, w in zip(o3, halves)])
    n4 = rms(z2, g3_ref[...])
    terms, kept = [], []
    for i, w in enumerate(halves):
        for c in range(2):
            h, slope = gelu_both(nn(n4, w.ffi(c)))
            h = h.astype(bf16)
            kept.append((h, slope))
            terms.append(nn(h, w.ffo(c)))
    out_ref[...] = (z2 + total(terms)).astype(bf16)
    g = cot_ref[...]
    terms = []
    for i, w in enumerate(halves):
        for c in range(2):
            h, slope = kept[2 * i + c]
            accs[i][at["ffo"] + 512 * c : at["ffo"] + 512 * c + 512] = tn(h, g).astype(bf16)
            du = (nt(g, w.ffo(c)) * slope).astype(bf16)
            accs[i][at["ffi"] + 512 * c : at["ffi"] + 512 * c + 512] = tn(n4, du).astype(bf16)
            terms.append(nt(du, w.ffi(c)))
    part, dg3 = rms_back(z2, g3_ref[...], total(terms))
    dz2 = g.astype(f32) + part
    move = Place(ids_ref, accs, keep_ref, send_ref, move_sems)
    done = 2048 // (dec_all.rows // 16)
    move.start(0, done)
    g = dz2.astype(bf16)
    n3 = rms(z1, g2_ref[...])
    terms = []
    for i, w in enumerate(halves):
        cols = slice(256 * i, 256 * i + 256)
        accs[i][at["cout"] : at["cout"] + 256] = tn(o3[i], g).astype(bf16)
        do = nt(g, w.cout()).astype(bf16)
        dq = []
        for r in range(rows_n):
            k3 = kv_ref[512 * r : 512 * r + 512, 256 * i : 256 * i + 256]
            v3 = kv_ref[512 * r : 512 * r + 512, 512 + 256 * i : 512 + 256 * i + 256]
            do_r = do[64 * r : 64 * r + 64]
            p = p_s[2 * r + i]
            dp = nn(v3, spread_t(jnp.transpose(do_r), 64))
            ds = (p * (dp - jnp.sum(p * dp, axis=0, keepdims=True))).astype(bf16)
            rows = slice(512 * r, 512 * r + 512)
            dkv_ref[rows, 256 * i : 256 * i + 256] = nn(
                ds, spread(q3_ref[64 * r : 64 * r + 64, cols], 64)
            ).astype(bf16)
            dkv_ref[rows, 512 + 256 * i : 512 + 256 * i + 256] = nn(
                p.astype(bf16), spread(do_r, 64)
            ).astype(bf16)
            dq.append(fold(tn(ds, k3), 64).astype(bf16))
        dq = jnp.concatenate(dq, axis=0)
        accs[i][at["cq"] : at["cq"] + 256] = one_grad(n3, dq).astype(bf16)
        terms.append(two_back(dq, w.cq))
    part, dg2 = rms_back(z1, g2_ref[...], total(terms))
    dz1 = dz2 + part
    g = dz1.astype(bf16)
    z = x_ref[...].astype(f32)
    n2 = rms(z, g1_ref[...])
    mask = dec_self_mask(ids_ref, dseg_ref, rows_n)
    terms = []
    diags = []
    for i, (w, tab) in enumerate(zip(halves, (taba_ref[...], tabb_ref[0:4, 256:288]))):
        q, k, v = (qkv_ref[:, 512 * c + 256 * i : 512 * c + 256 * i + 256] for c in range(3))
        accs[i][at["out"] : at["out"] + 256] = tn(o2_ref[:, 256 * i : 256 * i + 256], g).astype(bf16)
        do = nt(g, w.out()).astype(bf16)
        s = nn(k, spread_t(jnp.transpose(q), LANE)) + dec_bias_rows(tab, buckets_ref) + mask
        p = jnp.exp(s - lse_ref[i : i + 1, :])
        dp = nn(v, spread_t(jnp.transpose(do), LANE))
        ds = p * (dp - jnp.sum(p * dp, axis=0, keepdims=True))
        diags += [diagonal_sums(ds[:, LANE * h : LANE * h + LANE]) for h in range(4)]
        ds = ds.astype(bf16)
        dk = nn(ds, spread(q, LANE)).astype(bf16)
        dv = nn(p.astype(bf16), spread(do, LANE)).astype(bf16)
        dq = fold(tn(ds, k), LANE).astype(bf16)
        accs[i][at["qk"] : at["qk"] + 512, 0:256] = tn(n2, dq).astype(bf16)
        accs[i][at["qk"] : at["qk"] + 512, 256:512] = tn(n2, dk).astype(bf16)
        accs[i][at["v"] : at["v"] + 256] = one_grad(n2, dv).astype(bf16)
        terms += [nt(dq, w.qk(0)), nt(dk, w.qk(1)), two_back(dv, w.v)]
    part, dg1 = rms_back(z, g1_ref[...], total(terms))
    dx_ref[...] = dz1 + part
    dg_ref[...] = jnp.concatenate([dg1, dg2, dg3], axis=0)
    dtab_ref[:, 0:32] = bucket_sums(jnp.concatenate(diags, axis=0), dec_bucket_rows(buckets_ref))
    move.start(done)
    move.wait()


def dec_main(x, cot, g1, g2, g3, buckets, dseg, seg, pad, ids, qkv, o2, lse, z1, q3, kv, taba, tabb, own, early, pieces):
    n = x.shape[0]
    ins = [x, cot, g1, g2, g3, buckets, dseg, seg, pad, ids, qkv, o2, lse, z1, q3, kv, taba, tabb, *own, early]
    grads = sds((dec_all.rows, 512), bf16)
    outs = [
        sds((n, 512), bf16),
        sds((n, 512), f32),
        sds((kv.shape[0], 1024), bf16),
        grads,
        grads,
        sds((3, 512), f32),
        sds((8, LANE), f32),
    ]
    specs = [whole(a) for a in ins]
    specs[9] = smem
    return pl.pallas_call(
        dec_main_kernel,
        name="dec_cross_ff_back",
        grid=(1,),
        in_specs=specs + [anywhere] * len(pieces),
        out_specs=[anywhere if a is grads else whole(a) for a in outs],
        out_shape=outs,
        scratch_shapes=[
            pltpu.VMEM((512, LANE), f32),
            pltpu.VMEM((4, 512, 256), f32),
            pltpu.VMEM((dec_all.rows, 512), bf16),
            pltpu.VMEM((dec_all.rows, 512), bf16),
            pltpu.VMEM((dec_late.rows, 512), bf16),
            bring_sems(dec_late, len(pieces)),
            place_sems,
        ],
        compiler_params=params(60),
        cost_estimate=cost(6e9, 2e7),
    )(*ins, *pieces)


def natural(flat):
    shapes = {"out": (256, 512), "down": (1024, 512), "up": (512, 1024), "pair": (2, 512, 256), "one": (512, 256)}
    res = []
    for name, kind in flat.layout:
        if name == "qk":
            res.append(("q", (512, 256)))
        elif name == "v":
            res.append(("kv", (2, 512, 256)))
        else:
            res.append((name, shapes[kind]))
    return res


def finish_kernel(flat, small, ids_ref, *rest):
    pieces, rest = rest[:8], rest[8:]
    if small:
        small_ref, rest = rest[0], rest[1:]
        gains, tabs, rest = rest[-10:-4], rest[-4:-2], rest[:-10] + rest[-2:]
        for i, ref in enumerate(gains):
            ref[...] = small_ref[i : i + 1, :]
        for i, ref in enumerate(tabs):
            lanes = slice(LANE * i, LANE * i + 32)
            ref[...] = jnp.where(ids_ref[5] == 0, small_ref[8:12, lanes], small_ref[12:16, lanes])
    *outs, low, sems = rest
    outs = dict(zip([n for n, _ in natural(flat)], outs))
    size = flat.rows // 8
    copies = []
    for p, piece in enumerate(pieces):
        core = ids_ref[1] if p < 4 else 1 - ids_ref[1]
        high, last = p % 4 // 2, p % 2
        y = (high * (1 - core) + last * core) ^ ids_ref[2]
        z0 = (last * (1 - core) + high * core) ^ ids_ref[3]
        to = pl.multiple_of((core * 4 + y * 2 + z0) * size, 16)
        copies.append((piece, low.at[pl.ds(to, size), :]))
    run_all(copies, sems)

    def spread_rows(out, row, rows, from_lane=0, lanes=512, lead=(), to_row=0, to_lane=0):
        def body(t, _):
            src = pl.ds(pl.multiple_of(row + t * 64, 16), 64)
            dst = pl.ds(pl.multiple_of(to_row + t * 64, 16), 64)
            value = low[src, from_lane : from_lane + lanes].astype(f32)
            out[lead + (dst, slice(to_lane, to_lane + lanes))] = value
            return 0

        lax.fori_loop(0, rows // 64, body, 0)

    for name, kind in flat.layout:
        row = flat.at[name]
        if name == "qk":
            spread_rows(outs["q"], row, 512, 0, 256)
            spread_rows(outs["kv"], row, 512, 256, 256, (0,))
        elif name == "v":
            spread_rows(outs["kv"], row, 256, 0, 256, (1,))
            spread_rows(outs["kv"], row, 256, 256, 256, (1,), 256)
        elif kind in ("out", "down"):
            spread_rows(outs[name], row, outs[name].shape[0])
        elif kind == "up":
            spread_rows(outs[name], row, 512)
            spread_rows(outs[name], row + 512, 512, to_lane=512)
        elif kind == "pair":
            spread_rows(outs[name], row, 512, 0, 256, (0,))
            spread_rows(outs[name], row, 512, 256, 256, (1,))
        else:
            spread_rows(outs[name], row, 256, 0, 256)
            spread_rows(outs[name], row, 256, 256, 256, to_row=256)


def finish(flat, ids, pieces, small=None, after=()):
    names = natural(flat)
    ins = [ids, *pieces]
    if small is not None:
        ins.append(small)
        names = names + [(i, (1, 512)) for i in range(6)] + [("enc", (4, 32)), ("dec", (4, 32))]
    outs = [sds(shape, f32) for _, shape in names]
    res = pl.pallas_call(
        ordered(functools.partial(finish_kernel, flat, small is not None), ins, after),
        name="grads_out",
        grid=(1,),
        in_specs=[smem] + [anywhere] * 8 + [whole(a) for a in ins[9:]] + [unused] * len(after),
        out_specs=[whole(o) for o in outs],
        out_shape=outs,
        scratch_shapes=[pltpu.VMEM((flat.rows, 512), bf16), pltpu.SemaphoreType.DMA((8,))],
        compiler_params=params(),
        cost_estimate=cost(1e6, 6 * flat.rows * 512),
    )(*ins, *after)
    return {name: r for (name, _), r in zip(names, res)}


def hop(a, dim0, dim1=None):
    n, m = lax.axis_size("dp"), lax.axis_size("mp")
    pairs = []
    for i in range(n):
        dim = dim1 if dim1 is not None and i % 2 else dim0
        for j in range(m):
            to = (i, (j + 1) % m) if dim == "mp" else (i ^ dim, j)
            pairs.append((i * m + j, to[0] * m + to[1]))
    return lax.ppermute(a, ("dp", "mp"), pairs)


def join(*arrays):
    return lax.optimization_barrier(arrays)


def sum_kernel(*refs):
    refs[-1][...] = total([r[...].astype(f32) for r in refs[:-1]]).astype(bf16)


def sum_rows(terms, first, n, after):
    size = n if n <= 512 else n // 2
    block = pl.BlockSpec((size, 512), lambda t: (first // size + t, 0))
    return pl.pallas_call(
        ordered(sum_kernel, terms, after),
        name="sum_rows",
        grid=(n // size,),
        in_specs=[block] * len(terms) + [unused] * len(after),
        out_specs=pl.BlockSpec((size, 512), lambda t: (t, 0)),
        out_shape=sds((n, 512), bf16),
        compiler_params=params(24),
        cost_estimate=cost(1e6, 2 * 512 * n * (len(terms) + 1)),
    )(*terms, *after)


scatter_dims = [("mp", 4), (2, "mp"), (4, 2)]
gather_dims = [(4, 2), (2, 4)]


class Summed:
    def __init__(self, keep, send):
        self.terms = [keep, hop(send, 1)]
        self.rows = keep.shape[0]
        self.step = 0

    def forward(self, after):
        after = (after,)
        if self.step < len(scatter_dims):
            self.rows //= 2
            value = sum_rows(self.terms, self.rows, self.rows, after)
            self.terms.append(hop(value, *scatter_dims[self.step]))
        elif self.step == len(scatter_dims):
            value = sum_rows(self.terms, 0, self.rows, after)
            self.terms = [value, hop(value, 8)]
        else:
            value = sum_rows(self.terms, 0, self.rows, after)
            bit = 16
            while bit < lax.axis_size("dp"):
                value = sum_rows([value, hop(value, bit)], 0, self.rows, ())
                bit *= 2
            pieces = [value]
            for dims in gather_dims:
                pieces = pieces + [hop(p, *dims) for p in pieces]
            self.pieces = pieces + [hop(p, 1) for p in pieces]
        self.step += 1
        return value


small_dims = [("mp", 4), (2, "mp"), (4, 2), (8, 8), (1, 1)]


def sum_small(value):
    extra, bit = [], 16
    while bit < lax.axis_size("dp"):
        extra.append((bit, bit))
        bit *= 2
    for dims in small_dims + extra:
        value = value + hop(value, *dims)
    return value


def on_device(
    enc_in,
    enc_segments,
    enc_pad,
    enc_buckets,
    dec_in,
    dec_segments,
    dec_buckets,
    enc_cot,
    dec_cot,
    enc_norm1,
    enc_query,
    enc_kv,
    enc_out_proj,
    enc_bias,
    enc_norm2,
    enc_ff_in,
    enc_ff_out,
    enc_final,
    dec_norm1,
    dec_query,
    dec_kv,
    dec_out_proj,
    dec_bias,
    dec_norm2,
    cross_query,
    cross_kv,
    cross_out,
    dec_norm3,
    dec_ff_in,
    dec_ff_out,
):
    rows, length, width = enc_in.shape
    dp = lax.axis_index("dp")
    ids = jnp.stack([lax.axis_index("mp") * rows, dp % 2, dp // 2 % 2, dp // 4 % 2, dp // 8 % 2, lax.axis_index("mp")]).astype(jnp.int32)

    n1g, n2g, nfg = enc_norm1[None, :], enc_norm2[None, :], enc_final[None, :]
    d1g, d2g, d3g = dec_norm1[None, :], dec_norm2[None, :], dec_norm3[None, :]
    rev = jnp.pad(enc_buckets[::-1], (0, 1), constant_values=-1)[None, :]
    places = dec_buckets[None, :]
    x = enc_in.reshape(rows * length, width)
    xc = enc_cot.reshape(rows * length, width)
    z = dec_in.reshape(-1, width)
    zc = dec_cot.reshape(-1, width)

    def flat2(a):
        return a.reshape(rows * length, a.shape[-1])

    e_tab, d_tab = enc_bias.T, dec_bias.T
    q_send = pack_first(ids, e_tab, d_tab, enc_query, enc_kv, enc_out_proj)
    q0 = hop(q_send, "mp")
    m_send, e_send, l_send = pack_rest(
        ids, enc_ff_out, enc_ff_in, cross_kv, dec_ff_out, dec_ff_in, cross_out, cross_query, dec_out_proj,
        dec_query, dec_kv,
    )
    qkv_a, o_a, lse_a = enc_fwd(
        ids, enc_in, n1g, enc_segments, enc_pad, rev, [e_tab, enc_query, enc_kv]
    )
    o_a, q0, m_send = join(o_a, q0, m_send)
    q1 = hop(q0, 1)
    m0 = hop(m_send, "mp")
    qkv_b, o_b, lse_b, w_first, tabs = enc_fwd(ids, enc_in, n1g, enc_segments, enc_pad, rev, [q0, q1])
    o_b, m0, e_send = join(o_b, m0, e_send)
    m1 = hop(m0, 2, 4)
    e0 = hop(e_send, "mp")
    oa2, ob2 = flat2(o_a), flat2(o_b)
    x1, part, h_a, slope_a = mid_own(x, oa2, ob2, n2g, enc_out_proj, w_first, enc_ff_out, enc_ff_in)
    part, m1, e0, l_send = join(part, m1, e0, l_send)
    m2, m3 = hop(m0, 1), hop(m1, 1)
    e1 = hop(e0, 2, 4)
    l0 = hop(l_send, "mp")
    y, enc_out, mem, h_b, slope_b, kv3, w_mid = mid_other(ids, x1, part, n2g, nfg, cross_kv, [m0, m1, m2, m3])
    kv3, e1, l0 = join(kv3, e1, l0)
    e2, e3 = hop(e0, 1), hop(e1, 1)
    l1 = hop(l0, 2, 4)
    own_dec = [dec_ff_out, dec_ff_in, cross_out, cross_query, dec_out_proj, dec_query, dec_kv]
    dqkv, o2, lse2, z1, q3, w_early = dec_first(
        ids, z, d1g, d2g, dec_segments, places, d_tab, tabs, own_dec, [e0, e1, e2, e3]
    )
    z1, l1 = join(z1, l1)
    l2, l3 = hop(l0, 1), hop(l1, 1)
    dec_out, dec_grad, dkv3, dec_keep, dec_send, dgd, tab_d = dec_main(
        z, zc, d1g, d2g, d3g, places, dec_segments, enc_segments, enc_pad, ids,
        dqkv, o2, lse2, z1, q3, kv3, d_tab, tabs, own_dec, w_early, [l0, l1, l2, l3],
    )
    dec_sum = Summed(dec_keep, dec_send)
    dy, dgf = out_grad(dkv3, y, xc, nfg, cross_kv, w_mid)
    token = dec_sum.forward(dy)
    dx1, do, mid_keep, mid_send, dg2 = mid_bwd(
        ids, dy, dkv3, mem, x1, h_a, h_b, slope_a, slope_b, oa2, ob2, n2g, enc_out_proj, w_first,
        enc_ff_out, enc_ff_in, w_mid, (token,),
    )
    token = dec_sum.forward(dx1)
    mid_sum = Summed(mid_keep, mid_send)
    do = do.reshape(rows, length, width)
    dqkv_b, grads_b, tab_b = enc_bwd(
        1, ids, enc_in, n1g, enc_segments, enc_pad, rev, tabs, qkv_b, o_b, do, lse_b, after=(token,)
    )
    token = dec_sum.forward(dqkv_b)
    token = mid_sum.forward(token)
    dqkv_a, qkv_keep, qkv_send, tab_a = enc_bwd(
        0, ids, enc_in, n1g, enc_segments, enc_pad, rev, e_tab, qkv_a, o_a, do, lse_a, grads_b, (token,)
    )
    qkv_sum = Summed(qkv_keep, qkv_send)
    token = dec_sum.forward(dqkv_a)
    token = mid_sum.forward(token)
    enc_grad, small = enc_last(
        ids, x, dx1, flat2(dqkv_a), flat2(dqkv_b), n1g, enc_query, enc_kv, w_first,
        [dg2, dgf, dgd, tab_a, tab_b, tab_d], (token,),
    )
    small = sum_small(small)
    token = enc_grad
    for group in (qkv_sum, mid_sum, qkv_sum, mid_sum, dec_sum, qkv_sum, qkv_sum, mid_sum, qkv_sum):
        token = group.forward(token)
    dec_g = finish(dec_all, ids, dec_sum.pieces, after=(token,))
    qkv_g = finish(enc_qkv, ids, qkv_sum.pieces, small, after=(dec_g["ffo"],))
    mid_g = finish(enc_grads, ids, mid_sum.pieces, after=(qkv_g["q"],))
    return (
        enc_out.reshape(enc_in.shape),
        dec_out.reshape(dec_in.shape),
        enc_grad.reshape(enc_in.shape),
        dec_grad.reshape(dec_in.shape),
        qkv_g[0].reshape(-1),
        qkv_g["q"],
        qkv_g["kv"],
        mid_g["out"],
        qkv_g["enc"].T,
        qkv_g[1].reshape(-1),
        mid_g["ffi"],
        mid_g["ffo"],
        qkv_g[2].reshape(-1),
        qkv_g[3].reshape(-1),
        dec_g["q"],
        dec_g["kv"],
        dec_g["out"],
        qkv_g["dec"].T,
        qkv_g[4].reshape(-1),
        dec_g["cq"],
        mid_g["ckv"],
        dec_g["cout"],
        qkv_g[5].reshape(-1),
        dec_g["ffi"],
        dec_g["ffo"],
    )


def solution(mesh):
    in_specs = (
        P(("dp", "mp"), None, None),
        P("dp", None),
        P("dp", None),
        P(),
        P(("dp", "mp"), None, None),
        P("dp", None),
        P(),
        P(("dp", "mp"), None, None),
        P(("dp", "mp"), None, None),
        P(),
        P(None, "mp"),
        P(None, None, "mp"),
        P("mp", None),
        P(None, "mp"),
        P(),
        P(None, "mp"),
        P("mp", None),
        P(),
        P(),
        P(None, "mp"),
        P(None, None, "mp"),
        P("mp", None),
        P(None, "mp"),
        P(),
        P(None, "mp"),
        P(None, None, "mp"),
        P("mp", None),
        P(),
        P(None, "mp"),
        P("mp", None),
    )
    out_specs = (
        P(("dp", "mp"), None, None),
        P(("dp", "mp"), None, None),
        P(("dp", "mp"), None, None),
        P(("dp", "mp"), None, None),
        P(),
        P(None, "mp"),
        P(None, None, "mp"),
        P("mp", None),
        P(None, "mp"),
        P(),
        P(None, "mp"),
        P("mp", None),
        P(),
        P(),
        P(None, "mp"),
        P(None, None, "mp"),
        P("mp", None),
        P(None, "mp"),
        P(),
        P(None, "mp"),
        P(None, None, "mp"),
        P("mp", None),
        P(),
        P(None, "mp"),
        P("mp", None),
    )
    return jax.shard_map(
        on_device, mesh=mesh, in_specs=in_specs, out_specs=out_specs, check_vma=False
    )
```

```python
import functools

import jax
import jax.numpy as jnp
from jax import lax
from jax.experimental import pallas as pl
from jax.experimental.pallas import tpu as pltpu
from jax.sharding import PartitionSpec as P

f32 = jnp.float32
bf16 = jnp.bfloat16
neg = -1e30
eps = 1e-06
LANE = 128
MIB = 1 << 20


def nn(a, b):
    return lax.dot_general(a, b, (((1,), (0,)), ((), ())), preferred_element_type=f32)


def nt(a, b):
    return lax.dot_general(a, b, (((1,), (1,)), ((), ())), preferred_element_type=f32)


def tn(a, b):
    return lax.dot_general(a, b, (((0,), (0,)), ((), ())), preferred_element_type=f32)


def total(terms):
    return functools.reduce(lambda a, b: a + b, terms)


def rms_parts(v):
    r = lax.rsqrt(jnp.mean(v * v, axis=-1, keepdims=True) + eps)
    return v * r, r


def rms(v, g):
    return (rms_parts(v)[0] * g).astype(bf16)


def rms_back(v, g, dn):
    vr, r = rms_parts(v)
    dg = jnp.sum(dn * vr, axis=0, keepdims=True)
    t = dn * g
    return r * (t - vr * jnp.mean(t * vr, axis=-1, keepdims=True)), dg


def gelu_both(u):
    c = 0.7978845608028654
    u2 = u * u
    t = jnp.tanh(u * (c + (c * 0.044715) * u2))
    half = 0.5 + 0.5 * t
    slope = half + (0.5 * u) * (1.0 - t * t) * (c + (3 * c * 0.044715) * u2)
    return u * half, slope


def params(vmem_mib=56, **kw):
    return pltpu.CompilerParams(vmem_limit_bytes=vmem_mib * MIB, **kw)


def cost(flops, nbytes):
    return pl.CostEstimate(flops=int(flops * 4), bytes_accessed=int(nbytes * 4), transcendentals=0)


smem = pl.BlockSpec(memory_space=pltpu.SMEM)
anywhere = pl.BlockSpec(memory_space=pltpu.HBM)


def ordered(kernel, ins, after):
    n, k = len(ins), len(after)
    return lambda *refs: kernel(*refs[:n], *refs[n + k :])


unused = pl.BlockSpec(memory_space=pl.ANY)


def whole(a):
    return pl.BlockSpec(a.shape, lambda *_: (0,) * a.ndim, pipeline_mode=pl.Buffered(1))


def sds(shape, dtype):
    return jax.ShapeDtypeStruct(shape, dtype)


class Flat:
    sizes = {"out": 256, "up": 1024, "down": 1024, "pair": 512, "one": 256, "tabs": 32}

    def __init__(self, *layout):
        self.at, row = {}, 0
        for name, kind in layout:
            self.at[name] = row
            row += self.sizes[kind]
        self.rows = row
        self.layout = layout

    def blocks(self, n):
        res, row = [], 0
        for name, kind in self.layout:
            runs = 2 if kind == "up" else 1
            size = self.sizes[kind] // runs
            for run in range(runs):
                res.append((self.at[name] + run * size, size // n, row))
                row += size // n
        return res


enc_first = Flat(("out", "out"), ("qk", "pair"), ("v", "one"), ("tabs", "tabs"))
enc_tail = Flat(("qk", "pair"), ("v", "one"), ("small", "one"))
enc_mid = Flat(("ckv", "pair"), ("ffo", "down"), ("ffi", "up"))
dec_early = Flat(("out", "out"), ("cq", "one"), ("qk", "pair"), ("v", "one"))
dec_late = Flat(("ffo", "down"), ("ffi", "up"), ("cout", "out"))
enc_grads = Flat(("ckv", "pair"), ("ffo", "down"), ("ffi", "up"), ("out", "out"))
dec_all = Flat(
    ("ffo", "down"),
    ("ffi", "up"),
    ("cout", "out"),
    ("cq", "one"),
    ("out", "out"),
    ("qk", "pair"),
    ("v", "one"),
)


def chunk_ids(ids_ref, n):
    core, y, z0 = ids_ref[1], ids_ref[2], ids_ref[3]
    if n == 2:
        return [core, 1 - core]
    a = core * 2 + y * (1 - core) + z0 * core
    b = (1 - core) * 2 + z0 * (1 - core) + y * core
    return [a, a ^ 1, b, b ^ 1]


def run_all(copies, sems):
    copies = [pltpu.make_async_copy(a, b, sems.at[i]) for i, (a, b) in enumerate(copies)]
    for c in copies:
        c.start()
    for c in copies:
        c.wait()


def bring(ids_ref, flat, pieces, full, sems):
    n = len(pieces)
    copies = []
    for j, piece in zip(chunk_ids(ids_ref, n), pieces):
        for row, size, at in flat.blocks(n):
            to = pl.multiple_of(row + j * size, 16)
            copies.append((piece.at[at : at + size, :], full.at[pl.ds(to, size), :]))
    run_all(copies, sems)


def bring_sems(flat, n):
    return pltpu.SemaphoreType.DMA((n * len(flat.blocks(n)),))


def chunk_copies(flat, n, j, refs, out):
    copies, row = [], 0

    def add(src, start, rows, lanes=None):
        part = pl.ds(pl.multiple_of(start, 16), rows)
        to = out.at[row : row + rows, :] if lanes is None else out.at[row : row + rows, lanes]
        copies.append((src(part), to))

    left, right = slice(0, 256), slice(256, 512)
    for name, kind in flat.layout:
        ref = refs[name]
        size = flat.sizes[kind] // n
        if kind == "up":
            size //= 2
            add(lambda part: ref.at[part, 0:512], j * size, size)
            row += size
            add(lambda part: ref.at[part, 512:1024], j * size, size)
        elif kind == "pair":
            add(ref[0], j * size, size, left)
            add(ref[1], j * size, size, right)
        elif kind == "one":
            add(ref, j * size, size, left)
            add(ref, 256 + j * size, size, right)
        else:
            add(lambda part: ref.at[part, :], j * size, size)
        row += size
    return copies


def rows_at(ref, *lead):
    return lambda part: ref.at[lead + (part, slice(None))]


def pack_first_kernel(ids_ref, ebias, dbias, eq, ekv, eo, out, tabs, sems):
    tabs[...] = jnp.zeros_like(tabs)
    tabs[0:4, 0:32] = ebias[...]
    tabs[0:4, 256:288] = dbias[...]
    refs = {"qk": (rows_at(eq), rows_at(ekv, 0)), "v": rows_at(ekv, 1), "tabs": tabs, "out": eo}
    run_all(chunk_copies(enc_first, 2, chunk_ids(ids_ref, 2)[0], refs, out), sems)


def pack_rest_kernel(ids_ref, ffo, ffi, ckv, dffo, dffi, cout, cq, do, dq, dkv, sm, se, sl, sems):
    c = chunk_ids(ids_ref, 4)[0]
    mid = {"ckv": (rows_at(ckv, 0), rows_at(ckv, 1)), "ffo": ffo, "ffi": ffi}
    early = {"out": do, "cq": rows_at(cq), "qk": (rows_at(dq), rows_at(dkv, 0)), "v": rows_at(dkv, 1)}
    late = {"ffo": dffo, "ffi": dffi, "cout": cout}
    run_all(
        chunk_copies(enc_mid, 4, c, mid, sm)
        + chunk_copies(dec_early, 4, c, early, se)
        + chunk_copies(dec_late, 4, c, late, sl),
        sems,
    )


def pack_first(ids, ebias, dbias, *weights):
    out = sds((enc_first.rows // 2, 512), bf16)
    return pl.pallas_call(
        pack_first_kernel,
        name="pack_first",
        in_specs=[smem, whole(ebias), whole(dbias)] + [anywhere] * len(weights),
        out_specs=whole(out),
        out_shape=out,
        scratch_shapes=[pltpu.VMEM((32, 512), bf16), pltpu.SemaphoreType.DMA((6,))],
        compiler_params=params(60),
        cost_estimate=cost(1e6, 5e6),
    )(ids, ebias, dbias, *weights)


def pack_rest(ids, *weights):
    outs = [sds((flat.rows // 4, 512), bf16) for flat in (enc_mid, dec_early, dec_late)]
    return pl.pallas_call(
        pack_rest_kernel,
        name="pack_rest",
        in_specs=[smem] + [anywhere] * len(weights),
        out_specs=[whole(a) for a in outs],
        out_shape=outs,
        scratch_shapes=[pltpu.SemaphoreType.DMA((17,))],
        compiler_params=params(60),
        cost_estimate=cost(1e6, 5e6),
    )(ids, *weights)


def one_mul(a, w):
    return nn(a[:, :256], w[:, :256]) + nn(a[:, 256:], w[:, 256:])


def one_back(g, w):
    return jnp.concatenate([nt(g, w[:, :256]), nt(g, w[:, 256:])], axis=1)


def one_grad(a, g):
    full = tn(a, g)
    return jnp.concatenate([full[:256], full[256:]], axis=1)


def bucket_rows(rev_ref):
    rev = pltpu.roll(rev_ref[...], 1024 - 127, 1)
    return lax.broadcasted_iota(jnp.int32, (32, 1024), 0) == rev


def skew_rows(tab, rev_ref, skew_ref):
    w = nn(tab, bucket_rows(rev_ref).astype(bf16))
    for h in range(w.shape[0]):
        base = jnp.broadcast_to(w[h : h + 1], (LANE, 1024))
        skew_ref[h] = pltpu.roll(base, 0, 1, stride=1, stride_axis=0)


def diagonal_sums(a):
    rows, n = a.shape
    while rows > 1:
        rows //= 2
        a = a[:rows] + pltpu.roll(a[rows:], n - rows, 1)
    return a


def bucket_sums(diags, onehot):
    return lax.dot_general(
        diags,
        onehot.astype(f32),
        (((1,), (1,)), ((), ())),
        precision=lax.Precision.HIGHEST,
        preferred_element_type=f32,
    )


def key_codes(seg, pad):
    start = (lax.broadcasted_iota(jnp.int32, seg.shape, 1) == 0) | (seg != pltpu.roll(seg, 1, 1))
    segf = seg.astype(f32)
    return segf, jnp.where((pad == 1) | start, segf, -1.0)


def as_column(row):
    return jnp.transpose(jnp.broadcast_to(row, (LANE, row.shape[1])))


def mask_add(seg, pad, out_ref):
    code, key = key_codes(seg, pad)
    keyc = as_column(key)
    for b in range(seg.shape[1] // LANE):
        out_ref[:, b * LANE : (b + 1) * LANE] = jnp.where(
            keyc == code[:, b * LANE : (b + 1) * LANE], 0.0, neg
        )


def pad_half(a_t, low):
    z = jnp.zeros_like(a_t)
    return jnp.concatenate([a_t, z] if low else [z, a_t], axis=0)


def skew_block(skew_ref, h, q0, width, keys=512):
    return jnp.concatenate(
        [
            skew_ref[h, :, 384 - LANE * b + q0 : 384 - LANE * b + q0 + width]
            for b in range(keys // LANE)
        ],
        axis=0,
    )


QB = 512


def enc_fwd_kernel(own, ids_ref, x_ref, g_ref, seg_ref, pad_ref, rev_ref, *rest):
    step = pl.program_id(0)
    if own:
        tab_ref, wq_ref, wkv_ref, qkv_ref, o_ref, lse_ref, skew, madd, o_t = rest
    else:
        p0, p1, qkv_ref, o_ref, lse_ref, w_ref, tab_ref, skew, madd, o_t, sems = rest

        @pl.when(step == 0)
        def _():
            bring(ids_ref, enc_first, (p0, p1), w_ref, sems)
            tab_ref[...] = w_ref[1024:1056, :]

    @pl.when(step == 0)
    def _():
        skew_rows(tab_ref[0:4, 0:32], rev_ref, skew)

    row = pl.ds(ids_ref[0] + step, 1)
    mask_add(seg_ref[row, :], pad_ref[row, :], madd)
    n1 = rms(x_ref[0].astype(f32), g_ref[...])
    if own:
        q = nn(n1, wq_ref[...]).astype(bf16)
        k = nn(n1, wkv_ref[0]).astype(bf16)
        v = nn(n1, wkv_ref[1]).astype(bf16)
    else:
        qk = nn(n1, w_ref[256:768, :]).astype(bf16)
        q, k = qk[:, :256], qk[:, 256:]
        v = one_mul(n1, w_ref[768:1024, :]).astype(bf16)
    qkv_ref[0, :, 0:256] = q
    qkv_ref[0, :, 256:512] = k
    qkv_ref[0, :, 512:768] = v
    q_t, v_t = jnp.transpose(q), jnp.transpose(v)

    def scores(h):
        pair = slice(LANE * (h // 2), LANE * (h // 2) + LANE)
        qz = pad_half(q_t[64 * h : 64 * h + 64], h % 2 == 0)
        return nn(k[:, pair], qz) + skew_block(skew, h, 0, 512) + madd[...]

    ahead = scores(0)
    for h in range(4):
        s = ahead
        if h < 3:
            ahead = scores(h + 1)
        rows = slice(64 * h, 64 * h + 64)
        m = jnp.max(s, axis=0, keepdims=True)
        e = jnp.exp(s - m)
        norm = jnp.sum(e, axis=0, keepdims=True)
        o_t[rows, :] = nn(v_t[rows], e.astype(bf16)) * (1.0 / norm)
        lse_ref[0, h : h + 1, :] = m + jnp.log(norm)
    o_ref[0] = jnp.transpose(o_t[...]).astype(bf16)


def row_block(width, n=512, at=0):
    return pl.BlockSpec((1, n, width), lambda r: (r, 0, at))


def enc_fwd(ids, x, g, seg, pad, rev, ws):
    rows = x.shape[0]
    own = len(ws) == 3
    more = [] if own else [sds((enc_first.rows, 512), bf16), sds((32, 512), bf16)]
    return pl.pallas_call(
        functools.partial(enc_fwd_kernel, own),
        name="enc_attend_own" if own else "enc_attend_other",
        grid=(rows,),
        in_specs=[smem, row_block(512), whole(g), whole(seg), whole(pad), whole(rev)]
        + [whole(w) if own else anywhere for w in ws],
        out_specs=[row_block(768), row_block(256), row_block(512, 4)] + [whole(a) for a in more],
        out_shape=[
            sds((rows, 512, 768), bf16),
            sds((rows, 512, 256), bf16),
            sds((rows, 4, 512), f32),
        ]
        + more,
        scratch_shapes=[
            pltpu.VMEM((4, LANE, 1024), f32),
            pltpu.VMEM((512, 512), f32),
            pltpu.VMEM((256, 512), f32),
        ]
        + ([] if own else [bring_sems(enc_first, 2)]),
        compiler_params=params(),
        cost_estimate=cost(8e9, 4e6),
    )(ids, x, g, seg, pad, rev, *ws)


def enc_bwd_kernel(
    at_row, ids_ref, seg_ref, pad_ref, rev_ref, tab_ref, qkv_ref, o_ref, do_ref, lse_ref,
    dqkv_ref, dtab_ref, skew, dskew, madd, p_s, ds_s, dq_t, dk_t, dv_t,
):
    skew_rows(tab_ref[0:4, 0:32], rev_ref, skew)
    dskew[...] = jnp.zeros_like(dskew)
    row = pl.ds(ids_ref[0] + at_row, 1)
    mask_add(seg_ref[row, :], pad_ref[row, :], madd)
    q, k, v = qkv_ref[0, :, 0:256], qkv_ref[0, :, 256:512], qkv_ref[0, :, 512:768]
    q_t, k_t, do_t = jnp.transpose(q), jnp.transpose(k), jnp.transpose(do_ref[0])
    o_t = jnp.transpose(o_ref[0])

    def products(h, b):
        pair = slice(LANE * (h // 2), LANE * (h // 2) + LANE)
        rows, cols = slice(64 * h, 64 * h + 64), slice(b, b + QB)
        qz, doz = pad_half(q_t[rows, cols], h % 2 == 0), pad_half(do_t[rows, cols], h % 2 == 0)
        s = nn(k[:, pair], qz) + skew_block(skew, h, b, QB) + madd[:, cols]
        return s, nn(v[:, pair], doz)

    blocks = [(h, b) for h in range(4) for b in range(0, 512, QB)]
    ahead = products(*blocks[0])
    for i, (h, b) in enumerate(blocks):
        s, dp = ahead
        if i + 1 < len(blocks):
            ahead = products(*blocks[i + 1])
        rows, cols = slice(64 * h, 64 * h + 64), slice(b, b + QB)
        inner = jnp.sum(
            do_t[rows, cols].astype(f32) * o_t[rows, cols].astype(f32), axis=0, keepdims=True
        )
        p = jnp.exp(s - lse_ref[0, h : h + 1, cols])
        ds = p * (dp - inner)
        p_s[h % 2, :, cols] = p.astype(bf16)
        ds_s[h % 2, :, cols] = ds.astype(bf16)
        for kb in range(4):
            at = 384 - LANE * kb + b
            dskew[h, :, at : at + QB] += ds[LANE * kb : LANE * kb + LANE]
        if b + QB == 512:
            dv_t[rows] = nt(do_t[rows], p_s[h % 2])
            dk_t[rows] = nt(q_t[rows], ds_s[h % 2])
            dq_t[rows] = nn(k_t[rows], ds_s[h % 2])
    dqkv_ref[0, :, 0:256] = jnp.transpose(dq_t[...]).astype(bf16)
    dqkv_ref[0, :, 256:512] = jnp.transpose(dk_t[...]).astype(bf16)
    dqkv_ref[0, :, 512:768] = jnp.transpose(dv_t[...]).astype(bf16)
    diags = jnp.concatenate([diagonal_sums(dskew[h]) for h in range(4)], axis=0)
    dtab_ref[0:4, 0:32] = bucket_sums(diags, bucket_rows(rev_ref))


orders = {"dec": ("mzy", "zmy"), "mid": ("myz", "zmy"), "tail": ("myz", "zmy")}


def place_of(ids_ref, j, m, order):
    bits = {"m": m, "y": (j // 4 % 2) ^ ids_ref[2], "z": (j // 2 % 2) ^ ids_ref[3]}
    first, second, third = [bits[c] for c in order[j // 8]]
    return first * 8 + second * 4 + third * 2 + j % 2


class Place:
    def __init__(self, group, ids_ref, accs, keep_ref, send_ref, sems):
        self.order = orders[group]
        self.ids_ref, self.accs, self.outs, self.sems = ids_ref, accs, (keep_ref, send_ref), sems
        self.copies = []

    def start(self, first=0, last=16):
        size = self.accs[0].shape[0] // 16
        for j in range(first, last):
            for m in range(2):
                at = pl.multiple_of(place_of(self.ids_ref, j, m, self.order) * size, 16)
                src = self.accs[m].at[j * size : (j + 1) * size, :]
                keep, send = [
                    pltpu.make_async_copy(src, out.at[pl.ds(at, size), :], self.sems.at[2 * j + m])
                    for out in self.outs
                ]
                pl.when(self.ids_ref[1] == j // 8)(keep.start)
                pl.when(self.ids_ref[1] != j // 8)(send.start)
                self.copies.append(keep)

    def wait(self):
        for c in self.copies:
            c.wait()


place_sems = pltpu.SemaphoreType.DMA((32,))


def enc_bwd(half_at, at_row, ids, seg, pad, rev, tab, qkv, o, do, lse, before=None, after=()):
    rows = qkv.shape[0]
    ins = [ids, seg, pad, rev, tab, qkv, o, do, lse]
    more = ([] if before is None else [before]) + list(after)

    def block(width, n=512, at=0):
        return pl.BlockSpec((1, n, width), lambda t: (at_row, 0, at))

    return pl.pallas_call(
        ordered(functools.partial(enc_bwd_kernel, at_row), ins, more),
        name="enc_attend_other_back" if half_at else "enc_attend_own_back",
        grid=(1,),
        in_specs=[smem, whole(seg), whole(pad), whole(rev), whole(tab)]
        + [block(768), block(256), block(256, at=half_at), block(512, 4)]
        + [unused] * len(more),
        out_specs=[block(768), pl.BlockSpec((8, LANE), lambda t: (0, 0))],
        out_shape=[sds((rows, 512, 768), bf16), sds((8, LANE), f32)],
        input_output_aliases={} if before is None else {len(ins): 0},
        scratch_shapes=[
            pltpu.VMEM((4, LANE, 1024), f32),
            pltpu.VMEM((4, LANE, 1024), f32),
            pltpu.VMEM((512, 512), f32),
            pltpu.VMEM((2, 512, 512), bf16),
            pltpu.VMEM((2, 512, 512), bf16),
            pltpu.VMEM((256, 512), f32),
            pltpu.VMEM((256, 512), f32),
            pltpu.VMEM((256, 512), f32),
        ],
        compiler_params=params(),
        cost_estimate=cost(8e9, 4e6),
    )(*ins, *more)


class Mid:
    def __init__(self, ffo=None, ffi=None, ckv=None, flat=None):
        if flat is not None:
            at = enc_mid.at
            self.ffo = lambda c: flat[at["ffo"] + 512 * c : at["ffo"] + 512 * c + 512, :]
            self.ffi = lambda c: flat[at["ffi"] + 512 * c : at["ffi"] + 512 * c + 512, :]
            self.ckv = lambda c: flat[at["ckv"] : at["ckv"] + 512, 256 * c : 256 * c + 256]
        else:
            self.ffo = lambda c: ffo[512 * c : 512 * c + 512, :]
            self.ffi = lambda c: ffi[:, 512 * c : 512 * c + 512]
            self.ckv = lambda c: ckv[c]


def tile_block(tile, width, at=0):
    return pl.BlockSpec((tile, width), lambda t: (t, at))


def rows_of(a, first, n):
    return pl.BlockSpec((n, a.shape[1]), lambda *_: (first // n, 0), pipeline_mode=pl.Buffered(1))


def feed_forward(m1, w, h_ref, slope_ref):
    terms = []
    ahead = nn(m1, w.ffi(0))
    for c in range(2):
        u = ahead
        if c < 1:
            ahead = nn(m1, w.ffi(c + 1))
        h, slope = gelu_both(u)
        h = h.astype(bf16)
        cols = slice(512 * c, 512 * c + 512)
        h_ref[:, cols] = h
        slope_ref[:, cols] = slope.astype(bf16)
        terms.append(nn(h, w.ffo(c)))
    return total(terms)


def mid_own_kernel(x_ref, oa_ref, ob_ref, g2_ref, outa_ref, outb_ref, ffo_ref, ffi_ref, x1_ref, part_ref, h_ref, slope_ref):
    x1 = x_ref[...].astype(f32) + total([nn(oa_ref[...], outa_ref[...]), nn(ob_ref[...], outb_ref[...])])
    x1_ref[...] = x1
    m1 = rms(x1, g2_ref[...])
    part_ref[...] = x1 + feed_forward(m1, Mid(ffo_ref, ffi_ref), h_ref, slope_ref)


def mid_own(x, oa, ob, g2, out_a, w_first, ffo, ffi, tile=256):
    n = x.shape[0]
    return pl.pallas_call(
        mid_own_kernel,
        name="enc_middle_own",
        grid=(n // tile,),
        in_specs=[
            tile_block(tile, 512),
            tile_block(tile, 256),
            tile_block(tile, 256),
            whole(g2),
            whole(out_a),
            pl.BlockSpec((256, 512), lambda t: (0, 0), pipeline_mode=pl.Buffered(1)),
            whole(ffo),
            whole(ffi),
        ],
        out_specs=[tile_block(tile, 512), tile_block(tile, 512), tile_block(tile, 1024), tile_block(tile, 1024)],
        out_shape=[sds((n, 512), f32), sds((n, 512), f32), sds((n, 1024), bf16), sds((n, 1024), bf16)],
        compiler_params=params(),
        cost_estimate=cost(6e9, 1.2e7),
    )(x, oa, ob, g2, out_a, w_first, ffo, ffi)


def mid_other_kernel(ids_ref, x1_ref, part_ref, g2_ref, gf_ref, ckv_ref, p0, p1, p2, p3, y_ref, out_ref, mem_ref, h_ref, slope_ref, kv_ref, w_ref, sems):
    @pl.when(pl.program_id(0) == 0)
    def _():
        bring(ids_ref, enc_mid, (p0, p1, p2, p3), w_ref, sems)

    w = Mid(flat=w_ref)
    m1 = rms(x1_ref[...], g2_ref[...])
    y = part_ref[...] + feed_forward(m1, w, h_ref, slope_ref)
    y_ref[...] = y
    out_ref[...] = y.astype(bf16)
    mem = rms(y, gf_ref[...])
    mem_ref[...] = mem
    for c in range(2):
        for i, half in enumerate((Mid(ckv=ckv_ref), w)):
            at = 512 * c + 256 * i
            kv_ref[:, at : at + 256] = nn(mem, half.ckv(c)).astype(bf16)


def mid_other(ids, x1, part, g2, gf, ckv, pieces, tile=256):
    n = x1.shape[0]
    return pl.pallas_call(
        mid_other_kernel,
        name="enc_middle_other",
        grid=(n // tile,),
        in_specs=[smem, tile_block(tile, 512), tile_block(tile, 512), whole(g2), whole(gf), whole(ckv)]
        + [anywhere] * len(pieces),
        out_specs=[
            tile_block(tile, 512),
            tile_block(tile, 512),
            tile_block(tile, 512),
            tile_block(tile, 1024),
            tile_block(tile, 1024),
            tile_block(tile, 1024),
            whole(sds((enc_mid.rows, 512), bf16)),
        ],
        out_shape=[
            sds((n, 512), f32),
            sds((n, 512), bf16),
            sds((n, 512), bf16),
            sds((n, 1024), bf16),
            sds((n, 1024), bf16),
            sds((n, 1024), bf16),
            sds((enc_mid.rows, 512), bf16),
        ],
        scratch_shapes=[bring_sems(enc_mid, len(pieces))],
        compiler_params=params(),
        cost_estimate=cost(7e9, 1.5e7),
    )(ids, x1, part, g2, gf, ckv, *pieces)


def out_grad_kernel(dkv_ref, y_ref, cot_ref, gf_ref, ckva_ref, ckvb_ref, dy_ref, dgf_ref):
    step = pl.program_id(0)
    terms = []
    for c in range(2):
        for i in range(2):
            d = dkv_ref[:, 512 * c + 256 * i : 512 * c + 256 * i + 256]
            terms.append(nt(d, ckvb_ref[:, 256 * c : 256 * c + 256] if i else ckva_ref[c]))
    part, dgf = rms_back(y_ref[...], gf_ref[...], total(terms))
    dy_ref[...] = cot_ref[...].astype(f32) + part

    @pl.when(step == 0)
    def _():
        dgf_ref[...] = dgf

    @pl.when(step > 0)
    def _():
        dgf_ref[...] += dgf


def out_grad(dkv, y, cot, gf, ckv, w_mid, after=(), tile=256):
    n = y.shape[0]
    ins = [dkv, y, cot, gf, ckv, w_mid]
    return pl.pallas_call(
        ordered(out_grad_kernel, ins, after),
        name="enc_output_back",
        grid=(n // tile,),
        in_specs=[
            tile_block(tile, 1024),
            tile_block(tile, 512),
            tile_block(tile, 512),
            whole(gf),
            whole(ckv),
            rows_of(w_mid, enc_mid.at["ckv"], 512),
        ]
        + [unused] * len(after),
        out_specs=[tile_block(tile, 512), pl.BlockSpec((1, 512), lambda t: (0, 0))],
        out_shape=[sds((n, 512), f32), sds((1, 512), f32)],
        compiler_params=params(),
        cost_estimate=cost(2e9, 8e6),
    )(*ins, *after)


def mid_bwd_kernel(
    ids_ref, dy_ref, dkv_ref, mem_ref, x1_ref, oa_ref, ob_ref, g2_ref, outa_ref, outb_ref,
    ha_ref, hb_ref, sa_ref, sb_ref, ffoa_ref, ffob_ref, ffia_ref, ffib_ref,
    dx1_ref, do_ref, keep_ref, send_ref, dg2_ref, g_s, m1_s, dm1, acc_a, acc_b, sems,
):
    accs = (acc_a, acc_b)
    step = pl.program_id(0)
    at = enc_grads.at

    @pl.when(step == 0)
    def _():
        g_s[...] = dy_ref[...].astype(bf16)
        m1_s[...] = rms(x1_ref[...], g2_ref[...])
        for i in range(2):
            for c in range(2):
                d = dkv_ref[:, 512 * c + 256 * i : 512 * c + 256 * i + 256]
                rows = slice(at["ckv"], at["ckv"] + 512)
                accs[i][rows, 256 * c : 256 * c + 256] = tn(mem_ref[...], d).astype(bf16)

    out_row = pl.ds(pl.multiple_of(at["ffo"] + 256 * step, 256), 256)
    in_row = pl.ds(pl.multiple_of(at["ffi"] + 512 * (step // 2), 512), 512)
    in_lane = pl.ds(pl.multiple_of(256 * (step % 2), 256), 256)
    sides = (
        (acc_a, ha_ref, sa_ref, ffoa_ref, ffia_ref),
        (acc_b, hb_ref, sb_ref, ffob_ref, ffib_ref),
    )
    g = g_s[...]
    dhs = [nt(g, side[3][...]) for side in sides]
    dus = []
    for dh, (acc, h_ref, slope_ref, _, _) in zip(dhs, sides):
        acc[out_row, :] = tn(h_ref[...], g).astype(bf16)
        dus.append((dh * slope_ref[...].astype(f32)).astype(bf16))
    terms = []
    for du, (acc, _, _, _, ffi_ref) in zip(dus, sides):
        acc[in_row, in_lane] = tn(m1_s[...], du).astype(bf16)
        terms.append(nt(du, ffi_ref[...]))

    @pl.when(step == 0)
    def _():
        dm1[...] = total(terms)

    @pl.when(step > 0)
    def _():
        dm1[...] += total(terms)

    @pl.when(step == 3)
    def _():
        move = Place("mid", ids_ref, accs, keep_ref, send_ref, sems)
        ready = at["out"] // (enc_grads.rows // 16)
        move.start(0, ready)
        part, dg2_ref[...] = rms_back(x1_ref[...], g2_ref[...], dm1[...])
        dx1 = dy_ref[...] + part
        dx1_ref[...] = dx1
        g_s[...] = dx1.astype(bf16)
        for i, (o_ref, out_ref) in enumerate(((oa_ref, outa_ref), (ob_ref, outb_ref))):
            accs[i][at["out"] : at["out"] + 256, :] = tn(o_ref[...], g_s[...]).astype(bf16)
        move.start(ready)
        for i, out_ref in enumerate((outa_ref, outb_ref)):
            do_ref[:, 256 * i : 256 * i + 256] = nt(g_s[...], out_ref[...]).astype(bf16)
        move.wait()


def mid_bwd(ids, dy, dkv, mem, x1, ha, hb, sa, sb, oa, ob, g2, out_a, w_first, ffo, ffi, w_mid, after=()):
    n = dy.shape[0]
    grads = sds((enc_grads.rows, 512), bf16)
    hidden = pl.BlockSpec((n, 256), lambda t: (0, t))
    down, up = enc_mid.at["ffo"] // 256, enc_mid.at["ffi"] // 512
    outs = [sds((n, 512), f32), sds((n, 512), bf16), grads, grads, sds((1, 512), f32)]
    ins = [ids, dy, dkv, mem, x1, oa, ob, g2, out_a, w_first, ha, hb, sa, sb, ffo, w_mid, ffi, w_mid]
    return pl.pallas_call(
        ordered(mid_bwd_kernel, ins, after),
        name="enc_middle_back",
        grid=(4,),
        in_specs=[smem]
        + [whole(a) for a in (dy, dkv, mem, x1, oa, ob, g2, out_a)]
        + [
            pl.BlockSpec((256, 512), lambda t: (0, 0), pipeline_mode=pl.Buffered(1)),
            hidden,
            hidden,
            hidden,
            hidden,
            pl.BlockSpec((256, 512), lambda t: (t, 0)),
            pl.BlockSpec((256, 512), lambda t: (down + t, 0)),
            pl.BlockSpec((512, 256), lambda t: (0, t)),
            pl.BlockSpec((512, 256), lambda t: (up + t // 2, t % 2)),
        ]
        + [unused] * len(after),
        out_specs=[anywhere if a is grads else whole(a) for a in outs],
        out_shape=outs,
        scratch_shapes=[
            pltpu.VMEM((n, 512), bf16),
            pltpu.VMEM((n, 512), bf16),
            pltpu.VMEM((n, 512), f32),
            pltpu.VMEM((enc_grads.rows, 512), bf16),
            pltpu.VMEM((enc_grads.rows, 512), bf16),
            place_sems,
        ],
        compiler_params=params(56),
        cost_estimate=cost(20e9, 3e7),
    )(*ins, *after)


def enc_last_kernel(
    steps, ids_ref, x_ref, dx1_ref, da_ref, db_ref, g_ref, wq_ref, wkv_ref, w_ref, dg2_ref, dgf_ref, dgd_ref,
    ta0_ref, ta1_ref, tb0_ref, tb1_ref, tabd_ref, out_ref, keep_ref, send_ref, acc_a, acc_b, low_a, low_b, dg_s, sems,
):
    step = pl.program_id(0)
    da, db = da_ref[...], db_ref[...]
    x = x_ref[...].astype(f32)
    n1 = rms(x, g_ref[...])
    for acc, d in ((acc_a, da), (acc_b, db)):
        dqk = tn(n1, d[:, 0:512])
        dv = tn(n1, d[:, 512:768])

        @pl.when(step == 0)
        def _():
            acc[0:512] = dqk
            acc[512:768, 0:256] = dv[:256]
            acc[512:768, 256:512] = dv[256:]

        @pl.when(step > 0)
        def _():
            acc[0:512] += dqk
            acc[512:768, 0:256] += dv[:256]
            acc[512:768, 256:512] += dv[256:]

    dn = total(
        [
            nt(da[:, 0:256], wq_ref[...]),
            nt(da[:, 256:512], wkv_ref[0]),
            nt(da[:, 512:768], wkv_ref[1]),
            nt(db[:, 0:512], w_ref[256:768, :]),
            one_back(db[:, 512:768], w_ref[768:1024, :]),
        ]
    )
    part, dg = rms_back(x, g_ref[...], dn)
    out_ref[...] = dx1_ref[...] + part

    @pl.when(step == 0)
    def _():
        dg_s[0:1, :] = dg

    @pl.when(step > 0)
    def _():
        dg_s[0:1, :] += dg

    @pl.when(step == steps - 1)
    def _():
        same = jnp.concatenate(
            [dg_s[0:1, :], dg2_ref[...], dgf_ref[...], dgd_ref[...], jnp.zeros((2, 512), f32)], axis=0
        )
        for acc, low, t0, t1, first in ((acc_a, low_a, ta0_ref, ta1_ref, 0), (acc_b, low_b, tb0_ref, tb1_ref, 4)):
            low[0:768] = acc[...].astype(bf16)
            tabs = jnp.concatenate([(t0[...] + t1[...])[0:4], tabd_ref[first : first + 4, :]], axis=1)
            tabs = jnp.concatenate([tabs, jnp.zeros((4, 256), f32)], axis=1)
            small = jnp.concatenate([same, tabs, jnp.zeros((4, 512), f32)], axis=0)
            high = small.astype(bf16)
            low[768:784] = high
            low[784:800] = (small - high.astype(f32)).astype(bf16)
            low[800:1024] = jnp.zeros((224, 512), bf16)
        move = Place("tail", ids_ref, (low_a, low_b), keep_ref, send_ref, sems)
        move.start()
        move.wait()


def enc_last(ids, x, dx1, da, db, g, wq, wkv, w_first, smalls, after=(), tile=512):
    n = x.shape[0]
    grads = sds((enc_tail.rows, 512), bf16)
    ins = [ids, x, dx1, da, db, g, wq, wkv, w_first, *smalls]
    return pl.pallas_call(
        ordered(functools.partial(enc_last_kernel, n // tile), ins, after),
        name="enc_input_back",
        grid=(n // tile,),
        in_specs=[
            smem,
            tile_block(tile, 512),
            tile_block(tile, 512),
            tile_block(tile, 768),
            tile_block(tile, 768),
            whole(g),
            whole(wq),
            whole(wkv),
            whole(w_first),
        ]
        + [whole(a) for a in smalls]
        + [unused] * len(after),
        out_specs=[tile_block(tile, 512), anywhere, anywhere],
        out_shape=[sds((n, 512), f32), grads, grads],
        scratch_shapes=[pltpu.VMEM((768, 512), f32)] * 2
        + [pltpu.VMEM((1024, 512), bf16)] * 2
        + [pltpu.VMEM((8, 512), f32), place_sems],
        compiler_params=params(),
        cost_estimate=cost(6e9, 1e7),
    )(*ins, *after)


class Dec:
    def __init__(self, natural=None, early=None, late=None):
        if natural is not None:
            ffo, ffi, cout, cq, out, q, kv = natural
            self.ffo = lambda c: ffo[512 * c : 512 * c + 512, :]
            self.ffi = lambda c: ffi[:, 512 * c : 512 * c + 512]
            self.cout = lambda: cout[...]
            self.cq = lambda c: cq[256 * c : 256 * c + 256, :]
            self.out = lambda: out[...]
            self.qk = lambda c: q[...] if c == 0 else kv[0]
            self.v = lambda c: kv[1, 256 * c : 256 * c + 256, :]
        else:
            at = {**dec_early.at, **dec_late.at}
            self.ffo = lambda c: late[at["ffo"] + 512 * c : at["ffo"] + 512 * c + 512, :]
            self.ffi = lambda c: late[at["ffi"] + 512 * c : at["ffi"] + 512 * c + 512, :]
            self.cout = lambda: late[at["cout"] : at["cout"] + 256, :]
            self.cq = lambda c: early[at["cq"] : at["cq"] + 256, 256 * c : 256 * c + 256]
            self.out = lambda: early[at["out"] : at["out"] + 256, :]
            self.qk = lambda c: early[at["qk"] : at["qk"] + 512, 256 * c : 256 * c + 256]
            self.v = lambda c: early[at["v"] : at["v"] + 256, 256 * c : 256 * c + 256]


def two_mul(a, w):
    return nn(a[:, :256], w(0)) + nn(a[:, 256:], w(1))


def two_back(g, w):
    return jnp.concatenate([nt(g, w(0)), nt(g, w(1))], axis=1)


def spread_t(a_t, width):
    tiled = jnp.concatenate([a_t] * 4, axis=1)
    head = lax.broadcasted_iota(jnp.int32, tiled.shape, 0) // 64
    block = lax.broadcasted_iota(jnp.int32, tiled.shape, 1) // width
    return jnp.where(head == block, tiled, jnp.zeros((), a_t.dtype))


def spread(a, height):
    tiled = jnp.concatenate([a] * 4, axis=0)
    block = lax.broadcasted_iota(jnp.int32, tiled.shape, 0) // height
    head = lax.broadcasted_iota(jnp.int32, tiled.shape, 1) // 64
    return jnp.where(head == block, tiled, jnp.zeros((), a.dtype))


def fold(full, height):
    head = lax.broadcasted_iota(jnp.int32, (height, 256), 1) // 64
    total = jnp.zeros((height, 256), f32)
    for h in range(4):
        total = total + jnp.where(head == h, full[height * h : height * h + height], 0.0)
    return total


def dec_bucket_rows(buckets_ref):
    b = buckets_ref[...]
    b = jnp.concatenate([b, jnp.full((1, LANE - b.shape[1]), -1, jnp.int32)], axis=1)
    return lax.broadcasted_iota(jnp.int32, (32, LANE), 0) == b


def dec_bias_rows(tab, buckets_ref):
    w = nn(tab, dec_bucket_rows(buckets_ref).astype(bf16))
    return jnp.concatenate(
        [
            pltpu.roll(jnp.broadcast_to(w[h : h + 1], (LANE, LANE)), 0, 1, stride=1, stride_axis=0)
            for h in range(4)
        ],
        axis=1,
    )


def dec_self_mask(ids_ref, dseg_ref, rows):
    code = jnp.concatenate(
        [(dseg_ref[pl.ds(ids_ref[0] + r, 1), :] + 8 * r).astype(f32) for r in range(rows)], axis=1
    )
    key = as_column(code)
    j = lax.broadcasted_iota(jnp.int32, (LANE, LANE), 0)
    i = lax.broadcasted_iota(jnp.int32, (LANE, LANE), 1)
    one = jnp.where((key == code) & (j <= i), 0.0, neg)
    return jnp.concatenate([one] * 4, axis=1)


def dec_first_kernel(ids_ref, x_ref, g1_ref, g2_ref, dseg_ref, buckets_ref, taba_ref, tabb_ref, *rest):
    pieces = rest[7:11]
    qkv_ref, o_ref, lse_ref, z1_ref, q3_ref, w_ref, sems = rest[11:]
    halves = (Dec(rest[:7]), Dec(early=w_ref))
    bring(ids_ref, dec_early, pieces, w_ref, sems)
    z = x_ref[...].astype(f32)
    n2 = rms(z, g1_ref[...])
    mask = dec_self_mask(ids_ref, dseg_ref, x_ref.shape[0] // 64)
    terms = []
    for i, (w, tab) in enumerate(zip(halves, (taba_ref[...], tabb_ref[0:4, 256:288]))):
        q = nn(n2, w.qk(0)).astype(bf16)
        k = nn(n2, w.qk(1)).astype(bf16)
        v = two_mul(n2, w.v).astype(bf16)
        for c, a in enumerate((q, k, v)):
            qkv_ref[:, 512 * c + 256 * i : 512 * c + 256 * i + 256] = a
        s = nn(k, spread_t(jnp.transpose(q), LANE)) + dec_bias_rows(tab, buckets_ref) + mask
        m = jnp.max(s, axis=0, keepdims=True)
        e = jnp.exp(s - m)
        norm = jnp.sum(e, axis=0, keepdims=True)
        p = (e * (1.0 / norm)).astype(bf16)
        lse_ref[i : i + 1, :] = m + jnp.log(norm)
        o = fold(tn(p, v), LANE).astype(bf16)
        o_ref[:, 256 * i : 256 * i + 256] = o
        terms.append(nn(o, w.out()))
    z1 = z + total(terms)
    z1_ref[...] = z1
    n3 = rms(z1, g2_ref[...])
    for i, w in enumerate(halves):
        q3_ref[:, 256 * i : 256 * i + 256] = two_mul(n3, w.cq).astype(bf16)


def dec_first(ids, x, g1, g2, dseg, buckets, taba, tabb, own, pieces):
    n = x.shape[0]
    ins = [x, g1, g2, dseg, buckets, taba, tabb, *own]
    return pl.pallas_call(
        dec_first_kernel,
        name="dec_self",
        grid=(1,),
        in_specs=[smem] + [whole(a) for a in ins] + [anywhere] * len(pieces),
        out_specs=[
            pl.BlockSpec(s, lambda t: (0, 0))
            for s in ((n, 1536), (n, 512), (2, 512), (n, 512), (n, 512), (dec_early.rows, 512))
        ],
        out_shape=[
            sds((n, 1536), bf16),
            sds((n, 512), bf16),
            sds((2, 512), f32),
            sds((n, 512), f32),
            sds((n, 512), bf16),
            sds((dec_early.rows, 512), bf16),
        ],
        scratch_shapes=[bring_sems(dec_early, len(pieces))],
        compiler_params=params(),
        cost_estimate=cost(1e9, 8e6),
    )(ids, *ins, *pieces)


def dec_main_kernel(
    x_ref,
    cot_ref,
    g1_ref,
    g2_ref,
    g3_ref,
    buckets_ref,
    dseg_ref,
    seg_ref,
    pad_ref,
    ids_ref,
    qkv_ref,
    o2_ref,
    lse_ref,
    z1_ref,
    q3_ref,
    kv_ref,
    taba_ref,
    tabb_ref,
    *rest,
):
    early, pieces = rest[7], rest[8:12]
    out_ref, dx_ref, dkv_ref, keep_ref, send_ref, dg_ref, dtab_ref = rest[12:19]
    madd, p_s, acc_a, acc_b, late, sems, move_sems = rest[19:]
    halves = (Dec(rest[:7]), Dec(early=early, late=late))
    bring(ids_ref, dec_late, pieces, late, sems)
    accs = (acc_a, acc_b)
    at = dec_all.at
    rows_n = x_ref.shape[0] // 64
    z1 = z1_ref[...]
    mixed = [[None] * rows_n, [None] * rows_n]
    for r in range(rows_n):
        row = pl.ds(ids_ref[0] + r, 1)
        keyc = as_column(key_codes(seg_ref[row, :], pad_ref[row, :])[1])
        code = dseg_ref[row, :].astype(f32)
        madd[...] = jnp.where(keyc == jnp.concatenate([code, code], axis=1), 0.0, neg)
        both = jnp.concatenate([madd[...]] * 2, axis=1)
        for i in range(2):
            cols = slice(256 * i, 256 * i + 256)
            k3 = kv_ref[512 * r : 512 * r + 512, 256 * i : 256 * i + 256]
            v3 = kv_ref[512 * r : 512 * r + 512, 512 + 256 * i : 512 + 256 * i + 256]
            q_t = jnp.transpose(q3_ref[64 * r : 64 * r + 64, cols])
            s = nn(k3, spread_t(q_t, 64)) + both
            m = jnp.max(s, axis=0, keepdims=True)
            e = jnp.exp(s - m)
            p = e * (1.0 / jnp.sum(e, axis=0, keepdims=True))
            p_s[2 * r + i] = p
            mixed[i][r] = fold(tn(p.astype(bf16), v3), 64).astype(bf16)
    o3 = [jnp.concatenate(m, axis=0) for m in mixed]
    z2 = z1 + total([nn(o, w.cout()) for o, w in zip(o3, halves)])
    n4 = rms(z2, g3_ref[...])
    terms, kept = [], []
    for i, w in enumerate(halves):
        for c in range(2):
            h, slope = gelu_both(nn(n4, w.ffi(c)))
            h = h.astype(bf16)
            kept.append((h, slope))
            terms.append(nn(h, w.ffo(c)))
    out_ref[...] = (z2 + total(terms)).astype(bf16)
    g = cot_ref[...]
    terms = []
    for i, w in enumerate(halves):
        for c in range(2):
            h, slope = kept[2 * i + c]
            accs[i][at["ffo"] + 512 * c : at["ffo"] + 512 * c + 512] = tn(h, g).astype(bf16)
            du = (nt(g, w.ffo(c)) * slope).astype(bf16)
            accs[i][at["ffi"] + 512 * c : at["ffi"] + 512 * c + 512] = tn(n4, du).astype(bf16)
            terms.append(nt(du, w.ffi(c)))
    part, dg3 = rms_back(z2, g3_ref[...], total(terms))
    dz2 = g.astype(f32) + part
    move = Place("dec", ids_ref, accs, keep_ref, send_ref, move_sems)
    done = 2048 // (dec_all.rows // 16)
    move.start(0, done)
    g = dz2.astype(bf16)
    n3 = rms(z1, g2_ref[...])
    terms = []
    for i, w in enumerate(halves):
        cols = slice(256 * i, 256 * i + 256)
        accs[i][at["cout"] : at["cout"] + 256] = tn(o3[i], g).astype(bf16)
        do = nt(g, w.cout()).astype(bf16)
        dq = []
        for r in range(rows_n):
            k3 = kv_ref[512 * r : 512 * r + 512, 256 * i : 256 * i + 256]
            v3 = kv_ref[512 * r : 512 * r + 512, 512 + 256 * i : 512 + 256 * i + 256]
            do_r = do[64 * r : 64 * r + 64]
            p = p_s[2 * r + i]
            dp = nn(v3, spread_t(jnp.transpose(do_r), 64))
            ds = (p * (dp - jnp.sum(p * dp, axis=0, keepdims=True))).astype(bf16)
            rows = slice(512 * r, 512 * r + 512)
            dkv_ref[rows, 256 * i : 256 * i + 256] = nn(
                ds, spread(q3_ref[64 * r : 64 * r + 64, cols], 64)
            ).astype(bf16)
            dkv_ref[rows, 512 + 256 * i : 512 + 256 * i + 256] = nn(
                p.astype(bf16), spread(do_r, 64)
            ).astype(bf16)
            dq.append(fold(tn(ds, k3), 64).astype(bf16))
        dq = jnp.concatenate(dq, axis=0)
        accs[i][at["cq"] : at["cq"] + 256] = one_grad(n3, dq).astype(bf16)
        terms.append(two_back(dq, w.cq))
    part, dg2 = rms_back(z1, g2_ref[...], total(terms))
    dz1 = dz2 + part
    g = dz1.astype(bf16)
    z = x_ref[...].astype(f32)
    n2 = rms(z, g1_ref[...])
    mask = dec_self_mask(ids_ref, dseg_ref, rows_n)
    terms = []
    diags = []
    for i, (w, tab) in enumerate(zip(halves, (taba_ref[...], tabb_ref[0:4, 256:288]))):
        q, k, v = (qkv_ref[:, 512 * c + 256 * i : 512 * c + 256 * i + 256] for c in range(3))
        accs[i][at["out"] : at["out"] + 256] = tn(o2_ref[:, 256 * i : 256 * i + 256], g).astype(bf16)
        do = nt(g, w.out()).astype(bf16)
        s = nn(k, spread_t(jnp.transpose(q), LANE)) + dec_bias_rows(tab, buckets_ref) + mask
        p = jnp.exp(s - lse_ref[i : i + 1, :])
        dp = nn(v, spread_t(jnp.transpose(do), LANE))
        ds = p * (dp - jnp.sum(p * dp, axis=0, keepdims=True))
        diags += [diagonal_sums(ds[:, LANE * h : LANE * h + LANE]) for h in range(4)]
        ds = ds.astype(bf16)
        dk = nn(ds, spread(q, LANE)).astype(bf16)
        dv = nn(p.astype(bf16), spread(do, LANE)).astype(bf16)
        dq = fold(tn(ds, k), LANE).astype(bf16)
        accs[i][at["qk"] : at["qk"] + 512, 0:256] = tn(n2, dq).astype(bf16)
        accs[i][at["qk"] : at["qk"] + 512, 256:512] = tn(n2, dk).astype(bf16)
        accs[i][at["v"] : at["v"] + 256] = one_grad(n2, dv).astype(bf16)
        terms += [nt(dq, w.qk(0)), nt(dk, w.qk(1)), two_back(dv, w.v)]
    part, dg1 = rms_back(z, g1_ref[...], total(terms))
    dx_ref[...] = dz1 + part
    dg_ref[...] = jnp.concatenate([dg1, dg2, dg3], axis=0)
    dtab_ref[:, 0:32] = bucket_sums(jnp.concatenate(diags, axis=0), dec_bucket_rows(buckets_ref))
    move.start(done)
    move.wait()


def dec_main(x, cot, g1, g2, g3, buckets, dseg, seg, pad, ids, qkv, o2, lse, z1, q3, kv, taba, tabb, own, early, pieces):
    n = x.shape[0]
    ins = [x, cot, g1, g2, g3, buckets, dseg, seg, pad, ids, qkv, o2, lse, z1, q3, kv, taba, tabb, *own, early]
    grads = sds((dec_all.rows, 512), bf16)
    outs = [
        sds((n, 512), bf16),
        sds((n, 512), f32),
        sds((kv.shape[0], 1024), bf16),
        grads,
        grads,
        sds((3, 512), f32),
        sds((8, LANE), f32),
    ]
    specs = [whole(a) for a in ins]
    specs[9] = smem
    return pl.pallas_call(
        dec_main_kernel,
        name="dec_cross_ff_back",
        grid=(1,),
        in_specs=specs + [anywhere] * len(pieces),
        out_specs=[anywhere if a is grads else whole(a) for a in outs],
        out_shape=outs,
        scratch_shapes=[
            pltpu.VMEM((512, LANE), f32),
            pltpu.VMEM((4, 512, 256), f32),
            pltpu.VMEM((dec_all.rows, 512), bf16),
            pltpu.VMEM((dec_all.rows, 512), bf16),
            pltpu.VMEM((dec_late.rows, 512), bf16),
            bring_sems(dec_late, len(pieces)),
            place_sems,
        ],
        compiler_params=params(60),
        cost_estimate=cost(6e9, 2e7),
    )(*ins, *pieces)


def natural(flat):
    shapes = {"out": (256, 512), "down": (1024, 512), "up": (512, 1024), "pair": (2, 512, 256), "one": (512, 256)}
    res = []
    for name, kind in flat.layout:
        if name == "qk":
            res.append(("q", (512, 256)))
        elif name == "v":
            res.append(("kv", (2, 512, 256)))
        elif name == "small":
            res += [(i, (1, 512)) for i in range(6)] + [("enc", (4, 32)), ("dec", (4, 32))]
        else:
            res.append((name, shapes[kind]))
    return res


def finish_parts(flat):
    parts = []
    for name, kind in flat.layout:
        row = flat.at[name]
        if name == "qk":
            parts += [("q", (), row, 512, 0, 256, 0, 0), ("kv", (0,), row, 512, 256, 256, 0, 0)]
        elif name == "v":
            parts += [("kv", (1,), row, 256, 0, 256, 0, 0), ("kv", (1,), row, 256, 256, 256, 256, 0)]
        elif kind in ("out", "down"):
            for at in range(0, flat.sizes[kind], 256):
                parts.append((name, (), row + at, 256, 0, 512, at, 0))
        elif kind == "up":
            for at in range(0, 512, 256):
                parts.append((name, (), row + at, 256, 0, 512, at, 0))
                parts.append((name, (), row + 512 + at, 256, 0, 512, at, 512))
        elif kind == "pair":
            parts += [(name, (c,), row, 512, 256 * c, 256, 0, 0) for c in range(2)]
        elif name != "small":
            parts += [(name, (), row, 256, 256 * c, 256, 256 * c, 0) for c in range(2)]
    return parts


def finish_kernel(flat, ids_ref, *rest):
    parts = finish_parts(flat)
    pieces, (*outs, low, wide, sems, out_sems) = rest[:8], rest[8:]
    outs = dict(zip([n for n, _ in natural(flat)], outs))
    size = flat.rows // 8
    copies = []
    for p in range(8):
        piece = pieces[p]
        core = ids_ref[1] if p < 4 else 1 - ids_ref[1]
        high, last = p % 4 // 2, p % 2
        y = (high * (1 - core) + last * core) ^ ids_ref[2]
        z0 = (last * (1 - core) + high * core) ^ ids_ref[3]
        to = pl.multiple_of((core * 4 + y * 2 + z0) * size, 16)
        copies.append((piece, low.at[pl.ds(to, size), :]))
    run_all(copies, sems)
    sent = []
    for i, (name, lead, row, rows, lane, lanes, to_row, to_lane) in enumerate(parts):

        def body(t, _):
            src = pl.ds(pl.multiple_of(row + t * 64, 16), 64)
            dst = pl.ds(pl.multiple_of(t * 64, 16), 64)
            wide[i, dst, 0:lanes] = low[src, lane : lane + lanes].astype(f32)
            return 0

        lax.fori_loop(0, rows // 64, body, 0)
        copy = pltpu.make_async_copy(
            wide.at[i, 0:rows, 0:lanes],
            outs[name].at[lead + (slice(to_row, to_row + rows), slice(to_lane, to_lane + lanes))],
            out_sems.at[i],
        )
        copy.start()
        sent.append(copy)
    if "small" in flat.at:
        row = flat.at["small"]
        small = low[row : row + 16, :].astype(f32) + low[row + 16 : row + 32, :].astype(f32)
        for i in range(6):
            outs[i][...] = small[i : i + 1, :]
        outs["enc"][...] = small[8:12, 0:32]
        outs["dec"][...] = small[8:12, LANE : LANE + 32]
    for copy in sent:
        copy.wait()


def finish(flat, ids, pieces, after=()):
    names = natural(flat)
    ins = [ids, *pieces]
    outs = [sds(shape, f32) for _, shape in names]
    parts = finish_parts(flat)
    tall = max(p[3] for p in parts)
    moved = {p[0] for p in parts}
    res = pl.pallas_call(
        ordered(functools.partial(finish_kernel, flat), ins, after),
        name="grads_out",
        grid=(1,),
        in_specs=[smem] + [anywhere] * 8 + [unused] * len(after),
        out_specs=[anywhere if name in moved else whole(o) for (name, _), o in zip(names, outs)],
        out_shape=outs,
        scratch_shapes=[
            pltpu.VMEM((flat.rows, 512), bf16),
            pltpu.VMEM((len(parts), tall, 512), f32),
            pltpu.SemaphoreType.DMA((8,)),
            pltpu.SemaphoreType.DMA((len(parts),)),
        ],
        compiler_params=params(),
        cost_estimate=cost(1e6, 6 * flat.rows * 512),
    )(*ins, *after)
    return {name: r for (name, _), r in zip(names, res)}


def hop(a, dim0, dim1=None):
    n, m = lax.axis_size("dp"), lax.axis_size("mp")
    pairs = []
    for i in range(n):
        dim = dim1 if dim1 is not None and i % 2 else dim0
        for j in range(m):
            to = (i, (j + 1) % m) if dim == "mp" else (i ^ dim, j)
            pairs.append((i * m + j, to[0] * m + to[1]))
    return lax.ppermute(a, ("dp", "mp"), pairs)


def join(*arrays):
    return lax.optimization_barrier(arrays)


def sum_rows(terms, first, n):
    return total([t[first : first + n].astype(f32) for t in terms]).astype(bf16)


def sum_kernel(*refs):
    refs[-1][...] = total([r[...].astype(f32) for r in refs[:-1]]).astype(bf16)


def sum_after(terms, first, n, after):
    size = n if n <= 512 else n // 2
    block = pl.BlockSpec((size, 512), lambda t: (first // size + t, 0))
    return pl.pallas_call(
        ordered(sum_kernel, terms, (after,)),
        name="sum_rows",
        grid=(n // size,),
        in_specs=[block] * len(terms) + [unused],
        out_specs=pl.BlockSpec((size, 512), lambda t: (t, 0)),
        out_shape=sds((n, 512), bf16),
        compiler_params=params(24),
        cost_estimate=cost(1e6, 2 * 512 * n * (len(terms) + 1)),
    )(*terms, after)


axes = {"m": "mp", "y": 2, "z": 4}
TAIL = "mtdmttmtt"
gather_dims = [(4, 2), (2, 4)]


class Summed:
    def __init__(self, group, keep, send):
        self.dims = [(axes[a], axes[b]) for a, b in zip(*orders[group])]
        self.terms = [keep, hop(send, 1)]
        self.rows = keep.shape[0]
        self.step = 0

    def forward(self, after=None):
        def added(first, n):
            return sum_rows(self.terms, first, n) if after is None else sum_after(self.terms, first, n, after)

        if self.step < len(self.dims):
            self.rows //= 2
            value = added(self.rows, self.rows)
            self.terms.append(hop(value, *self.dims[self.step]))
        elif self.step == len(self.dims):
            value = added(0, self.rows)
            self.terms = [value, hop(value, 8)]
        else:
            value = added(0, self.rows)
            bit = 16
            while bit < lax.axis_size("dp"):
                value = sum_rows([value, hop(value, bit)], 0, self.rows)
                bit *= 2
            pieces = [value]
            for dims in gather_dims:
                pieces = pieces + [hop(p, *dims) for p in pieces]
            self.pieces = pieces + [hop(p, 1) for p in pieces]
        self.step += 1
        return value

    def finish(self):
        while self.step < len(self.dims) + 2:
            self.forward()
        return self.pieces


def on_device(
    enc_in,
    enc_segments,
    enc_pad,
    enc_buckets,
    dec_in,
    dec_segments,
    dec_buckets,
    enc_cot,
    dec_cot,
    enc_norm1,
    enc_query,
    enc_kv,
    enc_out_proj,
    enc_bias,
    enc_norm2,
    enc_ff_in,
    enc_ff_out,
    enc_final,
    dec_norm1,
    dec_query,
    dec_kv,
    dec_out_proj,
    dec_bias,
    dec_norm2,
    cross_query,
    cross_kv,
    cross_out,
    dec_norm3,
    dec_ff_in,
    dec_ff_out,
):
    rows, length, width = enc_in.shape
    dp = lax.axis_index("dp")
    ids = jnp.stack([lax.axis_index("mp") * rows, dp % 2, dp // 2 % 2, dp // 4 % 2, dp // 8 % 2, lax.axis_index("mp")]).astype(jnp.int32)

    n1g, n2g, nfg = enc_norm1[None, :], enc_norm2[None, :], enc_final[None, :]
    d1g, d2g, d3g = dec_norm1[None, :], dec_norm2[None, :], dec_norm3[None, :]
    rev = jnp.pad(enc_buckets[::-1], (0, 1), constant_values=-1)[None, :]
    places = dec_buckets[None, :]
    x = enc_in.reshape(rows * length, width)
    xc = enc_cot.reshape(rows * length, width)
    z = dec_in.reshape(-1, width)
    zc = dec_cot.reshape(-1, width)

    def flat2(a):
        return a.reshape(rows * length, a.shape[-1])

    e_tab, d_tab = enc_bias.T, dec_bias.T
    q_send = pack_first(ids, e_tab, d_tab, enc_query, enc_kv, enc_out_proj)
    q0 = hop(q_send, "mp")
    m_send, e_send, l_send = pack_rest(
        ids, enc_ff_out, enc_ff_in, cross_kv, dec_ff_out, dec_ff_in, cross_out, cross_query, dec_out_proj,
        dec_query, dec_kv,
    )
    qkv_a, o_a, lse_a = enc_fwd(
        ids, enc_in, n1g, enc_segments, enc_pad, rev, [e_tab, enc_query, enc_kv]
    )
    o_a, q0, m_send = join(o_a, q0, m_send)
    q1 = hop(q0, 1)
    m0 = hop(m_send, "mp")
    qkv_b, o_b, lse_b, w_first, tabs = enc_fwd(ids, enc_in, n1g, enc_segments, enc_pad, rev, [q0, q1])
    o_b, m0, e_send = join(o_b, m0, e_send)
    m1 = hop(m0, 2, 4)
    e0 = hop(e_send, "mp")
    oa2, ob2 = flat2(o_a), flat2(o_b)
    x1, part, h_a, slope_a = mid_own(x, oa2, ob2, n2g, enc_out_proj, w_first, enc_ff_out, enc_ff_in)
    part, m1, e0, l_send = join(part, m1, e0, l_send)
    m2, m3 = hop(m0, 1), hop(m1, 1)
    e1 = hop(e0, 2, 4)
    l0 = hop(l_send, "mp")
    y, enc_out, mem, h_b, slope_b, kv3, w_mid = mid_other(ids, x1, part, n2g, nfg, cross_kv, [m0, m1, m2, m3])
    kv3, e1, l0 = join(kv3, e1, l0)
    e2, e3 = hop(e0, 1), hop(e1, 1)
    l1 = hop(l0, 2, 4)
    own_dec = [dec_ff_out, dec_ff_in, cross_out, cross_query, dec_out_proj, dec_query, dec_kv]
    dqkv, o2, lse2, z1, q3, w_early = dec_first(
        ids, z, d1g, d2g, dec_segments, places, d_tab, tabs, own_dec, [e0, e1, e2, e3]
    )
    z1, l1 = join(z1, l1)
    l2, l3 = hop(l0, 1), hop(l1, 1)
    dec_out, dec_grad, dkv3, dec_keep, dec_send, dgd, tab_d = dec_main(
        z, zc, d1g, d2g, d3g, places, dec_segments, enc_segments, enc_pad, ids,
        dqkv, o2, lse2, z1, q3, kv3, d_tab, tabs, own_dec, w_early, [l0, l1, l2, l3],
    )
    dec_sum = Summed("dec", dec_keep, dec_send)
    dy, dgf = out_grad(dkv3, y, xc, nfg, cross_kv, w_mid)
    dx1, do, mid_keep, mid_send, dg2 = mid_bwd(
        ids, dy, dkv3, mem, x1, h_a, h_b, slope_a, slope_b, oa2, ob2, n2g, enc_out_proj, w_first,
        enc_ff_out, enc_ff_in, w_mid, (dec_sum.forward(),),
    )
    mid_sum = Summed("mid", mid_keep, mid_send)
    do = do.reshape(rows, length, width)

    def back(half, row, before, *after):
        if half:
            return enc_bwd(1, row, ids, enc_segments, enc_pad, rev, tabs, qkv_b, o_b, do, lse_b, before, after)
        return enc_bwd(0, row, ids, enc_segments, enc_pad, rev, e_tab, qkv_a, o_a, do, lse_a, before, after)

    dqkv_b, tb0 = back(1, 0, None, dec_sum.forward())
    dqkv_b, tb1 = back(1, 1, dqkv_b, mid_sum.forward())
    dqkv_a, ta0 = back(0, 0, None, dec_sum.forward(), tb1)
    dqkv_a, ta1 = back(0, 1, dqkv_a)
    enc_grad, tail_keep, tail_send = enc_last(
        ids, x, dx1, flat2(dqkv_a), flat2(dqkv_b), n1g, enc_query, enc_kv, w_first,
        [dg2, dgf, dgd, ta0, ta1, tb0, tb1, tab_d], (dec_sum.forward(), mid_sum.forward()),
    )
    tail_sum = Summed("tail", tail_keep, tail_send)
    dec_g = finish(dec_all, ids, dec_sum.finish())
    mid_g = finish(enc_grads, ids, mid_sum.finish())
    tail_g = finish(enc_tail, ids, tail_sum.finish())
    return (
        enc_out.reshape(enc_in.shape),
        dec_out.reshape(dec_in.shape),
        enc_grad.reshape(enc_in.shape),
        dec_grad.reshape(dec_in.shape),
        tail_g[0].reshape(-1),
        tail_g["q"],
        tail_g["kv"],
        mid_g["out"],
        tail_g["enc"].T,
        tail_g[1].reshape(-1),
        mid_g["ffi"],
        mid_g["ffo"],
        tail_g[2].reshape(-1),
        tail_g[3].reshape(-1),
        dec_g["q"],
        dec_g["kv"],
        dec_g["out"],
        tail_g["dec"].T,
        tail_g[4].reshape(-1),
        dec_g["cq"],
        mid_g["ckv"],
        dec_g["cout"],
        tail_g[5].reshape(-1),
        dec_g["ffi"],
        dec_g["ffo"],
    )


def solution(mesh):
    in_specs = (
        P(("dp", "mp"), None, None),
        P("dp", None),
        P("dp", None),
        P(),
        P(("dp", "mp"), None, None),
        P("dp", None),
        P(),
        P(("dp", "mp"), None, None),
        P(("dp", "mp"), None, None),
        P(),
        P(None, "mp"),
        P(None, None, "mp"),
        P("mp", None),
        P(None, "mp"),
        P(),
        P(None, "mp"),
        P("mp", None),
        P(),
        P(),
        P(None, "mp"),
        P(None, None, "mp"),
        P("mp", None),
        P(None, "mp"),
        P(),
        P(None, "mp"),
        P(None, None, "mp"),
        P("mp", None),
        P(),
        P(None, "mp"),
        P("mp", None),
    )
    out_specs = (
        P(("dp", "mp"), None, None),
        P(("dp", "mp"), None, None),
        P(("dp", "mp"), None, None),
        P(("dp", "mp"), None, None),
        P(),
        P(None, "mp"),
        P(None, None, "mp"),
        P("mp", None),
        P(None, "mp"),
        P(),
        P(None, "mp"),
        P("mp", None),
        P(),
        P(),
        P(None, "mp"),
        P(None, None, "mp"),
        P("mp", None),
        P(None, "mp"),
        P(),
        P(None, "mp"),
        P(None, None, "mp"),
        P("mp", None),
        P(),
        P(None, "mp"),
        P("mp", None),
    )
    return jax.shard_map(
        on_device, mesh=mesh, in_specs=in_specs, out_specs=out_specs, check_vma=False
    )
```

```python
import functools

import jax
import jax.numpy as jnp
from jax import lax
from jax.experimental import pallas as pl
from jax.experimental.pallas import tpu as pltpu
from jax.sharding import PartitionSpec as P

f32 = jnp.float32
bf16 = jnp.bfloat16
neg = -1e30
eps = 1e-06
LANE = 128
MIB = 1 << 20


def nn(a, b):
    return lax.dot_general(a, b, (((1,), (0,)), ((), ())), preferred_element_type=f32)


def nt(a, b):
    return lax.dot_general(a, b, (((1,), (1,)), ((), ())), preferred_element_type=f32)


def tn(a, b):
    return lax.dot_general(a, b, (((0,), (0,)), ((), ())), preferred_element_type=f32)


def total(terms):
    return functools.reduce(lambda a, b: a + b, terms)


def rms_parts(v):
    r = lax.rsqrt(jnp.mean(v * v, axis=-1, keepdims=True) + eps)
    return v * r, r


def rms(v, g):
    return (rms_parts(v)[0] * g).astype(bf16)


def rms_back(v, g, dn):
    vr, r = rms_parts(v)
    dg = jnp.sum(dn * vr, axis=0, keepdims=True)
    t = dn * g
    return r * (t - vr * jnp.mean(t * vr, axis=-1, keepdims=True)), dg


def gelu_both(u):
    c = 0.7978845608028654
    u2 = u * u
    t = jnp.tanh(u * (c + (c * 0.044715) * u2))
    half = 0.5 + 0.5 * t
    slope = half + (0.5 * u) * (1.0 - t * t) * (c + (3 * c * 0.044715) * u2)
    return u * half, slope


def params(vmem_mib=56, **kw):
    return pltpu.CompilerParams(vmem_limit_bytes=vmem_mib * MIB, **kw)


def cost(flops, nbytes):
    return pl.CostEstimate(flops=int(flops * 2), bytes_accessed=int(nbytes * 2), transcendentals=0)


smem = pl.BlockSpec(memory_space=pltpu.SMEM)
anywhere = pl.BlockSpec(memory_space=pltpu.HBM)


def ordered(kernel, ins, after):
    n, k = len(ins), len(after)
    return lambda *refs: kernel(*refs[:n], *refs[n + k :])


unused = pl.BlockSpec(memory_space=pl.ANY)


def whole(a):
    return pl.BlockSpec(a.shape, lambda *_: (0,) * a.ndim, pipeline_mode=pl.Buffered(1))


def sds(shape, dtype):
    return jax.ShapeDtypeStruct(shape, dtype)


class Flat:
    sizes = {"out": 256, "up": 1024, "down": 1024, "pair": 512, "one": 256, "tabs": 32}

    def __init__(self, *layout):
        self.at, row = {}, 0
        for name, kind in layout:
            self.at[name] = row
            row += self.sizes[kind]
        self.rows = row
        self.layout = layout

    def blocks(self, n):
        res, row = [], 0
        for name, kind in self.layout:
            runs = 2 if kind == "up" else 1
            size = self.sizes[kind] // runs
            for run in range(runs):
                res.append((self.at[name] + run * size, size // n, row))
                row += size // n
        return res


enc_first = Flat(("out", "out"), ("qk", "pair"), ("v", "one"), ("tabs", "tabs"))
enc_tail = Flat(("qk", "pair"), ("v", "one"), ("small", "one"))
enc_mid = Flat(("ckv", "pair"), ("ffo", "down"), ("ffi", "up"))
dec_early = Flat(("out", "out"), ("cq", "one"), ("qk", "pair"), ("v", "one"))
dec_late = Flat(("ffo", "down"), ("ffi", "up"), ("cout", "out"))
enc_grads = Flat(("ckv", "pair"), ("ffo", "down"), ("ffi", "up"), ("out", "out"))
dec_all = Flat(
    ("ffo", "down"),
    ("ffi", "up"),
    ("cout", "out"),
    ("cq", "one"),
    ("out", "out"),
    ("qk", "pair"),
    ("v", "one"),
)


def chunk_ids(ids_ref, n):
    core, y, z0 = ids_ref[1], ids_ref[2], ids_ref[3]
    if n == 2:
        return [core, 1 - core]
    a = core * 2 + y * (1 - core) + z0 * core
    b = (1 - core) * 2 + z0 * (1 - core) + y * core
    return [a, a ^ 1, b, b ^ 1]


def run_all(copies, sems):
    copies = [pltpu.make_async_copy(a, b, sems.at[i]) for i, (a, b) in enumerate(copies)]
    for c in copies:
        c.start()
    for c in copies:
        c.wait()


def bring(ids_ref, flat, pieces, full, sems):
    n = len(pieces)
    copies = []
    for j, piece in zip(chunk_ids(ids_ref, n), pieces):
        for row, size, at in flat.blocks(n):
            to = pl.multiple_of(row + j * size, 16)
            copies.append((piece.at[at : at + size, :], full.at[pl.ds(to, size), :]))
    run_all(copies, sems)


def bring_sems(flat, n):
    return pltpu.SemaphoreType.DMA((n * len(flat.blocks(n)),))


def chunk_copies(flat, n, j, refs, out):
    copies, row = [], 0

    def add(src, start, rows, lanes=None):
        part = pl.ds(pl.multiple_of(start, 16), rows)
        to = out.at[row : row + rows, :] if lanes is None else out.at[row : row + rows, lanes]
        copies.append((src(part), to))

    left, right = slice(0, 256), slice(256, 512)
    for name, kind in flat.layout:
        ref = refs[name]
        size = flat.sizes[kind] // n
        if kind == "up":
            size //= 2
            add(lambda part: ref.at[part, 0:512], j * size, size)
            row += size
            add(lambda part: ref.at[part, 512:1024], j * size, size)
        elif kind == "pair":
            add(ref[0], j * size, size, left)
            add(ref[1], j * size, size, right)
        elif kind == "one":
            add(ref, j * size, size, left)
            add(ref, 256 + j * size, size, right)
        else:
            add(lambda part: ref.at[part, :], j * size, size)
        row += size
    return copies


def rows_at(ref, *lead):
    return lambda part: ref.at[lead + (part, slice(None))]


def pack_first_kernel(ids_ref, ebias, dbias, eq, ekv, eo, out, tabs, sems):
    tabs[...] = jnp.zeros_like(tabs)
    tabs[0:4, 0:32] = ebias[...]
    tabs[0:4, 256:288] = dbias[...]
    refs = {"qk": (rows_at(eq), rows_at(ekv, 0)), "v": rows_at(ekv, 1), "tabs": tabs, "out": eo}
    run_all(chunk_copies(enc_first, 2, chunk_ids(ids_ref, 2)[0], refs, out), sems)


def pack_rest_kernel(ids_ref, ffo, ffi, ckv, dffo, dffi, cout, cq, do, dq, dkv, sm, se, sl, sems):
    c = chunk_ids(ids_ref, 4)[0]
    mid = {"ckv": (rows_at(ckv, 0), rows_at(ckv, 1)), "ffo": ffo, "ffi": ffi}
    early = {"out": do, "cq": rows_at(cq), "qk": (rows_at(dq), rows_at(dkv, 0)), "v": rows_at(dkv, 1)}
    late = {"ffo": dffo, "ffi": dffi, "cout": cout}
    run_all(
        chunk_copies(enc_mid, 4, c, mid, sm)
        + chunk_copies(dec_early, 4, c, early, se)
        + chunk_copies(dec_late, 4, c, late, sl),
        sems,
    )


def pack_first(ids, ebias, dbias, *weights):
    out = sds((enc_first.rows // 2, 512), bf16)
    return pl.pallas_call(
        pack_first_kernel,
        name="pack_first",
        in_specs=[smem, whole(ebias), whole(dbias)] + [anywhere] * len(weights),
        out_specs=whole(out),
        out_shape=out,
        scratch_shapes=[pltpu.VMEM((32, 512), bf16), pltpu.SemaphoreType.DMA((6,))],
        compiler_params=params(60),
        cost_estimate=cost(1e6, 5e6),
    )(ids, ebias, dbias, *weights)


def pack_rest(ids, *weights):
    outs = [sds((flat.rows // 4, 512), bf16) for flat in (enc_mid, dec_early, dec_late)]
    return pl.pallas_call(
        pack_rest_kernel,
        name="pack_rest",
        in_specs=[smem] + [anywhere] * len(weights),
        out_specs=[whole(a) for a in outs],
        out_shape=outs,
        scratch_shapes=[pltpu.SemaphoreType.DMA((17,))],
        compiler_params=params(60),
        cost_estimate=cost(1e6, 5e6),
    )(ids, *weights)


def one_mul(a, w):
    return nn(a[:, :256], w[:, :256]) + nn(a[:, 256:], w[:, 256:])


def one_back(g, w):
    return jnp.concatenate([nt(g, w[:, :256]), nt(g, w[:, 256:])], axis=1)


def one_grad(a, g):
    full = tn(a, g)
    return jnp.concatenate([full[:256], full[256:]], axis=1)


def bucket_rows(rev_ref):
    rev = pltpu.roll(rev_ref[...], 1024 - 127, 1)
    return lax.broadcasted_iota(jnp.int32, (32, 1024), 0) == rev


def skew_rows(tab, rev_ref, skew_ref):
    w = nn(tab, bucket_rows(rev_ref).astype(bf16))
    for h in range(w.shape[0]):
        base = jnp.broadcast_to(w[h : h + 1], (LANE, 1024))
        skew_ref[h] = pltpu.roll(base, 0, 1, stride=1, stride_axis=0)


def diagonal_sums(a):
    rows, n = a.shape
    while rows > 1:
        rows //= 2
        a = a[:rows] + pltpu.roll(a[rows:], n - rows, 1)
    return a


def bucket_sums(diags, onehot):
    return lax.dot_general(
        diags,
        onehot.astype(f32),
        (((1,), (1,)), ((), ())),
        precision=lax.Precision.HIGHEST,
        preferred_element_type=f32,
    )


def key_codes(seg, pad):
    start = (lax.broadcasted_iota(jnp.int32, seg.shape, 1) == 0) | (seg != pltpu.roll(seg, 1, 1))
    segf = seg.astype(f32)
    return segf, jnp.where((pad == 1) | start, segf, -1.0)


def as_column(row):
    return jnp.transpose(jnp.broadcast_to(row, (LANE, row.shape[1])))


def mask_add(seg, pad, out_ref):
    code, key = key_codes(seg, pad)
    keyc = as_column(key)
    for b in range(seg.shape[1] // LANE):
        out_ref[:, b * LANE : (b + 1) * LANE] = jnp.where(
            keyc == code[:, b * LANE : (b + 1) * LANE], 0.0, neg
        )


def pad_half(a_t, low):
    z = jnp.zeros_like(a_t)
    return jnp.concatenate([a_t, z] if low else [z, a_t], axis=0)


def skew_block(skew_ref, h, q0, width, keys=512):
    return jnp.concatenate(
        [
            skew_ref[h, :, 384 - LANE * b + q0 : 384 - LANE * b + q0 + width]
            for b in range(keys // LANE)
        ],
        axis=0,
    )


QB = 512


def enc_fwd_kernel(own, ids_ref, x_ref, g_ref, seg_ref, pad_ref, rev_ref, *rest):
    step = pl.program_id(0)
    if own:
        tab_ref, wq_ref, wkv_ref, qkv_ref, o_ref, lse_ref, skew, madd, o_t = rest
    else:
        p0, p1, qkv_ref, o_ref, lse_ref, w_ref, tab_ref, skew, madd, o_t, sems = rest

        @pl.when(step == 0)
        def _():
            bring(ids_ref, enc_first, (p0, p1), w_ref, sems)
            tab_ref[...] = w_ref[1024:1056, :]

    @pl.when(step == 0)
    def _():
        skew_rows(tab_ref[0:4, 0:32], rev_ref, skew)

    row = pl.ds(ids_ref[0] + step, 1)
    mask_add(seg_ref[row, :], pad_ref[row, :], madd)
    n1 = rms(x_ref[0].astype(f32), g_ref[...])
    if own:
        q = nn(n1, wq_ref[...]).astype(bf16)
        k = nn(n1, wkv_ref[0]).astype(bf16)
        v = nn(n1, wkv_ref[1]).astype(bf16)
    else:
        qk = nn(n1, w_ref[256:768, :]).astype(bf16)
        q, k = qk[:, :256], qk[:, 256:]
        v = one_mul(n1, w_ref[768:1024, :]).astype(bf16)
    qkv_ref[0, :, 0:256] = q
    qkv_ref[0, :, 256:512] = k
    qkv_ref[0, :, 512:768] = v
    q_t, v_t = jnp.transpose(q), jnp.transpose(v)

    def scores(h):
        pair = slice(LANE * (h // 2), LANE * (h // 2) + LANE)
        qz = pad_half(q_t[64 * h : 64 * h + 64], h % 2 == 0)
        return nn(k[:, pair], qz) + skew_block(skew, h, 0, 512) + madd[...]

    ahead = scores(0)
    for h in range(4):
        s = ahead
        if h < 3:
            ahead = scores(h + 1)
        rows = slice(64 * h, 64 * h + 64)
        m = jnp.max(s, axis=0, keepdims=True)
        e = jnp.exp(s - m)
        norm = jnp.sum(e, axis=0, keepdims=True)
        o_t[rows, :] = nn(v_t[rows], e.astype(bf16)) * (1.0 / norm)
        lse_ref[0, h : h + 1, :] = m + jnp.log(norm)
    o_ref[0] = jnp.transpose(o_t[...]).astype(bf16)


def row_block(width, n=512, at=0):
    return pl.BlockSpec((1, n, width), lambda r: (r, 0, at))


def enc_fwd(ids, x, g, seg, pad, rev, ws):
    rows = x.shape[0]
    own = len(ws) == 3
    more = [] if own else [sds((enc_first.rows, 512), bf16), sds((32, 512), bf16)]
    return pl.pallas_call(
        functools.partial(enc_fwd_kernel, own),
        name="enc_attend_own" if own else "enc_attend_other",
        grid=(rows,),
        in_specs=[smem, row_block(512), whole(g), whole(seg), whole(pad), whole(rev)]
        + [whole(w) if own else anywhere for w in ws],
        out_specs=[row_block(768), row_block(256), row_block(512, 4)] + [whole(a) for a in more],
        out_shape=[
            sds((rows, 512, 768), bf16),
            sds((rows, 512, 256), bf16),
            sds((rows, 4, 512), f32),
        ]
        + more,
        scratch_shapes=[
            pltpu.VMEM((4, LANE, 1024), f32),
            pltpu.VMEM((512, 512), f32),
            pltpu.VMEM((256, 512), f32),
        ]
        + ([] if own else [bring_sems(enc_first, 2)]),
        compiler_params=params(),
        cost_estimate=cost(8e9, 4e6),
    )(ids, x, g, seg, pad, rev, *ws)


def enc_bwd_kernel(
    at_row, ids_ref, seg_ref, pad_ref, rev_ref, tab_ref, qkv_ref, o_ref, do_ref, lse_ref,
    dqkv_ref, dtab_ref, skew, dskew, madd, p_s, ds_s, dq_t, dk_t, dv_t,
):
    skew_rows(tab_ref[0:4, 0:32], rev_ref, skew)
    dskew[...] = jnp.zeros_like(dskew)
    row = pl.ds(ids_ref[0] + at_row, 1)
    mask_add(seg_ref[row, :], pad_ref[row, :], madd)
    q, k, v = qkv_ref[0, :, 0:256], qkv_ref[0, :, 256:512], qkv_ref[0, :, 512:768]
    q_t, k_t, do_t = jnp.transpose(q), jnp.transpose(k), jnp.transpose(do_ref[0])
    o_t = jnp.transpose(o_ref[0])

    def products(h, b):
        pair = slice(LANE * (h // 2), LANE * (h // 2) + LANE)
        rows, cols = slice(64 * h, 64 * h + 64), slice(b, b + QB)
        qz, doz = pad_half(q_t[rows, cols], h % 2 == 0), pad_half(do_t[rows, cols], h % 2 == 0)
        s = nn(k[:, pair], qz) + skew_block(skew, h, b, QB) + madd[:, cols]
        return s, nn(v[:, pair], doz)

    blocks = [(h, b) for h in range(4) for b in range(0, 512, QB)]
    ahead = products(*blocks[0])
    for i, (h, b) in enumerate(blocks):
        s, dp = ahead
        if i + 1 < len(blocks):
            ahead = products(*blocks[i + 1])
        rows, cols = slice(64 * h, 64 * h + 64), slice(b, b + QB)
        inner = jnp.sum(
            do_t[rows, cols].astype(f32) * o_t[rows, cols].astype(f32), axis=0, keepdims=True
        )
        p = jnp.exp(s - lse_ref[0, h : h + 1, cols])
        ds = p * (dp - inner)
        p_s[h % 2, :, cols] = p.astype(bf16)
        ds_s[h % 2, :, cols] = ds.astype(bf16)
        for kb in range(4):
            at = 384 - LANE * kb + b
            dskew[h, :, at : at + QB] += ds[LANE * kb : LANE * kb + LANE]
        if b + QB == 512:
            dv_t[rows] = nt(do_t[rows], p_s[h % 2])
            dk_t[rows] = nt(q_t[rows], ds_s[h % 2])
            dq_t[rows] = nn(k_t[rows], ds_s[h % 2])
    dqkv_ref[0, :, 0:256] = jnp.transpose(dq_t[...]).astype(bf16)
    dqkv_ref[0, :, 256:512] = jnp.transpose(dk_t[...]).astype(bf16)
    dqkv_ref[0, :, 512:768] = jnp.transpose(dv_t[...]).astype(bf16)
    diags = jnp.concatenate([diagonal_sums(dskew[h]) for h in range(4)], axis=0)
    dtab_ref[0:4, 0:32] = bucket_sums(diags, bucket_rows(rev_ref))


orders = {"dec": ("mzy", "zmy"), "mid": ("myz", "zmy"), "tail": ("mzy", "ymz")}


def place_of(ids_ref, j, m, order):
    bits = {"m": m, "y": (j // 4 % 2) ^ ids_ref[2], "z": (j // 2 % 2) ^ ids_ref[3]}
    first, second, third = [bits[c] for c in order[j // 8]]
    return first * 8 + second * 4 + third * 2 + j % 2


class Place:
    def __init__(self, group, ids_ref, accs, keep_ref, send_ref, sems):
        self.order = orders[group]
        self.ids_ref, self.accs, self.outs, self.sems = ids_ref, accs, (keep_ref, send_ref), sems
        self.copies = []

    def start(self, first=0, last=16):
        size = self.accs[0].shape[0] // 16
        for j in range(first, last):
            for m in range(2):
                at = pl.multiple_of(place_of(self.ids_ref, j, m, self.order) * size, 16)
                src = self.accs[m].at[j * size : (j + 1) * size, :]
                keep, send = [
                    pltpu.make_async_copy(src, out.at[pl.ds(at, size), :], self.sems.at[2 * j + m])
                    for out in self.outs
                ]
                pl.when(self.ids_ref[1] == j // 8)(keep.start)
                pl.when(self.ids_ref[1] != j // 8)(send.start)
                self.copies.append(keep)

    def wait(self):
        for c in self.copies:
            c.wait()


place_sems = pltpu.SemaphoreType.DMA((32,))


def enc_bwd(half_at, at_row, ids, seg, pad, rev, tab, qkv, o, do, lse, before=None, after=()):
    rows = qkv.shape[0]
    ins = [ids, seg, pad, rev, tab, qkv, o, do, lse]
    more = ([] if before is None else [before]) + list(after)

    def block(width, n=512, at=0):
        return pl.BlockSpec((1, n, width), lambda t: (at_row, 0, at))

    return pl.pallas_call(
        ordered(functools.partial(enc_bwd_kernel, at_row), ins, more),
        name="enc_attend_other_back" if half_at else "enc_attend_own_back",
        grid=(1,),
        in_specs=[smem, whole(seg), whole(pad), whole(rev), whole(tab)]
        + [block(768), block(256), block(256, at=half_at), block(512, 4)]
        + [unused] * len(more),
        out_specs=[block(768), pl.BlockSpec((8, LANE), lambda t: (0, 0))],
        out_shape=[sds((rows, 512, 768), bf16), sds((8, LANE), f32)],
        input_output_aliases={} if before is None else {len(ins): 0},
        scratch_shapes=[
            pltpu.VMEM((4, LANE, 1024), f32),
            pltpu.VMEM((4, LANE, 1024), f32),
            pltpu.VMEM((512, 512), f32),
            pltpu.VMEM((2, 512, 512), bf16),
            pltpu.VMEM((2, 512, 512), bf16),
            pltpu.VMEM((256, 512), f32),
            pltpu.VMEM((256, 512), f32),
            pltpu.VMEM((256, 512), f32),
        ],
        compiler_params=params(),
        cost_estimate=cost(8e9, 4e6),
    )(*ins, *more)


class Mid:
    def __init__(self, ffo=None, ffi=None, ckv=None, flat=None):
        if flat is not None:
            at = enc_mid.at
            self.ffo = lambda c: flat[at["ffo"] + 512 * c : at["ffo"] + 512 * c + 512, :]
            self.ffi = lambda c: flat[at["ffi"] + 512 * c : at["ffi"] + 512 * c + 512, :]
            self.ckv = lambda c: flat[at["ckv"] : at["ckv"] + 512, 256 * c : 256 * c + 256]
        else:
            self.ffo = lambda c: ffo[512 * c : 512 * c + 512, :]
            self.ffi = lambda c: ffi[:, 512 * c : 512 * c + 512]
            self.ckv = lambda c: ckv[c]


def tile_block(tile, width, at=0):
    return pl.BlockSpec((tile, width), lambda t: (t, at))


def rows_of(a, first, n):
    return pl.BlockSpec((n, a.shape[1]), lambda *_: (first // n, 0), pipeline_mode=pl.Buffered(1))


def feed_forward(m1, w, h_ref, slope_ref):
    terms = []
    ahead = nn(m1, w.ffi(0))
    for c in range(2):
        u = ahead
        if c < 1:
            ahead = nn(m1, w.ffi(c + 1))
        h, slope = gelu_both(u)
        h = h.astype(bf16)
        cols = slice(512 * c, 512 * c + 512)
        h_ref[:, cols] = h
        slope_ref[:, cols] = slope.astype(bf16)
        terms.append(nn(h, w.ffo(c)))
    return total(terms)


def mid_own_kernel(x_ref, oa_ref, ob_ref, g2_ref, outa_ref, outb_ref, ffo_ref, ffi_ref, x1_ref, part_ref, h_ref, slope_ref):
    x1 = x_ref[...].astype(f32) + total([nn(oa_ref[...], outa_ref[...]), nn(ob_ref[...], outb_ref[...])])
    x1_ref[...] = x1
    m1 = rms(x1, g2_ref[...])
    part_ref[...] = x1 + feed_forward(m1, Mid(ffo_ref, ffi_ref), h_ref, slope_ref)


def mid_own(x, oa, ob, g2, out_a, w_first, ffo, ffi, tile=256):
    n = x.shape[0]
    return pl.pallas_call(
        mid_own_kernel,
        name="enc_middle_own",
        grid=(n // tile,),
        in_specs=[
            tile_block(tile, 512),
            tile_block(tile, 256),
            tile_block(tile, 256),
            whole(g2),
            whole(out_a),
            pl.BlockSpec((256, 512), lambda t: (0, 0), pipeline_mode=pl.Buffered(1)),
            whole(ffo),
            whole(ffi),
        ],
        out_specs=[tile_block(tile, 512), tile_block(tile, 512), tile_block(tile, 1024), tile_block(tile, 1024)],
        out_shape=[sds((n, 512), f32), sds((n, 512), f32), sds((n, 1024), bf16), sds((n, 1024), bf16)],
        compiler_params=params(),
        cost_estimate=cost(6e9, 1.2e7),
    )(x, oa, ob, g2, out_a, w_first, ffo, ffi)


def mid_other_kernel(ids_ref, x1_ref, part_ref, g2_ref, gf_ref, ckv_ref, p0, p1, p2, p3, y_ref, out_ref, mem_ref, h_ref, slope_ref, kv_ref, w_ref, sems):
    @pl.when(pl.program_id(0) == 0)
    def _():
        bring(ids_ref, enc_mid, (p0, p1, p2, p3), w_ref, sems)

    w = Mid(flat=w_ref)
    m1 = rms(x1_ref[...], g2_ref[...])
    y = part_ref[...] + feed_forward(m1, w, h_ref, slope_ref)
    y_ref[...] = y
    out_ref[...] = y.astype(bf16)
    mem = rms(y, gf_ref[...])
    mem_ref[...] = mem
    for c in range(2):
        for i, half in enumerate((Mid(ckv=ckv_ref), w)):
            at = 512 * c + 256 * i
            kv_ref[:, at : at + 256] = nn(mem, half.ckv(c)).astype(bf16)


def mid_other(ids, x1, part, g2, gf, ckv, pieces, tile=256):
    n = x1.shape[0]
    return pl.pallas_call(
        mid_other_kernel,
        name="enc_middle_other",
        grid=(n // tile,),
        in_specs=[smem, tile_block(tile, 512), tile_block(tile, 512), whole(g2), whole(gf), whole(ckv)]
        + [anywhere] * len(pieces),
        out_specs=[
            tile_block(tile, 512),
            tile_block(tile, 512),
            tile_block(tile, 512),
            tile_block(tile, 1024),
            tile_block(tile, 1024),
            tile_block(tile, 1024),
            whole(sds((enc_mid.rows, 512), bf16)),
        ],
        out_shape=[
            sds((n, 512), f32),
            sds((n, 512), bf16),
            sds((n, 512), bf16),
            sds((n, 1024), bf16),
            sds((n, 1024), bf16),
            sds((n, 1024), bf16),
            sds((enc_mid.rows, 512), bf16),
        ],
        scratch_shapes=[bring_sems(enc_mid, len(pieces))],
        compiler_params=params(),
        cost_estimate=cost(7e9, 1.5e7),
    )(ids, x1, part, g2, gf, ckv, *pieces)


def out_grad_kernel(dkv_ref, y_ref, cot_ref, gf_ref, ckva_ref, ckvb_ref, dy_ref, dgf_ref):
    step = pl.program_id(0)
    terms = []
    for c in range(2):
        for i in range(2):
            d = dkv_ref[:, 512 * c + 256 * i : 512 * c + 256 * i + 256]
            terms.append(nt(d, ckvb_ref[:, 256 * c : 256 * c + 256] if i else ckva_ref[c]))
    part, dgf = rms_back(y_ref[...], gf_ref[...], total(terms))
    dy_ref[...] = cot_ref[...].astype(f32) + part

    @pl.when(step == 0)
    def _():
        dgf_ref[...] = dgf

    @pl.when(step > 0)
    def _():
        dgf_ref[...] += dgf


def out_grad(dkv, y, cot, gf, ckv, w_mid, after=(), tile=256):
    n = y.shape[0]
    ins = [dkv, y, cot, gf, ckv, w_mid]
    return pl.pallas_call(
        ordered(out_grad_kernel, ins, after),
        name="enc_output_back",
        grid=(n // tile,),
        in_specs=[
            tile_block(tile, 1024),
            tile_block(tile, 512),
            tile_block(tile, 512),
            whole(gf),
            whole(ckv),
            rows_of(w_mid, enc_mid.at["ckv"], 512),
        ]
        + [unused] * len(after),
        out_specs=[tile_block(tile, 512), pl.BlockSpec((1, 512), lambda t: (0, 0))],
        out_shape=[sds((n, 512), f32), sds((1, 512), f32)],
        compiler_params=params(),
        cost_estimate=cost(2e9, 8e6),
    )(*ins, *after)


def mid_bwd_kernel(
    ids_ref, dy_ref, dkv_ref, mem_ref, x1_ref, oa_ref, ob_ref, g2_ref, outa_ref, outb_ref,
    ha_ref, hb_ref, sa_ref, sb_ref, ffoa_ref, ffob_ref, ffia_ref, ffib_ref,
    dx1_ref, do_ref, keep_ref, send_ref, dg2_ref, g_s, m1_s, dm1, acc_a, acc_b, sems,
):
    accs = (acc_a, acc_b)
    step = pl.program_id(0)
    at = enc_grads.at

    @pl.when(step == 0)
    def _():
        g_s[...] = dy_ref[...].astype(bf16)
        m1_s[...] = rms(x1_ref[...], g2_ref[...])
        for i in range(2):
            for c in range(2):
                d = dkv_ref[:, 512 * c + 256 * i : 512 * c + 256 * i + 256]
                rows = slice(at["ckv"], at["ckv"] + 512)
                accs[i][rows, 256 * c : 256 * c + 256] = tn(mem_ref[...], d).astype(bf16)

    out_row = pl.ds(pl.multiple_of(at["ffo"] + 256 * step, 256), 256)
    in_row = pl.ds(pl.multiple_of(at["ffi"] + 512 * (step // 2), 512), 512)
    in_lane = pl.ds(pl.multiple_of(256 * (step % 2), 256), 256)
    sides = (
        (acc_a, ha_ref, sa_ref, ffoa_ref, ffia_ref),
        (acc_b, hb_ref, sb_ref, ffob_ref, ffib_ref),
    )
    g = g_s[...]
    dhs = [nt(g, side[3][...]) for side in sides]
    dus = []
    for dh, (acc, h_ref, slope_ref, _, _) in zip(dhs, sides):
        acc[out_row, :] = tn(h_ref[...], g).astype(bf16)
        dus.append((dh * slope_ref[...].astype(f32)).astype(bf16))
    terms = []
    for du, (acc, _, _, _, ffi_ref) in zip(dus, sides):
        acc[in_row, in_lane] = tn(m1_s[...], du).astype(bf16)
        terms.append(nt(du, ffi_ref[...]))

    @pl.when(step == 0)
    def _():
        dm1[...] = total(terms)

    @pl.when(step > 0)
    def _():
        dm1[...] += total(terms)

    @pl.when(step == 3)
    def _():
        move = Place("mid", ids_ref, accs, keep_ref, send_ref, sems)
        ready = at["out"] // (enc_grads.rows // 16)
        move.start(0, ready)
        part, dg2_ref[...] = rms_back(x1_ref[...], g2_ref[...], dm1[...])
        dx1 = dy_ref[...] + part
        dx1_ref[...] = dx1
        g_s[...] = dx1.astype(bf16)
        for i, (o_ref, out_ref) in enumerate(((oa_ref, outa_ref), (ob_ref, outb_ref))):
            accs[i][at["out"] : at["out"] + 256, :] = tn(o_ref[...], g_s[...]).astype(bf16)
        move.start(ready)
        for i, out_ref in enumerate((outa_ref, outb_ref)):
            do_ref[:, 256 * i : 256 * i + 256] = nt(g_s[...], out_ref[...]).astype(bf16)
        move.wait()


def mid_bwd(ids, dy, dkv, mem, x1, ha, hb, sa, sb, oa, ob, g2, out_a, w_first, ffo, ffi, w_mid, after=()):
    n = dy.shape[0]
    grads = sds((enc_grads.rows, 512), bf16)
    hidden = pl.BlockSpec((n, 256), lambda t: (0, t))
    down, up = enc_mid.at["ffo"] // 256, enc_mid.at["ffi"] // 512
    outs = [sds((n, 512), f32), sds((n, 512), bf16), grads, grads, sds((1, 512), f32)]
    ins = [ids, dy, dkv, mem, x1, oa, ob, g2, out_a, w_first, ha, hb, sa, sb, ffo, w_mid, ffi, w_mid]
    return pl.pallas_call(
        ordered(mid_bwd_kernel, ins, after),
        name="enc_middle_back",
        grid=(4,),
        in_specs=[smem]
        + [whole(a) for a in (dy, dkv, mem, x1, oa, ob, g2, out_a)]
        + [
            pl.BlockSpec((256, 512), lambda t: (0, 0), pipeline_mode=pl.Buffered(1)),
            hidden,
            hidden,
            hidden,
            hidden,
            pl.BlockSpec((256, 512), lambda t: (t, 0)),
            pl.BlockSpec((256, 512), lambda t: (down + t, 0)),
            pl.BlockSpec((512, 256), lambda t: (0, t)),
            pl.BlockSpec((512, 256), lambda t: (up + t // 2, t % 2)),
        ]
        + [unused] * len(after),
        out_specs=[anywhere if a is grads else whole(a) for a in outs],
        out_shape=outs,
        scratch_shapes=[
            pltpu.VMEM((n, 512), bf16),
            pltpu.VMEM((n, 512), bf16),
            pltpu.VMEM((n, 512), f32),
            pltpu.VMEM((enc_grads.rows, 512), bf16),
            pltpu.VMEM((enc_grads.rows, 512), bf16),
            place_sems,
        ],
        compiler_params=params(56),
        cost_estimate=cost(20e9, 3e7),
    )(*ins, *after)


def enc_last_kernel(x_ref, dx1_ref, da_ref, db_ref, g_ref, wq_ref, wkv_ref, w_ref, out_ref, dg_ref):
    step = pl.program_id(0)
    da, db = da_ref[...], db_ref[...]
    dn = total(
        [
            nt(da[:, 0:256], wq_ref[...]),
            nt(da[:, 256:512], wkv_ref[0]),
            nt(da[:, 512:768], wkv_ref[1]),
            nt(db[:, 0:512], w_ref[256:768, :]),
            one_back(db[:, 512:768], w_ref[768:1024, :]),
        ]
    )
    part, dg = rms_back(x_ref[...].astype(f32), g_ref[...], dn)
    out_ref[...] = dx1_ref[...] + part

    @pl.when(step == 0)
    def _():
        dg_ref[...] = dg

    @pl.when(step > 0)
    def _():
        dg_ref[...] += dg


def enc_last(x, dx1, da, db, g, wq, wkv, w_first, after=(), tile=256):
    n = x.shape[0]
    ins = [x, dx1, da, db, g, wq, wkv, w_first]
    return pl.pallas_call(
        ordered(enc_last_kernel, ins, after),
        name="enc_input_back",
        grid=(n // tile,),
        in_specs=[
            tile_block(tile, 512),
            tile_block(tile, 512),
            tile_block(tile, 768),
            tile_block(tile, 768),
            whole(g),
            whole(wq),
            whole(wkv),
            whole(w_first),
        ]
        + [unused] * len(after),
        out_specs=[tile_block(tile, 512), pl.BlockSpec((1, 512), lambda t: (0, 0))],
        out_shape=[sds((n, 512), f32), sds((1, 512), f32)],
        compiler_params=params(),
        cost_estimate=cost(4e9, 1e7),
    )(*ins, *after)


def tail_grads_kernel(
    ids_ref, x_ref, da_ref, db_ref, g_ref, dg1_ref, dg2_ref, dgf_ref, dgd_ref,
    ta0_ref, ta1_ref, tb0_ref, tb1_ref, tabd_ref, keep_ref, send_ref, low_a, low_b, sems,
):
    n1 = rms(x_ref[...].astype(f32), g_ref[...])
    same = jnp.concatenate(
        [dg1_ref[...], dg2_ref[...], dgf_ref[...], dgd_ref[...], jnp.zeros((2, 512), f32)], axis=0
    )
    for d, low, t0, t1, first in ((da_ref, low_a, ta0_ref, ta1_ref, 0), (db_ref, low_b, tb0_ref, tb1_ref, 4)):
        low[0:512, :] = tn(n1, d[:, 0:512]).astype(bf16)
        dv = tn(n1, d[:, 512:768]).astype(bf16)
        low[512:768, 0:256] = dv[:256]
        low[512:768, 256:512] = dv[256:]
        tabs = jnp.concatenate([(t0[...] + t1[...])[0:4], tabd_ref[first : first + 4, :]], axis=1)
        tabs = jnp.concatenate([tabs, jnp.zeros((4, 256), f32)], axis=1)
        small = jnp.concatenate([same, tabs, jnp.zeros((4, 512), f32)], axis=0)
        high = small.astype(bf16)
        low[768:784, :] = high
        low[784:800, :] = (small - high.astype(f32)).astype(bf16)
        low[800:1024, :] = jnp.zeros((224, 512), bf16)
    move = Place("tail", ids_ref, (low_a, low_b), keep_ref, send_ref, sems)
    move.start()
    move.wait()


def tail_grads(ids, x, da, db, g, smalls, after=()):
    grads = sds((enc_tail.rows, 512), bf16)
    ins = [ids, x, da, db, g, *smalls]
    return pl.pallas_call(
        ordered(tail_grads_kernel, ins, after),
        name="enc_qkv_back",
        grid=(1,),
        in_specs=[smem] + [whole(a) for a in ins[1:]] + [unused] * len(after),
        out_specs=[anywhere, anywhere],
        out_shape=[grads, grads],
        scratch_shapes=[pltpu.VMEM((enc_tail.rows, 512), bf16)] * 2 + [place_sems],
        compiler_params=params(),
        cost_estimate=cost(4e9, 6e6),
    )(*ins, *after)


class Dec:
    def __init__(self, natural=None, early=None, late=None):
        if natural is not None:
            ffo, ffi, cout, cq, out, q, kv = natural
            self.ffo = lambda c: ffo[512 * c : 512 * c + 512, :]
            self.ffi = lambda c: ffi[:, 512 * c : 512 * c + 512]
            self.cout = lambda: cout[...]
            self.cq = lambda c: cq[256 * c : 256 * c + 256, :]
            self.out = lambda: out[...]
            self.qk = lambda c: q[...] if c == 0 else kv[0]
            self.v = lambda c: kv[1, 256 * c : 256 * c + 256, :]
        else:
            at = {**dec_early.at, **dec_late.at}
            self.ffo = lambda c: late[at["ffo"] + 512 * c : at["ffo"] + 512 * c + 512, :]
            self.ffi = lambda c: late[at["ffi"] + 512 * c : at["ffi"] + 512 * c + 512, :]
            self.cout = lambda: late[at["cout"] : at["cout"] + 256, :]
            self.cq = lambda c: early[at["cq"] : at["cq"] + 256, 256 * c : 256 * c + 256]
            self.out = lambda: early[at["out"] : at["out"] + 256, :]
            self.qk = lambda c: early[at["qk"] : at["qk"] + 512, 256 * c : 256 * c + 256]
            self.v = lambda c: early[at["v"] : at["v"] + 256, 256 * c : 256 * c + 256]


def two_mul(a, w):
    return nn(a[:, :256], w(0)) + nn(a[:, 256:], w(1))


def two_back(g, w):
    return jnp.concatenate([nt(g, w(0)), nt(g, w(1))], axis=1)


def spread_t(a_t, width):
    tiled = jnp.concatenate([a_t] * 4, axis=1)
    head = lax.broadcasted_iota(jnp.int32, tiled.shape, 0) // 64
    block = lax.broadcasted_iota(jnp.int32, tiled.shape, 1) // width
    return jnp.where(head == block, tiled, jnp.zeros((), a_t.dtype))


def spread(a, height):
    tiled = jnp.concatenate([a] * 4, axis=0)
    block = lax.broadcasted_iota(jnp.int32, tiled.shape, 0) // height
    head = lax.broadcasted_iota(jnp.int32, tiled.shape, 1) // 64
    return jnp.where(head == block, tiled, jnp.zeros((), a.dtype))


def fold(full, height):
    head = lax.broadcasted_iota(jnp.int32, (height, 256), 1) // 64
    total = jnp.zeros((height, 256), f32)
    for h in range(4):
        total = total + jnp.where(head == h, full[height * h : height * h + height], 0.0)
    return total


def dec_bucket_rows(buckets_ref):
    b = buckets_ref[...]
    b = jnp.concatenate([b, jnp.full((1, LANE - b.shape[1]), -1, jnp.int32)], axis=1)
    return lax.broadcasted_iota(jnp.int32, (32, LANE), 0) == b


def dec_bias_rows(tab, buckets_ref):
    w = nn(tab, dec_bucket_rows(buckets_ref).astype(bf16))
    return jnp.concatenate(
        [
            pltpu.roll(jnp.broadcast_to(w[h : h + 1], (LANE, LANE)), 0, 1, stride=1, stride_axis=0)
            for h in range(4)
        ],
        axis=1,
    )


def dec_self_mask(ids_ref, dseg_ref, rows):
    code = jnp.concatenate(
        [(dseg_ref[pl.ds(ids_ref[0] + r, 1), :] + 8 * r).astype(f32) for r in range(rows)], axis=1
    )
    key = as_column(code)
    j = lax.broadcasted_iota(jnp.int32, (LANE, LANE), 0)
    i = lax.broadcasted_iota(jnp.int32, (LANE, LANE), 1)
    one = jnp.where((key == code) & (j <= i), 0.0, neg)
    return jnp.concatenate([one] * 4, axis=1)


def dec_first_kernel(ids_ref, x_ref, g1_ref, g2_ref, dseg_ref, buckets_ref, taba_ref, tabb_ref, *rest):
    pieces = rest[7:11]
    qkv_ref, o_ref, lse_ref, z1_ref, q3_ref, w_ref, sems = rest[11:]
    halves = (Dec(rest[:7]), Dec(early=w_ref))
    bring(ids_ref, dec_early, pieces, w_ref, sems)
    z = x_ref[...].astype(f32)
    n2 = rms(z, g1_ref[...])
    mask = dec_self_mask(ids_ref, dseg_ref, x_ref.shape[0] // 64)
    terms = []
    for i, (w, tab) in enumerate(zip(halves, (taba_ref[...], tabb_ref[0:4, 256:288]))):
        q = nn(n2, w.qk(0)).astype(bf16)
        k = nn(n2, w.qk(1)).astype(bf16)
        v = two_mul(n2, w.v).astype(bf16)
        for c, a in enumerate((q, k, v)):
            qkv_ref[:, 512 * c + 256 * i : 512 * c + 256 * i + 256] = a
        s = nn(k, spread_t(jnp.transpose(q), LANE)) + dec_bias_rows(tab, buckets_ref) + mask
        m = jnp.max(s, axis=0, keepdims=True)
        e = jnp.exp(s - m)
        norm = jnp.sum(e, axis=0, keepdims=True)
        p = (e * (1.0 / norm)).astype(bf16)
        lse_ref[i : i + 1, :] = m + jnp.log(norm)
        o = fold(tn(p, v), LANE).astype(bf16)
        o_ref[:, 256 * i : 256 * i + 256] = o
        terms.append(nn(o, w.out()))
    z1 = z + total(terms)
    z1_ref[...] = z1
    n3 = rms(z1, g2_ref[...])
    for i, w in enumerate(halves):
        q3_ref[:, 256 * i : 256 * i + 256] = two_mul(n3, w.cq).astype(bf16)


def dec_first(ids, x, g1, g2, dseg, buckets, taba, tabb, own, pieces):
    n = x.shape[0]
    ins = [x, g1, g2, dseg, buckets, taba, tabb, *own]
    return pl.pallas_call(
        dec_first_kernel,
        name="dec_self",
        grid=(1,),
        in_specs=[smem] + [whole(a) for a in ins] + [anywhere] * len(pieces),
        out_specs=[
            pl.BlockSpec(s, lambda t: (0, 0))
            for s in ((n, 1536), (n, 512), (2, 512), (n, 512), (n, 512), (dec_early.rows, 512))
        ],
        out_shape=[
            sds((n, 1536), bf16),
            sds((n, 512), bf16),
            sds((2, 512), f32),
            sds((n, 512), f32),
            sds((n, 512), bf16),
            sds((dec_early.rows, 512), bf16),
        ],
        scratch_shapes=[bring_sems(dec_early, len(pieces))],
        compiler_params=params(),
        cost_estimate=cost(1e9, 8e6),
    )(ids, *ins, *pieces)


def dec_main_kernel(
    x_ref,
    cot_ref,
    g1_ref,
    g2_ref,
    g3_ref,
    buckets_ref,
    dseg_ref,
    seg_ref,
    pad_ref,
    ids_ref,
    qkv_ref,
    o2_ref,
    lse_ref,
    z1_ref,
    q3_ref,
    kv_ref,
    taba_ref,
    tabb_ref,
    *rest,
):
    early, pieces = rest[7], rest[8:12]
    out_ref, dx_ref, dkv_ref, keep_ref, send_ref, dg_ref, dtab_ref = rest[12:19]
    madd, p_s, acc_a, acc_b, late, sems, move_sems = rest[19:]
    halves = (Dec(rest[:7]), Dec(early=early, late=late))
    bring(ids_ref, dec_late, pieces, late, sems)
    accs = (acc_a, acc_b)
    at = dec_all.at
    rows_n = x_ref.shape[0] // 64
    z1 = z1_ref[...]
    mixed = [[None] * rows_n, [None] * rows_n]
    for r in range(rows_n):
        row = pl.ds(ids_ref[0] + r, 1)
        keyc = as_column(key_codes(seg_ref[row, :], pad_ref[row, :])[1])
        code = dseg_ref[row, :].astype(f32)
        madd[...] = jnp.where(keyc == jnp.concatenate([code, code], axis=1), 0.0, neg)
        both = jnp.concatenate([madd[...]] * 2, axis=1)
        for i in range(2):
            cols = slice(256 * i, 256 * i + 256)
            k3 = kv_ref[512 * r : 512 * r + 512, 256 * i : 256 * i + 256]
            v3 = kv_ref[512 * r : 512 * r + 512, 512 + 256 * i : 512 + 256 * i + 256]
            q_t = jnp.transpose(q3_ref[64 * r : 64 * r + 64, cols])
            s = nn(k3, spread_t(q_t, 64)) + both
            m = jnp.max(s, axis=0, keepdims=True)
            e = jnp.exp(s - m)
            p = e * (1.0 / jnp.sum(e, axis=0, keepdims=True))
            p_s[2 * r + i] = p
            mixed[i][r] = fold(tn(p.astype(bf16), v3), 64).astype(bf16)
    o3 = [jnp.concatenate(m, axis=0) for m in mixed]
    z2 = z1 + total([nn(o, w.cout()) for o, w in zip(o3, halves)])
    n4 = rms(z2, g3_ref[...])
    terms, kept = [], []
    for i, w in enumerate(halves):
        for c in range(2):
            h, slope = gelu_both(nn(n4, w.ffi(c)))
            h = h.astype(bf16)
            kept.append((h, slope))
            terms.append(nn(h, w.ffo(c)))
    out_ref[...] = (z2 + total(terms)).astype(bf16)
    g = cot_ref[...]
    terms = []
    for i, w in enumerate(halves):
        for c in range(2):
            h, slope = kept[2 * i + c]
            accs[i][at["ffo"] + 512 * c : at["ffo"] + 512 * c + 512] = tn(h, g).astype(bf16)
            du = (nt(g, w.ffo(c)) * slope).astype(bf16)
            accs[i][at["ffi"] + 512 * c : at["ffi"] + 512 * c + 512] = tn(n4, du).astype(bf16)
            terms.append(nt(du, w.ffi(c)))
    part, dg3 = rms_back(z2, g3_ref[...], total(terms))
    dz2 = g.astype(f32) + part
    move = Place("dec", ids_ref, accs, keep_ref, send_ref, move_sems)
    done = 2048 // (dec_all.rows // 16)
    move.start(0, done)
    g = dz2.astype(bf16)
    n3 = rms(z1, g2_ref[...])
    terms = []
    for i, w in enumerate(halves):
        cols = slice(256 * i, 256 * i + 256)
        accs[i][at["cout"] : at["cout"] + 256] = tn(o3[i], g).astype(bf16)
        do = nt(g, w.cout()).astype(bf16)
        dq = []
        for r in range(rows_n):
            k3 = kv_ref[512 * r : 512 * r + 512, 256 * i : 256 * i + 256]
            v3 = kv_ref[512 * r : 512 * r + 512, 512 + 256 * i : 512 + 256 * i + 256]
            do_r = do[64 * r : 64 * r + 64]
            p = p_s[2 * r + i]
            dp = nn(v3, spread_t(jnp.transpose(do_r), 64))
            ds = (p * (dp - jnp.sum(p * dp, axis=0, keepdims=True))).astype(bf16)
            rows = slice(512 * r, 512 * r + 512)
            dkv_ref[rows, 256 * i : 256 * i + 256] = nn(
                ds, spread(q3_ref[64 * r : 64 * r + 64, cols], 64)
            ).astype(bf16)
            dkv_ref[rows, 512 + 256 * i : 512 + 256 * i + 256] = nn(
                p.astype(bf16), spread(do_r, 64)
            ).astype(bf16)
            dq.append(fold(tn(ds, k3), 64).astype(bf16))
        dq = jnp.concatenate(dq, axis=0)
        accs[i][at["cq"] : at["cq"] + 256] = one_grad(n3, dq).astype(bf16)
        terms.append(two_back(dq, w.cq))
    part, dg2 = rms_back(z1, g2_ref[...], total(terms))
    dz1 = dz2 + part
    g = dz1.astype(bf16)
    z = x_ref[...].astype(f32)
    n2 = rms(z, g1_ref[...])
    mask = dec_self_mask(ids_ref, dseg_ref, rows_n)
    terms = []
    diags = []
    for i, (w, tab) in enumerate(zip(halves, (taba_ref[...], tabb_ref[0:4, 256:288]))):
        q, k, v = (qkv_ref[:, 512 * c + 256 * i : 512 * c + 256 * i + 256] for c in range(3))
        accs[i][at["out"] : at["out"] + 256] = tn(o2_ref[:, 256 * i : 256 * i + 256], g).astype(bf16)
        do = nt(g, w.out()).astype(bf16)
        s = nn(k, spread_t(jnp.transpose(q), LANE)) + dec_bias_rows(tab, buckets_ref) + mask
        p = jnp.exp(s - lse_ref[i : i + 1, :])
        dp = nn(v, spread_t(jnp.transpose(do), LANE))
        ds = p * (dp - jnp.sum(p * dp, axis=0, keepdims=True))
        diags += [diagonal_sums(ds[:, LANE * h : LANE * h + LANE]) for h in range(4)]
        ds = ds.astype(bf16)
        dk = nn(ds, spread(q, LANE)).astype(bf16)
        dv = nn(p.astype(bf16), spread(do, LANE)).astype(bf16)
        dq = fold(tn(ds, k), LANE).astype(bf16)
        accs[i][at["qk"] : at["qk"] + 512, 0:256] = tn(n2, dq).astype(bf16)
        accs[i][at["qk"] : at["qk"] + 512, 256:512] = tn(n2, dk).astype(bf16)
        accs[i][at["v"] : at["v"] + 256] = one_grad(n2, dv).astype(bf16)
        terms += [nt(dq, w.qk(0)), nt(dk, w.qk(1)), two_back(dv, w.v)]
    part, dg1 = rms_back(z, g1_ref[...], total(terms))
    dx_ref[...] = dz1 + part
    dg_ref[...] = jnp.concatenate([dg1, dg2, dg3], axis=0)
    dtab_ref[:, 0:32] = bucket_sums(jnp.concatenate(diags, axis=0), dec_bucket_rows(buckets_ref))
    move.start(done)
    move.wait()


def dec_main(x, cot, g1, g2, g3, buckets, dseg, seg, pad, ids, qkv, o2, lse, z1, q3, kv, taba, tabb, own, early, pieces):
    n = x.shape[0]
    ins = [x, cot, g1, g2, g3, buckets, dseg, seg, pad, ids, qkv, o2, lse, z1, q3, kv, taba, tabb, *own, early]
    grads = sds((dec_all.rows, 512), bf16)
    outs = [
        sds((n, 512), bf16),
        sds((n, 512), f32),
        sds((kv.shape[0], 1024), bf16),
        grads,
        grads,
        sds((3, 512), f32),
        sds((8, LANE), f32),
    ]
    specs = [whole(a) for a in ins]
    specs[9] = smem
    return pl.pallas_call(
        dec_main_kernel,
        name="dec_cross_ff_back",
        grid=(1,),
        in_specs=specs + [anywhere] * len(pieces),
        out_specs=[anywhere if a is grads else whole(a) for a in outs],
        out_shape=outs,
        scratch_shapes=[
            pltpu.VMEM((512, LANE), f32),
            pltpu.VMEM((4, 512, 256), f32),
            pltpu.VMEM((dec_all.rows, 512), bf16),
            pltpu.VMEM((dec_all.rows, 512), bf16),
            pltpu.VMEM((dec_late.rows, 512), bf16),
            bring_sems(dec_late, len(pieces)),
            place_sems,
        ],
        compiler_params=params(60),
        cost_estimate=cost(6e9, 2e7),
    )(*ins, *pieces)


def natural(flat):
    shapes = {"out": (256, 512), "down": (1024, 512), "up": (512, 1024), "pair": (2, 512, 256), "one": (512, 256)}
    res = []
    for name, kind in flat.layout:
        if name == "qk":
            res.append(("q", (512, 256)))
        elif name == "v":
            res.append(("kv", (2, 512, 256)))
        elif name == "small":
            res += [(i, (1, 512)) for i in range(6)] + [("enc", (4, 32)), ("dec", (4, 32))]
        else:
            res.append((name, shapes[kind]))
    return res


def finish_parts(flat):
    parts = []
    for name, kind in flat.layout:
        row = flat.at[name]
        if name == "qk":
            parts += [("q", (), row, 512, 0, 256, 0, 0), ("kv", (0,), row, 512, 256, 256, 0, 0)]
        elif name == "v":
            parts += [("kv", (1,), row, 256, 0, 256, 0, 0), ("kv", (1,), row, 256, 256, 256, 256, 0)]
        elif kind in ("out", "down"):
            for at in range(0, flat.sizes[kind], 256):
                parts.append((name, (), row + at, 256, 0, 512, at, 0))
        elif kind == "up":
            for at in range(0, 512, 256):
                parts.append((name, (), row + at, 256, 0, 512, at, 0))
                parts.append((name, (), row + 512 + at, 256, 0, 512, at, 512))
        elif kind == "pair":
            parts += [(name, (c,), row, 512, 256 * c, 256, 0, 0) for c in range(2)]
        elif name != "small":
            parts += [(name, (), row, 256, 256 * c, 256, 256 * c, 0) for c in range(2)]
    return parts


def finish_kernel(flat, ids_ref, *rest):
    parts = finish_parts(flat)
    pieces, (*outs, low, wide, sems, out_sems) = rest[:8], rest[8:]
    outs = dict(zip([n for n, _ in natural(flat)], outs))
    size = flat.rows // 8
    copies = []
    for p in range(8):
        piece = pieces[p]
        core = ids_ref[1] if p < 4 else 1 - ids_ref[1]
        high, last = p % 4 // 2, p % 2
        y = (high * (1 - core) + last * core) ^ ids_ref[2]
        z0 = (last * (1 - core) + high * core) ^ ids_ref[3]
        to = pl.multiple_of((core * 4 + y * 2 + z0) * size, 16)
        copies.append((piece, low.at[pl.ds(to, size), :]))
    run_all(copies, sems)
    sent = []
    for i, (name, lead, row, rows, lane, lanes, to_row, to_lane) in enumerate(parts):

        def body(t, _):
            src = pl.ds(pl.multiple_of(row + t * 64, 16), 64)
            dst = pl.ds(pl.multiple_of(t * 64, 16), 64)
            wide[i, dst, 0:lanes] = low[src, lane : lane + lanes].astype(f32)
            return 0

        lax.fori_loop(0, rows // 64, body, 0)
        copy = pltpu.make_async_copy(
            wide.at[i, 0:rows, 0:lanes],
            outs[name].at[lead + (slice(to_row, to_row + rows), slice(to_lane, to_lane + lanes))],
            out_sems.at[i],
        )
        copy.start()
        sent.append(copy)
    if "small" in flat.at:
        row = flat.at["small"]
        small = low[row : row + 16, :].astype(f32) + low[row + 16 : row + 32, :].astype(f32)
        for i in range(6):
            outs[i][...] = small[i : i + 1, :]
        outs["enc"][...] = small[8:12, 0:32]
        outs["dec"][...] = small[8:12, LANE : LANE + 32]
    for copy in sent:
        copy.wait()


def finish(flat, ids, pieces, after=()):
    names = natural(flat)
    ins = [ids, *pieces]
    outs = [sds(shape, f32) for _, shape in names]
    parts = finish_parts(flat)
    tall = max(p[3] for p in parts)
    moved = {p[0] for p in parts}
    res = pl.pallas_call(
        ordered(functools.partial(finish_kernel, flat), ins, after),
        name="grads_out",
        grid=(1,),
        in_specs=[smem] + [anywhere] * 8 + [unused] * len(after),
        out_specs=[anywhere if name in moved else whole(o) for (name, _), o in zip(names, outs)],
        out_shape=outs,
        scratch_shapes=[
            pltpu.VMEM((flat.rows, 512), bf16),
            pltpu.VMEM((len(parts), tall, 512), f32),
            pltpu.SemaphoreType.DMA((8,)),
            pltpu.SemaphoreType.DMA((len(parts),)),
        ],
        compiler_params=params(),
        cost_estimate=cost(1e6, 6 * flat.rows * 512),
    )(*ins, *after)
    return {name: r for (name, _), r in zip(names, res)}


def hop(a, dim0, dim1=None):
    n, m = lax.axis_size("dp"), lax.axis_size("mp")
    pairs = []
    for i in range(n):
        dim = dim1 if dim1 is not None and i % 2 else dim0
        for j in range(m):
            to = (i, (j + 1) % m) if dim == "mp" else (i ^ dim, j)
            pairs.append((i * m + j, to[0] * m + to[1]))
    return lax.ppermute(a, ("dp", "mp"), pairs)


def join(*arrays):
    return lax.optimization_barrier(arrays)


def sum_rows(terms, first, n):
    return total([t[first : first + n].astype(f32) for t in terms]).astype(bf16)


def sum_kernel(*refs):
    refs[-1][...] = total([r[...].astype(f32) for r in refs[:-1]]).astype(bf16)


def sum_after(terms, first, n, after):
    size = n if n <= 512 else n // 2
    block = pl.BlockSpec((size, 512), lambda t: (first // size + t, 0))
    return pl.pallas_call(
        ordered(sum_kernel, terms, (after,)),
        name="sum_rows",
        grid=(n // size,),
        in_specs=[block] * len(terms) + [unused],
        out_specs=pl.BlockSpec((size, 512), lambda t: (t, 0)),
        out_shape=sds((n, 512), bf16),
        compiler_params=params(24),
        cost_estimate=cost(1e6, 2 * 512 * n * (len(terms) + 1)),
    )(*terms, after)


axes = {"m": "mp", "y": 2, "z": 4}
gather_dims = [(4, 2), (2, 4)]


class Summed:
    def __init__(self, group, keep, send):
        self.dims = [(axes[a], axes[b]) for a, b in zip(*orders[group])]
        self.terms = [keep, hop(send, 1)]
        self.rows = keep.shape[0]
        self.step = 0

    def forward(self, after=None):
        def added(first, n):
            return sum_rows(self.terms, first, n) if after is None else sum_after(self.terms, first, n, after)

        if self.step < len(self.dims):
            self.rows //= 2
            value = added(self.rows, self.rows)
            self.terms.append(hop(value, *self.dims[self.step]))
        elif self.step == len(self.dims):
            value = added(0, self.rows)
            self.terms = [value, hop(value, 8)]
        else:
            value = added(0, self.rows)
            bit = 16
            while bit < lax.axis_size("dp"):
                value = sum_rows([value, hop(value, bit)], 0, self.rows)
                bit *= 2
            pieces = [value]
            for dims in gather_dims:
                pieces = pieces + [hop(p, *dims) for p in pieces]
            self.pieces = pieces + [hop(p, 1) for p in pieces]
        self.step += 1
        return value

    def finish(self):
        while self.step < len(self.dims) + 2:
            self.forward()
        return self.pieces


def on_device(
    enc_in,
    enc_segments,
    enc_pad,
    enc_buckets,
    dec_in,
    dec_segments,
    dec_buckets,
    enc_cot,
    dec_cot,
    enc_norm1,
    enc_query,
    enc_kv,
    enc_out_proj,
    enc_bias,
    enc_norm2,
    enc_ff_in,
    enc_ff_out,
    enc_final,
    dec_norm1,
    dec_query,
    dec_kv,
    dec_out_proj,
    dec_bias,
    dec_norm2,
    cross_query,
    cross_kv,
    cross_out,
    dec_norm3,
    dec_ff_in,
    dec_ff_out,
):
    rows, length, width = enc_in.shape
    dp = lax.axis_index("dp")
    ids = jnp.stack([lax.axis_index("mp") * rows, dp % 2, dp // 2 % 2, dp // 4 % 2, dp // 8 % 2, lax.axis_index("mp")]).astype(jnp.int32)

    n1g, n2g, nfg = enc_norm1[None, :], enc_norm2[None, :], enc_final[None, :]
    d1g, d2g, d3g = dec_norm1[None, :], dec_norm2[None, :], dec_norm3[None, :]
    rev = jnp.pad(enc_buckets[::-1], (0, 1), constant_values=-1)[None, :]
    places = dec_buckets[None, :]
    x = enc_in.reshape(rows * length, width)
    xc = enc_cot.reshape(rows * length, width)
    z = dec_in.reshape(-1, width)
    zc = dec_cot.reshape(-1, width)

    def flat2(a):
        return a.reshape(rows * length, a.shape[-1])

    e_tab, d_tab = enc_bias.T, dec_bias.T
    q_send = pack_first(ids, e_tab, d_tab, enc_query, enc_kv, enc_out_proj)
    q0 = hop(q_send, "mp")
    m_send, e_send, l_send = pack_rest(
        ids, enc_ff_out, enc_ff_in, cross_kv, dec_ff_out, dec_ff_in, cross_out, cross_query, dec_out_proj,
        dec_query, dec_kv,
    )
    qkv_a, o_a, lse_a = enc_fwd(
        ids, enc_in, n1g, enc_segments, enc_pad, rev, [e_tab, enc_query, enc_kv]
    )
    o_a, q0, m_send = join(o_a, q0, m_send)
    q1 = hop(q0, 1)
    m0 = hop(m_send, "mp")
    qkv_b, o_b, lse_b, w_first, tabs = enc_fwd(ids, enc_in, n1g, enc_segments, enc_pad, rev, [q0, q1])
    o_b, m0, e_send = join(o_b, m0, e_send)
    m1 = hop(m0, 2, 4)
    e0 = hop(e_send, "mp")
    oa2, ob2 = flat2(o_a), flat2(o_b)
    x1, part, h_a, slope_a = mid_own(x, oa2, ob2, n2g, enc_out_proj, w_first, enc_ff_out, enc_ff_in)
    part, m1, e0, l_send = join(part, m1, e0, l_send)
    m2, m3 = hop(m0, 1), hop(m1, 1)
    e1 = hop(e0, 2, 4)
    l0 = hop(l_send, "mp")
    y, enc_out, mem, h_b, slope_b, kv3, w_mid = mid_other(ids, x1, part, n2g, nfg, cross_kv, [m0, m1, m2, m3])
    kv3, e1, l0 = join(kv3, e1, l0)
    e2, e3 = hop(e0, 1), hop(e1, 1)
    l1 = hop(l0, 2, 4)
    own_dec = [dec_ff_out, dec_ff_in, cross_out, cross_query, dec_out_proj, dec_query, dec_kv]
    dqkv, o2, lse2, z1, q3, w_early = dec_first(
        ids, z, d1g, d2g, dec_segments, places, d_tab, tabs, own_dec, [e0, e1, e2, e3]
    )
    z1, l1 = join(z1, l1)
    l2, l3 = hop(l0, 1), hop(l1, 1)
    dec_out, dec_grad, dkv3, dec_keep, dec_send, dgd, tab_d = dec_main(
        z, zc, d1g, d2g, d3g, places, dec_segments, enc_segments, enc_pad, ids,
        dqkv, o2, lse2, z1, q3, kv3, d_tab, tabs, own_dec, w_early, [l0, l1, l2, l3],
    )
    dec_sum = Summed("dec", dec_keep, dec_send)
    dy, dgf = out_grad(dkv3, y, xc, nfg, cross_kv, w_mid)
    dx1, do, mid_keep, mid_send, dg2 = mid_bwd(
        ids, dy, dkv3, mem, x1, h_a, h_b, slope_a, slope_b, oa2, ob2, n2g, enc_out_proj, w_first,
        enc_ff_out, enc_ff_in, w_mid, (dec_sum.forward(),),
    )
    mid_sum = Summed("mid", mid_keep, mid_send)
    do = do.reshape(rows, length, width)

    def back(half, row, before, *after):
        if half:
            return enc_bwd(1, row, ids, enc_segments, enc_pad, rev, tabs, qkv_b, o_b, do, lse_b, before, after)
        return enc_bwd(0, row, ids, enc_segments, enc_pad, rev, e_tab, qkv_a, o_a, do, lse_a, before, after)

    dqkv_b, tb0 = back(1, 0, None, dec_sum.forward())
    dqkv_b, tb1 = back(1, 1, dqkv_b, mid_sum.forward())
    dqkv_a, ta0 = back(0, 0, None, dec_sum.forward(tb1))
    dqkv_a, ta1 = back(0, 1, dqkv_a)
    enc_grad, dg1 = enc_last(
        x, dx1, flat2(dqkv_a), flat2(dqkv_b), n1g, enc_query, enc_kv, w_first,
        (dec_sum.forward(), mid_sum.forward()),
    )
    tail_sum = Summed("tail", *tail_grads(
        ids, x, flat2(dqkv_a), flat2(dqkv_b), n1g, [dg1, dg2, dgf, dgd, ta0, ta1, tb0, tb1, tab_d], (mid_sum.terms[-1], dec_sum.terms[-1])
    ))
    dec_g = finish(dec_all, ids, dec_sum.finish())
    mid_g = finish(enc_grads, ids, mid_sum.finish(), (dec_g["cout"],))
    tail_g = finish(enc_tail, ids, tail_sum.finish(), (mid_g["out"],))
    return (
        enc_out.reshape(enc_in.shape),
        dec_out.reshape(dec_in.shape),
        enc_grad.reshape(enc_in.shape),
        dec_grad.reshape(dec_in.shape),
        tail_g[0].reshape(-1),
        tail_g["q"],
        tail_g["kv"],
        mid_g["out"],
        tail_g["enc"].T,
        tail_g[1].reshape(-1),
        mid_g["ffi"],
        mid_g["ffo"],
        tail_g[2].reshape(-1),
        tail_g[3].reshape(-1),
        dec_g["q"],
        dec_g["kv"],
        dec_g["out"],
        tail_g["dec"].T,
        tail_g[4].reshape(-1),
        dec_g["cq"],
        mid_g["ckv"],
        dec_g["cout"],
        tail_g[5].reshape(-1),
        dec_g["ffi"],
        dec_g["ffo"],
    )


def solution(mesh):
    in_specs = (
        P(("dp", "mp"), None, None),
        P("dp", None),
        P("dp", None),
        P(),
        P(("dp", "mp"), None, None),
        P("dp", None),
        P(),
        P(("dp", "mp"), None, None),
        P(("dp", "mp"), None, None),
        P(),
        P(None, "mp"),
        P(None, None, "mp"),
        P("mp", None),
        P(None, "mp"),
        P(),
        P(None, "mp"),
        P("mp", None),
        P(),
        P(),
        P(None, "mp"),
        P(None, None, "mp"),
        P("mp", None),
        P(None, "mp"),
        P(),
        P(None, "mp"),
        P(None, None, "mp"),
        P("mp", None),
        P(),
        P(None, "mp"),
        P("mp", None),
    )
    out_specs = (
        P(("dp", "mp"), None, None),
        P(("dp", "mp"), None, None),
        P(("dp", "mp"), None, None),
        P(("dp", "mp"), None, None),
        P(),
        P(None, "mp"),
        P(None, None, "mp"),
        P("mp", None),
        P(None, "mp"),
        P(),
        P(None, "mp"),
        P("mp", None),
        P(),
        P(),
        P(None, "mp"),
        P(None, None, "mp"),
        P("mp", None),
        P(None, "mp"),
        P(),
        P(None, "mp"),
        P(None, None, "mp"),
        P("mp", None),
        P(),
        P(None, "mp"),
        P("mp", None),
    )
    return jax.shard_map(
        on_device, mesh=mesh, in_specs=in_specs, out_specs=out_specs, check_vma=False
    )
```
